128 devices in a mesh: group: 8 (over z_lo, y), member: 16 (over z_hi, x, core).
Axes of the slice: x: 4, y: 4, z: 4 (z_hi: 2, z_lo: 2; z = z_hi * 2 + z_lo), core: 2. Of those that a mesh axis runs over, the one named last changes fastest.
Arguments:
- rows: float32 [65536, 1024], P(('group', 'member'))
- old_list: int32 [65536], P(('group', 'member')), may hold values from 0 to 63
- old_centroids: float32 [64, 1024], replicated, may hold values from -6 to 6
- dest_device: int32 [65536, 1], P(('group', 'member')), may hold values from 0 to 127; in each aligned block of 512 rows (0 to 511, 512 to 1023, ...) at most 8 rows name the same one
- new_local: int32 [65536], P(('group', 'member')), may hold values from 0 to 1
- centroids: float32 [16, 1024], P('group'), may hold values from -6 to 6
Outputs:
- whitened: float32 [131072, 1024], P(('group', 'member'))
- factors: float32 [16, 1024, 1024], P('group')
The draws below stay inside these ranges and needn't reach their ends.
Inputs may be any that keep to these rules, and one draw needn't show every extreme that they name: `dest_device`: among the rows of one device, no destination is named by more than 8 rows, a bound that some block reaches.
All inputs are finite; a program needn't handle non-finite values.
Results may differ from the reference program's by a relative error of at most 0.0003.
Values sent between devices are 32-bit elements; how exact they have to be, the bound alone decides.
A program may use at most 128 MiB of HBM per device.

```python
import math
import jax
import jax.numpy as jnp
import numpy as np
from jax import lax

D = 1024
ROW_DEV = 512
LIST_GRP = 2
OLD = 64
CAP = 8
ROWS = 65536
LISTS = 16
N_GROUP = 8
N_MEMBER = 16
DEVICES = 128


def draw_rows(key, part):
    first, second = jax.random.split(key)
    base = jax.random.normal(first, (ROWS, D), jnp.float32)
    scales = jnp.exp(jax.random.uniform(second, (D,), jnp.float32, 0.0, 1.4))
    mixed = base + 0.8 * jnp.roll(base, 1, axis=1)
    return (mixed * scales[None, :]).astype(jnp.float32)


def with_ends(entries, rng, smallest, largest):
    place = [jax.random.randint(jax.random.fold_in(rng, axis), (), 0, length) for axis, length in enumerate(entries.shape)]
    main_axis = entries.shape.index(max(entries.shape))
    neighbour = place[:main_axis] + [(place[main_axis] + 1) % entries.shape[main_axis]] + place[main_axis + 1:]
    return entries.at[tuple(place)].set(smallest).at[tuple(neighbour)].set(largest)


def levels(own_key, extent, pieces, smallest, largest):
    def one(dim, blocks):
        draws = jax.random.uniform(jax.random.fold_in(jax.random.fold_in(own_key, 6), dim), (blocks,), jnp.float32, smallest / len(pieces), largest / len(pieces))
        return jnp.repeat(jnp.exp(draws), extent[dim] // blocks).reshape((-1,) + (1,) * (len(extent) - dim - 1))

    gain = one(*pieces[0])
    for cut in pieces[1:]:
        gain = gain * one(*cut)
    return gain


def deal_out(key, own, number, rows, count, top, limit, skew):
    ranking = jax.random.permutation(key, count)
    heavy_load, ordinary = load_shares(count, rows * top, limit, skew, True), load_shares(count, rows * top, limit, skew, False)
    places = jnp.arange(count)

    def named(tallies, rotation):
        used = int((tallies > 0).sum())
        fixed = max(1, used // 4)
        moved = fixed + (places - fixed + rotation * (used - fixed)) % max(1, count - fixed)
        return jnp.zeros((count,), jnp.int32).at[ranking[jnp.where(places < fixed, places, moved)]].set(jnp.asarray(tallies, jnp.int32))

    tallies = jnp.where(number % 4 == 0, named(heavy_load, number // 4), named(ordinary, number - number // 4 - 1))
    mixed = jax.random.permutation(jax.random.fold_in(own, 3), count)
    donor, sink = mixed[0:count // 2 * 2:2], mixed[1:count // 2 * 2:2]
    slack = jnp.minimum(tallies[donor] - 1, limit - tallies[sink]) // 2
    slack = jnp.where((donor == ranking[0]) | (sink == ranking[0]) | (tallies[sink] == 0), 0, jnp.maximum(slack, 0))
    moved = jax.random.randint(jax.random.fold_in(own, 4), (count // 2,), 0, 1 << 20) % (slack + 1)
    tallies = tallies.at[donor].add(-moved).at[sink].add(moved)
    items = jnp.searchsorted(jnp.cumsum(tallies), jnp.arange(rows * top), side="right").astype(jnp.int32)
    grid = items.reshape(top, rows).T
    grid = grid[jax.random.permutation(jax.random.fold_in(own, 1), rows)]
    rotation = jax.random.randint(jax.random.fold_in(own, 2), (rows, 1), 0, top)
    return jnp.take_along_axis(grid, (jnp.arange(top)[None, :] + rotation) % top, axis=1)


def load_shares(amount, total, limit, lean, full):
    loads = [(1 << 20) // math.isqrt(rank ** lean) + 1 for rank in range(1, amount + 1)]
    largest = limit if full else min(limit, max(-(-total // amount), total * loads[0] // sum(loads)))
    least = 1 if total - largest >= amount - 1 else 0
    given, surplus = [largest] + [least] * (amount - 1), total - largest - least * (amount - 1)
    while surplus > 0:
        free = [i for i in range(1, amount) if given[i] < largest] or [i for i in range(1, amount) if given[i] < limit]
        pool, budget = sum([loads[i] for i in free]), surplus
        for i in free:
            extra = min(limit - given[i], max(1, budget * loads[i] // pool), surplus)
            given[i] = given[i] + extra
            surplus = surplus - extra
    return np.array(given)


def normal_values(key, shape, width, bound, pieces=(), kind=jnp.bfloat16):
    drawn = width * jax.random.normal(key, shape, jnp.float32)
    if pieces:
        drawn = drawn * levels(key, shape, pieces, -0.22, 0.18)
    return jnp.clip(drawn, -bound, bound).astype(kind)


def setup_inputs(seed: int = 0) -> dict:
    splits = jax.random.split(jax.random.key(seed), 7)
    rows = draw_rows(jax.random.fold_in(splits[6], 71), 0)
    old_list = with_ends(jax.random.randint(splits[1], (ROWS,), 0, OLD), jax.random.fold_in(splits[1], 1), 0, OLD - 1).astype(jnp.int32)
    old_centroids = normal_values(splits[2], (OLD, D), 1.0, 6.0, (), jnp.float32)
    dest_device_keys = jax.random.split(jax.random.fold_in(splits[3], 1), ROWS // ROW_DEV)
    dest_device_turns = jax.random.permutation(jax.random.fold_in(splits[3], 3), ROWS // ROW_DEV)
    dest_device = jax.vmap(lambda own, number: deal_out(jax.random.fold_in(splits[3], 2), own, number, ROW_DEV, DEVICES, 1, CAP, 2))(dest_device_keys, dest_device_turns).reshape((ROWS, 1))
    new_local = with_ends(jax.random.randint(splits[4], (ROWS,), 0, LIST_GRP), jax.random.fold_in(splits[4], 1), 0, LIST_GRP - 1).astype(jnp.int32)
    centroids = normal_values(splits[5], (LISTS, D), 1.0, 6.0, ((0, 8),), jnp.float32)
    return dict(rows=rows, old_list=old_list, old_centroids=old_centroids, dest_device=dest_device, new_local=new_local, centroids=centroids)


ridge = 0.1

def reference(rows, old_list, old_centroids, dest_device, new_local, centroids):
    devices = N_GROUP * N_MEMBER
    vectors = rows + old_centroids[old_list]
    dest = dest_device[:, 0].astype(jnp.int32)
    source = (jnp.arange(ROWS) // ROW_DEV).astype(jnp.int32)
    blocks = dest.reshape(devices, ROW_DEV)
    onehot = (blocks[:, :, None] == jnp.arange(devices, dtype=jnp.int32)[None, None, :]).astype(jnp.int32)
    ranks = jnp.sum(jnp.cumsum(onehot, axis=1) * onehot, axis=2) - 1
    position = (dest * devices * CAP + source * CAP + ranks.reshape(-1)).astype(jnp.int32)
    slots = devices * devices * CAP
    tag_all = jnp.zeros((slots,), jnp.int32).at[position].set(new_local.astype(jnp.int32) + 1)
    buffer = jnp.zeros((slots, D), jnp.float32).at[position].set(vectors)
    buffer = buffer.reshape(N_GROUP, N_MEMBER * devices * CAP, D)
    tag_all = tag_all.reshape(N_GROUP, N_MEMBER * devices * CAP)
    cents = centroids.reshape(N_GROUP, LIST_GRP, D)

    def per_group(items):
        block, tags, cent = items
        select = (tags[:, None] == jnp.arange(1, LIST_GRP + 1, dtype=jnp.int32)[None, :]).astype(jnp.float32)
        residual = jnp.where(tags[:, None] > 0, block - jnp.dot(select, cent, precision=lax.Precision.HIGHEST), 0.0)
        counts = jnp.sum(select, axis=0)
        result = jnp.zeros_like(residual)
        chol = []
        for j in range(LIST_GRP):
            masked = residual * select[:, j:j + 1]
            gram = lax.dot_general(masked, masked, (((0,), (0,)), ((), ())), precision=lax.Precision.HIGHEST)
            cov = gram / jnp.maximum(counts[j], 1.0) + ridge * jnp.eye(D, dtype=jnp.float32)
            lower = jnp.linalg.cholesky(cov)
            chol.append(lower)
            solved = jax.scipy.linalg.solve_triangular(lower, residual.T, lower=True).T
            result = result + select[:, j:j + 1] * solved
        return (jnp.stack(chol), result)
    lowers, outs = lax.map(per_group, (buffer, tag_all, cents))
    return (outs.reshape(slots, D), lowers.reshape(LISTS, D, D))
```

```python
import functools

import jax, jax.numpy as jnp
from jax import lax
from jax.experimental import pallas as pl
from jax.experimental.pallas import tpu as pltpu
from jax.sharding import PartitionSpec as P
NT = (((1,), (1,)), ((), ()))
NN = (((1,), (0,)), ((), ()))
B = 128

def split(x):
    hi = x.astype(jnp.bfloat16)
    return hi, (x - hi.astype(jnp.float32)).astype(jnp.bfloat16)

def dot3(a, b, dims):
    f = functools.partial(lax.dot_general, dimension_numbers=dims, preferred_element_type=jnp.float32)
    return f(a[0], b[0]) + (f(a[0], b[1]) + f(a[1], b[0]))

def rcp(d):
    y = pl.reciprocal(d, approx=True)
    return y * (2.0 - d * y)

def factor_gen(load, eye_rows, row, out):
    n = B // 8
    w = [load(i) for i in range(n)]
    v = list(eye_rows)
    U = []; V = []
    nxt = None
    for m in range(n):
        p, q = w[m], v[m]
        M = [jnp.broadcast_to(p[:, 8*m+k:8*m+k+1], (8, B)) for k in range(8)]
        last = m == n - 1
        if not last:
            N = [jnp.broadcast_to(w[m+1][:, 8*m+k:8*m+k+1], (8, B)) for k in range(8)]
        G = {}
        for k in range(8):
            for j in range(k, 8):
                G[k, j] = jnp.broadcast_to(M[j][k:k+1, :], (8, B))
        yield
        r = []
        dvec = None
        for k in range(8):
            d = G[k, k]
            rk = rcp(d)
            r.append(rk)
            for i in range(k + 1, 8):
                f = G[k, i] * rk
                for j in range(i, 8):
                    G[i, j] = G[i, j] - f * G[k, j]
            dvec = d if dvec is None else jnp.where(row >= k, d, dvec)
        for k in range(8):
            F = jnp.where(row > k, M[k], 0.0) * r[k]
            for j in range(k + 1, 8):
                M[j] = M[j] - F * G[k, j]
            p = p - F * p[k:k+1, :]
            q = q - F * q[k:k+1, :]
            if not last:
                Fn = N[k] * r[k]
                for j in range(k + 1, 8):
                    N[j] = N[j] - Fn * G[k, j]
                w[m+1] = w[m+1] - Fn * p[k:k+1, :]
                v[m+1] = v[m+1] - Fn * q[k:k+1, :]
        yield
        s = lax.rsqrt(dvec)
        s = s * (1.5 - 0.5 * dvec * s * s)
        u8 = jnp.where(lane_iota() >= 8 * m + row, p * s, 0.0)
        v8 = q * s
        U.append(u8); V.append(v8)
        if m + 2 < n:
            t = u8.T
            for i in range(m + 2, n):
                ti = t[8*i:8*i+8, :]
                for k in range(8):
                    c = jnp.broadcast_to(ti[:, k:k+1], (8, B))
                    w[i] = w[i] - c * u8[k:k+1, :]
                    v[i] = v[i] - c * v8[k:k+1, :]
        yield
    out.append((jnp.concatenate(U, axis=0), jnp.concatenate(V, axis=0)))

def lane_iota():
    return lax.broadcasted_iota(jnp.int32, (8, B), 1)

def factor2(load0, load1):
    row = lax.broadcasted_iota(jnp.int32, (8, B), 0)
    lane = lane_iota()
    eye = [jnp.where(lane == row + 8 * i, 1.0, 0.0) for i in range(B // 8)]
    outs = [[], []]
    gens = [factor_gen(load0, eye, row, outs[0]), factor_gen(load1, eye, row, outs[1])]
    done = False
    while not done:
        done = True
        for g in gens:
            try:
                next(g); done = False
            except StopIteration:
                pass
    return outs[0][0], outs[1][0]

def chol_kernel(blocks, cov_ref, res_ref, sel_ref, fac_ref, out_ref, a_ref, r_ref, uv_ref):
    D = blocks * B
    a_ref[...] = cov_ref[...]
    r_ref[...] = res_ref[...]
    fac_ref[...] = jnp.zeros_like(fac_ref)

    def body(kb, _):
        off = pl.multiple_of(kb * B, B)
        def load(l):
            return lambda i: a_ref[l, pl.ds(pl.multiple_of(off + 8 * i, 8), 8), pl.ds(off, B)]
        for l, (u, v) in enumerate(factor2(load(0), load(1))):
            uv_ref[l] = v
            fac_ref[l, pl.ds(off, B), pl.ds(off, B)] = u.T
        for s in range(blocks):
            @pl.when(kb == s)
            def _():
                o = s * B
                vs = [split(uv_ref[l]) for l in range(2)]
                n = D - o - B
                if n:
                    for l in range(2):
                        panel = split(a_ref[l, o+B:D, o:o+B])
                        lp = dot3(panel, vs[l], NT)
                        fac_ref[l, o+B:D, o:o+B] = lp
                        lh = split(lp)
                        for j in range(s + 1, blocks, 2):
                            j2 = min(j + 2, blocks)
                            rj = (j - s - 1) * B
                            left = tuple(x[rj:] for x in lh)
                            right = tuple(x[rj:(j2 - s - 1) * B] for x in lh)
                            a_ref[l, j*B:D, j*B:j2*B] -= dot3(left, right, NT)
                vcat = tuple(jnp.concatenate([vs[0][i], vs[1][i]], axis=0) for i in range(2))
                if n:
                    lcat = split(jnp.concatenate([fac_ref[0, o+B:D, o:o+B], fac_ref[1, o+B:D, o:o+B]], axis=1))
                rows = r_ref.shape[0]
                step = 256
                for c in range(0, rows, step):
                    y = dot3(split(r_ref[c:c+step, o:o+B]), vcat, NT)
                    x0 = y[:, :B] * sel_ref[c:c+step, 0:B]
                    x1 = y[:, B:] * sel_ref[c:c+step, B:2*B]
                    out_ref[c:c+step, o:o+B] = x0 + x1
                    if n:
                        xs = split(jnp.concatenate([x0, x1], axis=1))
                        r_ref[c:c+step, o+B:D] -= dot3(xs, lcat, NT)
        return 0
    lax.fori_loop(0, blocks, body, 0)

def chol_whiten(cov, res, sel):
    D = cov.shape[1]
    return pl.pallas_call(
        functools.partial(chol_kernel, D // B),
        out_shape=(jax.ShapeDtypeStruct(cov.shape, jnp.float32), jax.ShapeDtypeStruct(res.shape, jnp.float32)),
        in_specs=[pl.BlockSpec(memory_space=pltpu.VMEM)] * 3,
        out_specs=[pl.BlockSpec(memory_space=pltpu.VMEM)] * 2,
        scratch_shapes=[pltpu.VMEM(cov.shape, jnp.float32), pltpu.VMEM(res.shape, jnp.float32), pltpu.VMEM((2, B, B), jnp.float32)],
        compiler_params=pltpu.CompilerParams(vmem_limit_bytes=60 * 2**20),
    )(cov, res, sel)

ridge = 0.1
SUB = 256


def on_device(rows, old_list, old_centroids, dest_device, new_local, centroids):
    n_group = lax.axis_size("group")
    n_member = lax.axis_size("member")
    devices = n_group * n_member
    row_dev = rows.shape[0]
    width = rows.shape[1]
    capacity = max(2, 2 * row_dev // devices)
    slots = devices * capacity
    old_hot = (
        old_list[:, None] == jnp.arange(old_centroids.shape[0], dtype=jnp.int32)[None, :]
    ).astype(jnp.float32)
    vectors = rows + jnp.dot(old_hot, old_centroids, precision=lax.Precision.HIGHEST)
    dest = dest_device[:, 0]
    index = jnp.arange(row_dev, dtype=jnp.int32)
    earlier = (dest[:, None] == dest[None, :]) & (index[None, :] < index[:, None])
    ranks = jnp.sum(earlier.astype(jnp.int32), axis=1)
    position = dest * capacity + ranks
    outgoing = jnp.zeros((slots, width), jnp.float32).at[position].set(vectors)
    out_tags = jnp.zeros((slots,), jnp.int32).at[position].set(new_local + 1)
    arrived, in_tags = (
        lax.all_to_all(
            outgoing.reshape(devices, capacity, width),
            ("group", "member"),
            split_axis=0,
            concat_axis=0,
            tiled=True,
        ),
        lax.all_to_all(
            out_tags.reshape(devices, capacity),
            ("group", "member"),
            split_axis=0,
            concat_axis=0,
            tiled=True,
        ),
    )
    flat = arrived.reshape(slots, width)
    flat_tags = in_tags.reshape(-1)
    lists = centroids.shape[0]
    select = (flat_tags[:, None] == jnp.arange(1, lists + 1, dtype=jnp.int32)[None, :]).astype(
        jnp.float32
    )
    residual = jnp.where(
        flat_tags[:, None] > 0,
        flat - jnp.dot(select, centroids, precision=lax.Precision.HIGHEST),
        0.0,
    )
    pieces = []
    for j in range(lists):
        masked = residual * select[:, j : j + 1]
        for c in range(0, width, SUB):
            gram = lax.dot_general(
                masked[:, c:],
                masked[:, c : c + SUB],
                (((0,), (0,)), ((), ())),
                precision=lax.Precision.HIGH,
            )
            pieces.append(gram)
    local_counts = jnp.sum(select, axis=0)
    summed, counts = lax.psum((jnp.concatenate(pieces), local_counts), "member")
    columns = []
    at = 0
    for j in range(lists):
        own = []
        for c in range(0, width, SUB):
            part = summed[at : at + width - c] / jnp.maximum(counts[j], 1.0)
            own.append(jnp.pad(part, ((c, 0), (0, 0))))
            at += width - c
        columns.append(jnp.concatenate(own, axis=1))
    covs = jnp.stack(columns) + ridge * jnp.eye(width, dtype=jnp.float32)[None]
    sel = jnp.repeat(select, B, axis=1)
    factors, result = chol_whiten(covs, residual, sel)
    return (result, factors)


def solution(mesh):
    return jax.shard_map(
        on_device,
        mesh=mesh,
        in_specs=(
            P(("group", "member"), None),
            P(("group", "member")),
            P(),
            P(("group", "member"), None),
            P(("group", "member")),
            P("group", None),
        ),
        out_specs=(P(("group", "member"), None), P("group", None, None)),
        check_vma=False,
    )
```

```python
import functools

import jax, jax.numpy as jnp
from jax import lax
from jax.experimental import pallas as pl
from jax.experimental.pallas import tpu as pltpu
from jax.sharding import PartitionSpec as P
NT = (((1,), (1,)), ((), ()))
NN = (((1,), (0,)), ((), ()))
B = 128
ridge = 0.1

def split(x):
    hi = x.astype(jnp.bfloat16)
    return hi, (x - hi.astype(jnp.float32)).astype(jnp.bfloat16)

def dot3(a, b, dims):
    f = functools.partial(lax.dot_general, dimension_numbers=dims, preferred_element_type=jnp.float32)
    return f(a[0], b[0]) + (f(a[0], b[1]) + f(a[1], b[0]))

def lane_iota():
    return lax.broadcasted_iota(jnp.int32, (8, B), 1)


def row_iota():
    return lax.broadcasted_iota(jnp.int32, (8, B), 0)


def across(x, k):
    return jnp.broadcast_to(x[:, k : k + 1], (8, B))


def down(x, k):
    return jnp.broadcast_to(x[k : k + 1, :], (8, B))


def factor_steps(load, out):
    n = B // 8
    row, lane = row_iota(), lane_iota()
    z = [load(i) for i in range(n)]
    upper, inverse = [], []
    for m in range(n):
        lo = 8 * m
        last = m == n - 1
        here = (lane >= lo) & (lane < lo + 8)
        p = z[m]
        M = [across(p, lo + k) for k in range(8)]
        q = jnp.where(here, jnp.where(lane == row + lo, 1.0, 0.0), p)
        if not last:
            x = z[m + 1]
            N = [across(x, lo + k) for k in range(8)]
            x = jnp.where(here, 0.0, x)
        yield
        for k in range(8):
            pivots = [down(M[j], k) for j in range(k, 8)]
            s = lax.rsqrt(pivots[0])
            g = [None] * k + [v * s for v in pivots]
            F = jnp.where(row > k, M[k] * s, 0.0)
            for j in range(k + 1, 8):
                M[j] = M[j] - F * g[j]
            p = jnp.where(row == k, p * s, p)
            q = jnp.where(row == k, q * s, q)
            pk, qk = down(p, k), down(q, k)
            p = p - F * pk
            q = q - F * qk
            if not last:
                f = N[k] * s
                for j in range(k + 1, 8):
                    N[j] = N[j] - f * g[j]
                x = x - f * qk
        yield
        if not last:
            z[m + 1] = x
        upper.append(jnp.where(lane >= lo + 8, q, jnp.where(lane >= lo + row, p, 0.0)))
        inverse.append(jnp.where(lane < lo + 8, q, 0.0))
        if m + 2 < n:
            qh, ql = split(q)
            d = lax.dot_general(
                jnp.concatenate([qh, ql, qh], 0),
                jnp.concatenate([qh, qh, ql], 0),
                (((0,), (0,)), ((), ())),
                preferred_element_type=jnp.float32,
            )
            for i in range(m + 2, n):
                z[i] = jnp.where(here, 0.0, z[i]) - d[8 * i : 8 * i + 8, :]
        yield
    out.append((jnp.concatenate(upper, axis=0), jnp.concatenate(inverse, axis=0)))


def factor2(load0, load1):
    outs = [[], []]
    pair = [factor_steps(load0, outs[0]), factor_steps(load1, outs[1])]
    for _ in zip(*pair):
        pass
    for one in pair:
        for _ in one:
            pass
    return outs[0][0], outs[1][0]


PW = 256
CHIPS = 8
MESH = pl.DeviceIdType.MESH


def rows_of(flat_ref, sel_ref, cent_ref, rows, cols, l):
    width = flat_ref[rows, cols].shape[1]
    s = sel_ref[rows, pl.ds(pl.multiple_of(l * B, B), B)]
    s = jnp.concatenate([s] * (width // B), axis=1)
    return (flat_ref[rows, cols] - cent_ref[pl.ds(l, 1), cols]) * s


def gram_kernel(chips, flat_ref, sel_ref, cent_ref, out_ref, rt_ref, give_ref, take_ref, acc_ref, part_ref, cov_ref,
                pair_send, pair_recv, rs_send, rs_recv, ag_send, ag_recv, fw_send, fw_recv, out_sem):
    D = flat_ref.shape[1]
    slots = flat_ref.shape[0]
    group = lax.axis_index("group")
    me = lax.axis_index("member")
    chip = me // 2
    core = lax.rem(me, 2)
    partner = chip * 2 + (1 - core)
    others = [lax.rem(chip + d, chips) * 2 + core for d in range(1, chips)]

    barrier = pltpu.get_barrier_semaphore()
    for peer in [partner] + others:
        pl.semaphore_signal(barrier, inc=1, device_id=(group, peer), device_id_type=MESH)
    pl.semaphore_wait(barrier, chips)

    panels = D // PW
    first = [sum(D - PW * i for i in range(p)) for p in range(panels)]

    def remote(src, dst, ss, rs, peer):
        return pltpu.make_async_remote_copy(
            src_ref=src, dst_ref=dst, send_sem=ss, recv_sem=rs, device_id=(group, peer), device_id_type=MESH)

    @pl.loop(0, slots // 256)
    def _(i):
        rows = pl.ds(pl.multiple_of(i * 256, 256), 256)
        for c in range(0, D, 256):
            cols = pl.ds(c, 256)
            x = rows_of(flat_ref, sel_ref, cent_ref, rows, cols, 0) + rows_of(flat_ref, sel_ref, cent_ref, rows, cols, 1)
            hi, lo = split(x.T)
            rt_ref[0, pl.ds(c, 256), rows] = hi
            rt_ref[1, pl.ds(c, 256), rows] = lo

    def gram(p, l, dst):
        cols = pl.ds(p * PW, PW)
        mh, ml = split(rows_of(flat_ref, sel_ref, cent_ref, pl.ds(0, slots), cols, l))
        dot = functools.partial(lax.dot_general, dimension_numbers=NN, preferred_element_type=jnp.float32)

        @pl.loop(0, (D - p * PW) // 256)
        def _(i):
            feat = pl.ds(pl.multiple_of(p * PW + i * 256, 256), 256)
            th, tl = rt_ref[0, feat, :], rt_ref[1, feat, :]
            dst[pl.ds(pl.multiple_of(first[p] + i * 256, 256), 256), :] = dot(th, mh) + (dot(th, ml) + dot(tl, mh))
        if p == 0:
            count = jnp.sum(sel_ref[:, pl.ds(pl.multiple_of(l * B, B), B)], axis=0, keepdims=True)
            dst[0:8, B:2 * B] = jnp.broadcast_to(count, (8, B))

    def span(p):
        return pl.ds(first[p], D - p * PW)

    def pair(p):
        return remote(give_ref.at[span(p), :], take_ref.at[span(p), :], pair_send.at[p], pair_recv.at[p], partner)

    def share(p):
        return (D - p * PW) // chips

    def scatter(p, d):
        n = share(p)
        t = lax.rem(chip + d, chips)
        return remote(
            acc_ref.at[pl.ds(pl.multiple_of(first[p] + t * n, 8), n), :],
            part_ref.at[d - 1, pl.ds(first[p] // chips, n), :],
            rs_send.at[p, d - 1], rs_recv.at[p, d - 1], others[d - 1])

    def own(p):
        n = share(p)
        return cov_ref.at[core, pl.ds(pl.multiple_of(p * PW + chip * n, 8), n), pl.ds(p * PW, PW)]

    def gather(p, d):
        return remote(own(p), own(p), ag_send.at[p, d - 1], ag_recv.at[p, d - 1], others[d - 1])

    def forward(p):
        ref = cov_ref.at[core, pl.ds(p * PW, D - p * PW), pl.ds(p * PW, PW)]
        return remote(ref, ref, fw_send.at[p], fw_recv.at[p], partner)

    def compute(p):
        gram(p, 1 - core, give_ref)
        pair(p).start()
        gram(p, core, acc_ref)

    def reduce_pair(p):
        pair(p).wait_recv()
        acc_ref[span(p), :] += take_ref[span(p), :]
        for d in range(1, chips):
            scatter(p, d).start()

    def reduce_chips(p):
        n = share(p)
        for d in range(1, chips):
            scatter(p, d).wait_recv()
        total = acc_ref[pl.ds(pl.multiple_of(first[p] + chip * n, 8), n), :]
        for d in range(1, chips):
            total = total + part_ref[d - 1, pl.ds(first[p] // chips, n), :]
        own(p)[...] = total
        for d in range(1, chips):
            gather(p, d).start()

    def spread(p):
        for d in range(1, chips):
            gather(p, d).wait_recv()
        forward(p).start()

    compute(0)
    compute(1)
    reduce_pair(0)
    compute(2)
    reduce_pair(1)
    compute(3)
    reduce_pair(2)
    reduce_pair(3)
    reduce_chips(0)
    reduce_chips(1)
    spread(0)
    reduce_chips(2)
    spread(1)
    reduce_chips(3)
    spread(2)
    spread(3)
    copies = []
    for p in range(panels):
        forward(p).wait_recv()
        region = (pl.ds(0, 2), pl.ds(p * PW, D - p * PW), pl.ds(p * PW, PW))
        copies.append(pltpu.make_async_copy(cov_ref.at[region], out_ref.at[region], out_sem.at[p]))
        copies[-1].start()
    for p in range(panels):
        pair(p).wait_send()
        for d in range(1, chips):
            scatter(p, d).wait_send()
            gather(p, d).wait_send()
        forward(p).wait_send()
        copies[p].wait()


def gram_sum(flat, sel, cent):
    slots, D = flat.shape
    panels = D // PW
    total = sum(D - PW * i for i in range(panels))
    dma = pltpu.SemaphoreType.DMA
    return pl.pallas_call(
        functools.partial(gram_kernel, CHIPS),
        out_shape=jax.ShapeDtypeStruct((2, D, D), jnp.float32),
        in_specs=[pl.BlockSpec(memory_space=pltpu.VMEM)] * 3,
        out_specs=pl.BlockSpec(memory_space=pl.ANY),
        scratch_shapes=[
            pltpu.VMEM((2, D, slots), jnp.bfloat16),
            pltpu.VMEM((total, PW), jnp.float32),
            pltpu.VMEM((total, PW), jnp.float32),
            pltpu.VMEM((total, PW), jnp.float32),
            pltpu.VMEM((CHIPS - 1, total // CHIPS, PW), jnp.float32),
            pltpu.VMEM((2, D, D), jnp.float32),
            dma((panels,)), dma((panels,)),
            dma((panels, CHIPS - 1)), dma((panels, CHIPS - 1)),
            dma((panels, CHIPS - 1)), dma((panels, CHIPS - 1)),
            dma((panels,)), dma((panels,)), dma((panels,)),
        ],
        compiler_params=pltpu.CompilerParams(
            collective_id=0, has_side_effects=True, vmem_limit_bytes=60 * 2**20),
    )(flat, sel, cent)


def chol_kernel(blocks, gram_ref, flat_ref, sel_ref, cent_ref, fac_ref, out_ref, a_ref, r_ref, uv_ref):
    D = blocks * B
    for l in range(2):
        count = jnp.maximum(gram_ref[l, 0:1, B:2 * B], 1.0)
        scale = jnp.concatenate([1.0 / count] * 2, axis=1)
        for p in range(0, D, 2 * B):
            a_ref[l, p:D, p:p + 2 * B] = gram_ref[l, p:D, p:p + 2 * B] * scale
        row, col = (lax.broadcasted_iota(jnp.int32, (B, B), i) for i in range(2))
        eye = jnp.where(row == col, ridge, 0.0)
        for p in range(0, D, B):
            a_ref[l, p:p + B, p:p + B] += eye
    for c in range(0, D, 256):
        cols = pl.ds(c, 256)
        every = pl.ds(0, flat_ref.shape[0])
        r_ref[:, c:c + 256] = rows_of(flat_ref, sel_ref, cent_ref, every, cols, 0) + rows_of(
            flat_ref, sel_ref, cent_ref, every, cols, 1)
    fac_ref[...] = jnp.zeros_like(fac_ref)

    def body(kb, _):
        off = pl.multiple_of(kb * B, B)
        def load(l):
            return lambda i: a_ref[l, pl.ds(pl.multiple_of(off + 8 * i, 8), 8), pl.ds(off, B)]
        for l, (u, v) in enumerate(factor2(load(0), load(1))):
            uv_ref[l] = v
            fac_ref[l, pl.ds(off, B), pl.ds(off, B)] = u.T
        for s in range(blocks):
            @pl.when(kb == s)
            def _():
                o = s * B
                vs = [split(uv_ref[l]) for l in range(2)]
                n = D - o - B
                if n:
                    for l in range(2):
                        panel = split(a_ref[l, o+B:D, o:o+B])
                        lp = dot3(panel, vs[l], NT)
                        fac_ref[l, o+B:D, o:o+B] = lp
                        lh = split(lp)
                        for j in range(s + 1, blocks, 2):
                            j2 = min(j + 2, blocks)
                            rj = (j - s - 1) * B
                            left = tuple(x[rj:] for x in lh)
                            right = tuple(x[rj:(j2 - s - 1) * B] for x in lh)
                            a_ref[l, j*B:D, j*B:j2*B] -= dot3(left, right, NT)
                vcat = tuple(jnp.concatenate([vs[0][i], vs[1][i]], axis=0) for i in range(2))
                if n:
                    lcat = split(jnp.concatenate([fac_ref[0, o+B:D, o:o+B], fac_ref[1, o+B:D, o:o+B]], axis=1))
                rows = r_ref.shape[0]
                step = 256
                for c in range(0, rows, step):
                    y = dot3(split(r_ref[c:c+step, o:o+B]), vcat, NT)
                    x0 = y[:, :B] * sel_ref[c:c+step, 0:B]
                    x1 = y[:, B:] * sel_ref[c:c+step, B:2*B]
                    out_ref[c:c+step, o:o+B] = x0 + x1
                    if n:
                        xs = split(jnp.concatenate([x0, x1], axis=1))
                        r_ref[c:c+step, o+B:D] -= dot3(xs, lcat, NT)
        return 0
    lax.fori_loop(0, blocks, body, 0)

def chol_whiten(gram, flat, sel, cent):
    D = gram.shape[1]
    return pl.pallas_call(
        functools.partial(chol_kernel, D // B),
        out_shape=(
            jax.ShapeDtypeStruct(gram.shape, jnp.float32),
            jax.ShapeDtypeStruct(flat.shape, jnp.float32),
        ),
        in_specs=[pl.BlockSpec(memory_space=pltpu.VMEM)] * 4,
        out_specs=[pl.BlockSpec(memory_space=pltpu.VMEM)] * 2,
        scratch_shapes=[
            pltpu.VMEM(gram.shape, jnp.float32),
            pltpu.VMEM(flat.shape, jnp.float32),
            pltpu.VMEM((2, B, B), jnp.float32),
        ],
        compiler_params=pltpu.CompilerParams(vmem_limit_bytes=60 * 2**20),
    )(gram, flat, sel, cent)


def on_device(rows, old_list, old_centroids, dest_device, new_local, centroids):
    n_group = lax.axis_size("group")
    n_member = lax.axis_size("member")
    devices = n_group * n_member
    row_dev = rows.shape[0]
    width = rows.shape[1]
    capacity = max(2, 2 * row_dev // devices)
    slots = devices * capacity
    old_hot = (
        old_list[:, None] == jnp.arange(old_centroids.shape[0], dtype=jnp.int32)[None, :]
    ).astype(jnp.float32)
    vectors = rows + jnp.dot(old_hot, old_centroids, precision=lax.Precision.HIGHEST)
    dest = dest_device[:, 0]
    index = jnp.arange(row_dev, dtype=jnp.int32)
    earlier = (dest[:, None] == dest[None, :]) & (index[None, :] < index[:, None])
    ranks = jnp.sum(earlier.astype(jnp.int32), axis=1)
    position = dest * capacity + ranks
    outgoing = jnp.zeros((slots, width), jnp.float32).at[position].set(vectors)
    out_tags = jnp.zeros((slots,), jnp.int32).at[position].set(new_local + 1)
    arrived, in_tags = (
        lax.all_to_all(
            outgoing.reshape(devices, capacity, width),
            ("group", "member"),
            split_axis=0,
            concat_axis=0,
            tiled=True,
        ),
        lax.all_to_all(
            out_tags.reshape(devices, capacity),
            ("group", "member"),
            split_axis=0,
            concat_axis=0,
            tiled=True,
        ),
    )
    flat = arrived.reshape(slots, width)
    flat_tags = in_tags.reshape(-1)
    lists = centroids.shape[0]
    lane = lax.broadcasted_iota(jnp.int32, (slots, lists * B), 1)
    sel = (flat_tags[:, None] == 1 + lane // B).astype(jnp.float32)
    gram = gram_sum(flat, sel, centroids)
    factors, result = chol_whiten(gram, flat, sel, centroids)
    return (result, factors)


def solution(mesh):
    return jax.shard_map(
        on_device,
        mesh=mesh,
        in_specs=(
            P(("group", "member"), None),
            P(("group", "member")),
            P(),
            P(("group", "member"), None),
            P(("group", "member")),
            P("group", None),
        ),
        out_specs=(P(("group", "member"), None), P("group", None, None)),
        check_vma=False,
    )
```

```python
import functools

import jax, jax.numpy as jnp
from jax import lax
from jax.experimental import pallas as pl
from jax.experimental.pallas import tpu as pltpu
from jax.sharding import PartitionSpec as P
NT = (((1,), (1,)), ((), ()))
NN = (((1,), (0,)), ((), ()))
B = 128
ridge = 0.1

def split(x):
    hi = x.astype(jnp.bfloat16)
    return hi, (x - hi.astype(jnp.float32)).astype(jnp.bfloat16)

def dot3(a, b, dims):
    f = functools.partial(lax.dot_general, dimension_numbers=dims, preferred_element_type=jnp.float32)
    return f(a[0], b[0]) + (f(a[0], b[1]) + f(a[1], b[0]))

def lane_iota():
    return lax.broadcasted_iota(jnp.int32, (8, B), 1)


def row_iota():
    return lax.broadcasted_iota(jnp.int32, (8, B), 0)


def across(x, k):
    return jnp.broadcast_to(x[:, k : k + 1], (8, B))


def down(x, k):
    return jnp.broadcast_to(x[k : k + 1, :], (8, B))


def factor_steps(load, out):
    n = B // 8
    row, lane = row_iota(), lane_iota()
    z = [load(i) for i in range(n)]
    upper, inverse = [], []
    for m in range(n):
        lo = 8 * m
        last = m == n - 1
        here = (lane >= lo) & (lane < lo + 8)
        p = z[m]
        M = [across(p, lo + k) for k in range(8)]
        q = jnp.where(here, jnp.where(lane == row + lo, 1.0, 0.0), p)
        if not last:
            x = z[m + 1]
            N = [across(x, lo + k) for k in range(8)]
            x = jnp.where(here, 0.0, x)
        yield
        for k in range(8):
            pivots = [down(M[j], k) for j in range(k, 8)]
            s = lax.rsqrt(pivots[0])
            g = [None] * k + [v * s for v in pivots]
            F = jnp.where(row > k, M[k] * s, 0.0)
            for j in range(k + 1, 8):
                M[j] = M[j] - F * g[j]
            p = jnp.where(row == k, p * s, p)
            q = jnp.where(row == k, q * s, q)
            pk, qk = down(p, k), down(q, k)
            p = p - F * pk
            q = q - F * qk
            if not last:
                f = N[k] * s
                for j in range(k + 1, 8):
                    N[j] = N[j] - f * g[j]
                x = x - f * qk
        yield
        if not last:
            z[m + 1] = x
        upper.append(jnp.where(lane >= lo + 8, q, jnp.where(lane >= lo + row, p, 0.0)))
        inverse.append(jnp.where(lane < lo + 8, q, 0.0))
        if m + 2 < n:
            qh, ql = split(q)
            d = lax.dot_general(
                jnp.concatenate([qh, ql, qh], 0),
                jnp.concatenate([qh, qh, ql], 0),
                (((0,), (0,)), ((), ())),
                preferred_element_type=jnp.float32,
            )
            for i in range(m + 2, n):
                z[i] = jnp.where(here, 0.0, z[i]) - d[8 * i : 8 * i + 8, :]
        yield
    out.append((jnp.concatenate(upper, axis=0), jnp.concatenate(inverse, axis=0)))


def factor2(load0, load1):
    outs = [[], []]
    pair = [factor_steps(load0, outs[0]), factor_steps(load1, outs[1])]
    for _ in zip(*pair):
        pass
    for one in pair:
        for _ in one:
            pass
    return outs[0][0], outs[1][0]


PW = 256
CHIPS = 8
MESH = pl.DeviceIdType.MESH


def rows_of(flat_ref, sel_ref, cent_ref, rows, cols, l):
    width = flat_ref[rows, cols].shape[1]
    s = sel_ref[rows, pl.ds(pl.multiple_of(l * B, B), B)]
    s = jnp.concatenate([s] * (width // B), axis=1)
    return (flat_ref[rows, cols] - cent_ref[pl.ds(l, 1), cols]) * s


def gram_kernel(chips, flat_ref, sel_ref, cent_ref, out_ref, rt_ref, give_ref, take_ref, acc_ref, part_ref, cov_ref,
                pair_send, pair_recv, rs_send, rs_recv, ag_send, ag_recv, fw_send, fw_recv, out_sem):
    D = flat_ref.shape[1]
    slots = flat_ref.shape[0]
    group = lax.axis_index("group")
    me = lax.axis_index("member")
    chip = me // 2
    core = lax.rem(me, 2)
    partner = chip * 2 + (1 - core)
    others = [lax.rem(chip + d, chips) * 2 + core for d in range(1, chips)]

    barrier = pltpu.get_barrier_semaphore()
    for peer in [partner] + others:
        pl.semaphore_signal(barrier, inc=1, device_id=(group, peer), device_id_type=MESH)
    pl.semaphore_wait(barrier, chips)

    panels = D // PW
    first = [sum(D - PW * i for i in range(p)) for p in range(panels)]

    def remote(src, dst, ss, rs, peer):
        return pltpu.make_async_remote_copy(
            src_ref=src, dst_ref=dst, send_sem=ss, recv_sem=rs, device_id=(group, peer), device_id_type=MESH)

    @pl.loop(0, slots // 256)
    def _(i):
        rows = pl.ds(pl.multiple_of(i * 256, 256), 256)
        for c in range(0, D, 256):
            cols = pl.ds(c, 256)
            x = rows_of(flat_ref, sel_ref, cent_ref, rows, cols, 0) + rows_of(flat_ref, sel_ref, cent_ref, rows, cols, 1)
            hi, lo = split(x.T)
            rt_ref[0, pl.ds(c, 256), rows] = hi
            rt_ref[1, pl.ds(c, 256), rows] = lo

    def gram(p, l, dst):
        cols = pl.ds(p * PW, PW)
        mh, ml = split(rows_of(flat_ref, sel_ref, cent_ref, pl.ds(0, slots), cols, l))
        dot = functools.partial(lax.dot_general, dimension_numbers=NN, preferred_element_type=jnp.float32)

        @pl.loop(0, (D - p * PW) // 256)
        def _(i):
            feat = pl.ds(pl.multiple_of(p * PW + i * 256, 256), 256)
            th, tl = rt_ref[0, feat, :], rt_ref[1, feat, :]
            dst[pl.ds(pl.multiple_of(first[p] + i * 256, 256), 256), :] = dot(th, mh) + (dot(th, ml) + dot(tl, mh))
        if p == 0:
            count = jnp.sum(sel_ref[:, pl.ds(pl.multiple_of(l * B, B), B)], axis=0, keepdims=True)
            dst[0:8, B:2 * B] = jnp.broadcast_to(count, (8, B))

    def span(p):
        return pl.ds(first[p], D - p * PW)

    def pair(p):
        return remote(give_ref.at[span(p), :], take_ref.at[span(p), :], pair_send.at[p], pair_recv.at[p], partner)

    def share(p):
        return (D - p * PW) // chips

    def scatter(p, d):
        n = share(p)
        t = lax.rem(chip + d, chips)
        return remote(
            acc_ref.at[pl.ds(pl.multiple_of(first[p] + t * n, 8), n), :],
            part_ref.at[d - 1, pl.ds(first[p] // chips, n), :],
            rs_send.at[p, d - 1], rs_recv.at[p, d - 1], others[d - 1])

    def own(p):
        n = share(p)
        return cov_ref.at[core, pl.ds(pl.multiple_of(p * PW + chip * n, 8), n), pl.ds(p * PW, PW)]

    def gather(p, d):
        return remote(own(p), own(p), ag_send.at[p, d - 1], ag_recv.at[p, d - 1], others[d - 1])

    def forward(p):
        ref = cov_ref.at[core, pl.ds(p * PW, D - p * PW), pl.ds(p * PW, PW)]
        return remote(ref, ref, fw_send.at[p], fw_recv.at[p], partner)

    def compute(p):
        gram(p, 1 - core, give_ref)
        pair(p).start()
        gram(p, core, acc_ref)

    def reduce_pair(p):
        pair(p).wait_recv()
        acc_ref[span(p), :] += take_ref[span(p), :]
        for d in range(1, chips):
            scatter(p, d).start()

    def reduce_chips(p):
        n = share(p)
        for d in range(1, chips):
            scatter(p, d).wait_recv()
        total = acc_ref[pl.ds(pl.multiple_of(first[p] + chip * n, 8), n), :]
        for d in range(1, chips):
            total = total + part_ref[d - 1, pl.ds(first[p] // chips, n), :]
        own(p)[...] = total
        for d in range(1, chips):
            gather(p, d).start()

    def spread(p):
        for d in range(1, chips):
            gather(p, d).wait_recv()
        forward(p).start()

    compute(0)
    compute(1)
    reduce_pair(0)
    compute(2)
    reduce_pair(1)
    compute(3)
    reduce_pair(2)
    reduce_pair(3)
    reduce_chips(0)
    reduce_chips(1)
    spread(0)
    reduce_chips(2)
    spread(1)
    reduce_chips(3)
    spread(2)
    spread(3)
    copies = []
    for p in range(panels):
        forward(p).wait_recv()
        region = (pl.ds(0, 2), pl.ds(p * PW, D - p * PW), pl.ds(p * PW, PW))
        copies.append(pltpu.make_async_copy(cov_ref.at[region], out_ref.at[region], out_sem.at[p]))
        copies[-1].start()
    for p in range(panels):
        pair(p).wait_send()
        for d in range(1, chips):
            scatter(p, d).wait_send()
            gather(p, d).wait_send()
        forward(p).wait_send()
        copies[p].wait()


def gram_sum(flat, sel, cent):
    slots, D = flat.shape
    panels = D // PW
    total = sum(D - PW * i for i in range(panels))
    dma = pltpu.SemaphoreType.DMA
    return pl.pallas_call(
        functools.partial(gram_kernel, CHIPS),
        out_shape=jax.ShapeDtypeStruct((2, D, D), jnp.float32),
        in_specs=[pl.BlockSpec(memory_space=pltpu.VMEM)] * 3,
        out_specs=pl.BlockSpec(memory_space=pl.ANY),
        scratch_shapes=[
            pltpu.VMEM((2, D, slots), jnp.bfloat16),
            pltpu.VMEM((total, PW), jnp.float32),
            pltpu.VMEM((total, PW), jnp.float32),
            pltpu.VMEM((total, PW), jnp.float32),
            pltpu.VMEM((CHIPS - 1, total // CHIPS, PW), jnp.float32),
            pltpu.VMEM((2, D, D), jnp.float32),
            dma((panels,)), dma((panels,)),
            dma((panels, CHIPS - 1)), dma((panels, CHIPS - 1)),
            dma((panels, CHIPS - 1)), dma((panels, CHIPS - 1)),
            dma((panels,)), dma((panels,)), dma((panels,)),
        ],
        compiler_params=pltpu.CompilerParams(
            collective_id=0, has_side_effects=True, vmem_limit_bytes=60 * 2**20),
    )(flat, sel, cent)


def move_kernel(groups, members, vec_ref, dest_ref, rank_ref, tag_ref, flat_ref, tags_ref, split_ref, data_ref, mark_ref,
                data_send, data_recv, mark_send, mark_recv, own_sem):
    group = lax.axis_index("group")
    member = lax.axis_index("member")
    me = group * members + member
    devices = groups * members
    cap = data_ref.shape[0] // devices
    row_dev, D = vec_ref.shape
    block = members * cap

    x = vec_ref[...]
    for i in range(3):
        part = x.astype(jnp.bfloat16)
        split_ref[i] = part
        x = x - part.astype(jnp.float32)

    dest = dest_ref[...]
    rank = rank_ref[...]
    device = lax.broadcasted_iota(jnp.int32, (devices, row_dev), 0)
    slot = lax.broadcasted_iota(jnp.int32, (B, row_dev), 0)
    to_device = jnp.where(device == dest, 1.0, 0.0).astype(jnp.bfloat16)
    to_slot = jnp.where(slot == rank, tag_ref[...], 0.0).astype(jnp.bfloat16)
    marks = lax.dot_general(to_device, to_slot, NT, preferred_element_type=jnp.float32)
    mark_ref[...] = marks.reshape(devices, 1, B)

    def data(g, m, there):
        rows = pl.ds(pl.multiple_of((g * members + m) * cap, cap), cap)
        mine = pl.ds(pl.multiple_of(me * cap, cap), cap)
        if there is None:
            return pltpu.make_async_copy(data_ref.at[rows, :], flat_ref.at[mine, :], own_sem.at[0])
        return pltpu.make_async_remote_copy(
            src_ref=data_ref.at[rows, :], dst_ref=flat_ref.at[mine, :], send_sem=data_send, recv_sem=data_recv,
            device_id=there, device_id_type=MESH)

    def mark(g, m, there):
        if there is None:
            return pltpu.make_async_copy(mark_ref.at[pl.ds(me, 1)], tags_ref.at[pl.ds(me, 1)], own_sem.at[1])
        return pltpu.make_async_remote_copy(
            src_ref=mark_ref.at[pl.ds(g * members + m, 1)], dst_ref=tags_ref.at[pl.ds(me, 1)],
            send_sem=mark_send, recv_sem=mark_recv, device_id=there, device_id_type=MESH)

    @pl.loop(0, groups)
    def _(i):
        g = lax.rem(group + i, groups)
        base = g * block
        hit = slot[:block] + base == dest * cap + rank
        pick = jnp.where(hit, 1.0, 0.0).astype(jnp.bfloat16)
        at = pl.ds(pl.multiple_of(base, block), block)
        for c in range(0, D, 256):
            a, b, d = (
                lax.dot_general(pick, split_ref[k, :, c:c + 256], NN, preferred_element_type=jnp.float32)
                for k in range(3)
            )
            data_ref[at, c:c + 256] = (a + b) + d

        @pl.loop(0, members)
        def _(j):
            m = lax.rem(member + j, members)

            @pl.when(i + j > 0)
            def _():
                data(g, m, (g, m)).start()
                mark(g, m, (g, m)).start()

    data(group, member, None).start()
    mark(group, member, None).start()
    data(group, member, None).wait()
    mark(group, member, None).wait()
    rest = pl.ds(0, (devices - 1) * cap)
    far = lax.rem(group + 1, groups)
    everything = pltpu.make_async_remote_copy(
        src_ref=data_ref.at[rest, :], dst_ref=flat_ref.at[rest, :], send_sem=data_send, recv_sem=data_recv,
        device_id=(far, member), device_id_type=MESH)
    rest = pl.ds(0, devices - 1)
    marked = pltpu.make_async_remote_copy(
        src_ref=mark_ref.at[rest], dst_ref=tags_ref.at[rest], send_sem=mark_send, recv_sem=mark_recv,
        device_id=(far, member), device_id_type=MESH)
    everything.wait_send()
    marked.wait_send()
    marked.wait_recv()
    everything.wait_recv()


def move(vectors, dest, rank, tag, groups, members, slots):
    row_dev, D = vectors.shape
    dma = pltpu.SemaphoreType.DMA
    devices = groups * members
    return pl.pallas_call(
        functools.partial(move_kernel, groups, members),
        out_shape=(
            jax.ShapeDtypeStruct((slots, D), jnp.float32),
            jax.ShapeDtypeStruct((devices, 1, B), jnp.float32),
        ),
        in_specs=[pl.BlockSpec(memory_space=pltpu.VMEM)] * 4,
        out_specs=[pl.BlockSpec(memory_space=pl.ANY)] * 2,
        scratch_shapes=[
            pltpu.VMEM((3, row_dev, D), jnp.bfloat16),
            pltpu.VMEM((slots, D), jnp.float32),
            pltpu.VMEM((devices, 1, B), jnp.float32),
            dma, dma, dma, dma, dma((2,)),
        ],
        compiler_params=pltpu.CompilerParams(has_side_effects=True, vmem_limit_bytes=60 * 2**20),
    )(vectors, dest, rank, tag)


def chol_kernel(blocks, gram_ref, flat_ref, sel_ref, cent_ref, fac_ref, out_ref, a_ref, r_ref, uv_ref):
    D = blocks * B
    for l in range(2):
        count = jnp.maximum(gram_ref[l, 0:1, B:2 * B], 1.0)
        scale = jnp.concatenate([1.0 / count] * 2, axis=1)
        for p in range(0, D, 2 * B):
            a_ref[l, p:D, p:p + 2 * B] = gram_ref[l, p:D, p:p + 2 * B] * scale
        row, col = (lax.broadcasted_iota(jnp.int32, (B, B), i) for i in range(2))
        eye = jnp.where(row == col, ridge, 0.0)
        for p in range(0, D, B):
            a_ref[l, p:p + B, p:p + B] += eye
    for c in range(0, D, 256):
        cols = pl.ds(c, 256)
        every = pl.ds(0, flat_ref.shape[0])
        r_ref[:, c:c + 256] = rows_of(flat_ref, sel_ref, cent_ref, every, cols, 0) + rows_of(
            flat_ref, sel_ref, cent_ref, every, cols, 1)
    fac_ref[...] = jnp.zeros_like(fac_ref)

    def body(kb, _):
        off = pl.multiple_of(kb * B, B)
        def load(l):
            return lambda i: a_ref[l, pl.ds(pl.multiple_of(off + 8 * i, 8), 8), pl.ds(off, B)]
        for l, (u, v) in enumerate(factor2(load(0), load(1))):
            uv_ref[l] = v
            fac_ref[l, pl.ds(off, B), pl.ds(off, B)] = u.T
        for s in range(blocks):
            @pl.when(kb == s)
            def _():
                o = s * B
                vs = [split(uv_ref[l]) for l in range(2)]
                n = D - o - B
                if n:
                    for l in range(2):
                        panel = split(a_ref[l, o+B:D, o:o+B])
                        lp = dot3(panel, vs[l], NT)
                        fac_ref[l, o+B:D, o:o+B] = lp
                        lh = split(lp)
                        for j in range(s + 1, blocks, 2):
                            j2 = min(j + 2, blocks)
                            rj = (j - s - 1) * B
                            left = tuple(x[rj:] for x in lh)
                            right = tuple(x[rj:(j2 - s - 1) * B] for x in lh)
                            a_ref[l, j*B:D, j*B:j2*B] -= dot3(left, right, NT)
                vcat = tuple(jnp.concatenate([vs[0][i], vs[1][i]], axis=0) for i in range(2))
                if n:
                    lcat = split(jnp.concatenate([fac_ref[0, o+B:D, o:o+B], fac_ref[1, o+B:D, o:o+B]], axis=1))
                rows = r_ref.shape[0]
                step = 256
                for c in range(0, rows, step):
                    y = dot3(split(r_ref[c:c+step, o:o+B]), vcat, NT)
                    x0 = y[:, :B] * sel_ref[c:c+step, 0:B]
                    x1 = y[:, B:] * sel_ref[c:c+step, B:2*B]
                    out_ref[c:c+step, o:o+B] = x0 + x1
                    if n:
                        xs = split(jnp.concatenate([x0, x1], axis=1))
                        r_ref[c:c+step, o+B:D] -= dot3(xs, lcat, NT)
        return 0
    lax.fori_loop(0, blocks, body, 0)

def chol_whiten(gram, flat, sel, cent):
    D = gram.shape[1]
    return pl.pallas_call(
        functools.partial(chol_kernel, D // B),
        out_shape=(
            jax.ShapeDtypeStruct(gram.shape, jnp.float32),
            jax.ShapeDtypeStruct(flat.shape, jnp.float32),
        ),
        in_specs=[pl.BlockSpec(memory_space=pltpu.VMEM)] * 4,
        out_specs=[pl.BlockSpec(memory_space=pltpu.VMEM)] * 2,
        scratch_shapes=[
            pltpu.VMEM(gram.shape, jnp.float32),
            pltpu.VMEM(flat.shape, jnp.float32),
            pltpu.VMEM((2, B, B), jnp.float32),
        ],
        compiler_params=pltpu.CompilerParams(vmem_limit_bytes=60 * 2**20),
    )(gram, flat, sel, cent)


def on_device(rows, old_list, old_centroids, dest_device, new_local, centroids):
    n_group = lax.axis_size("group")
    n_member = lax.axis_size("member")
    devices = n_group * n_member
    row_dev = rows.shape[0]
    width = rows.shape[1]
    capacity = max(2, 2 * row_dev // devices)
    slots = devices * capacity
    old_hot = (
        old_list[:, None] == jnp.arange(old_centroids.shape[0], dtype=jnp.int32)[None, :]
    ).astype(jnp.float32)
    vectors = rows + jnp.dot(old_hot, old_centroids, precision=lax.Precision.HIGHEST)
    dest = dest_device[:, 0]
    index = jnp.arange(row_dev, dtype=jnp.int32)
    earlier = (dest[:, None] == dest[None, :]) & (index[None, :] < index[:, None])
    ranks = jnp.sum(earlier.astype(jnp.int32), axis=1)
    tag = (new_local + 1).astype(jnp.float32)
    flat, marks = move(vectors, dest[None, :], ranks[None, :], tag[None, :], n_group, n_member, slots)
    flat_tags = marks.reshape(devices, B)[:, :capacity].reshape(-1)
    lists = centroids.shape[0]
    lane = lax.broadcasted_iota(jnp.int32, (slots, lists * B), 1)
    sel = (flat_tags[:, None] == (1 + lane // B).astype(jnp.float32)).astype(jnp.float32)
    gram = gram_sum(flat, sel, centroids)
    factors, result = chol_whiten(gram, flat, sel, centroids)
    return (result, factors)


def solution(mesh):
    return jax.shard_map(
        on_device,
        mesh=mesh,
        in_specs=(
            P(("group", "member"), None),
            P(("group", "member")),
            P(),
            P(("group", "member"), None),
            P(("group", "member")),
            P("group", None),
        ),
        out_specs=(P(("group", "member"), None), P("group", None, None)),
        check_vma=False,
    )
```

```python
import functools

import jax, jax.numpy as jnp
from jax import lax
from jax.experimental import pallas as pl
from jax.experimental.pallas import tpu as pltpu
from jax.sharding import PartitionSpec as P
NT = (((1,), (1,)), ((), ()))
NN = (((1,), (0,)), ((), ()))
B = 128
ridge = 0.1

def split(x):
    hi = x.astype(jnp.bfloat16)
    return hi, (x - hi.astype(jnp.float32)).astype(jnp.bfloat16)

def dot3(a, b, dims):
    f = functools.partial(lax.dot_general, dimension_numbers=dims, preferred_element_type=jnp.float32)
    return f(a[0], b[0]) + (f(a[0], b[1]) + f(a[1], b[0]))

def lane_iota():
    return lax.broadcasted_iota(jnp.int32, (8, B), 1)


def row_iota():
    return lax.broadcasted_iota(jnp.int32, (8, B), 0)


def across(x, k):
    return jnp.broadcast_to(x[:, k : k + 1], (8, B))


def down(x, k):
    return jnp.broadcast_to(x[k : k + 1, :], (8, B))


def factor_steps(load, out):
    n = B // 8
    row, lane = row_iota(), lane_iota()
    z = [load(i) for i in range(n)]
    upper, inverse = [], []
    for m in range(n):
        lo = 8 * m
        last = m == n - 1
        here = (lane >= lo) & (lane < lo + 8)
        p = z[m]
        M = [across(p, lo + k) for k in range(8)]
        q = jnp.where(here, jnp.where(lane == row + lo, 1.0, 0.0), p)
        if not last:
            x = z[m + 1]
            N = [across(x, lo + k) for k in range(8)]
            x = jnp.where(here, 0.0, x)
        yield
        for k in range(8):
            pivots = [down(M[j], k) for j in range(k, 8)]
            s = lax.rsqrt(pivots[0])
            g = [None] * k + [v * s for v in pivots]
            F = jnp.where(row > k, M[k] * s, 0.0)
            for j in range(k + 1, 8):
                M[j] = M[j] - F * g[j]
            p = jnp.where(row == k, p * s, p)
            q = jnp.where(row == k, q * s, q)
            pk, qk = down(p, k), down(q, k)
            p = p - F * pk
            q = q - F * qk
            if not last:
                f = N[k] * s
                for j in range(k + 1, 8):
                    N[j] = N[j] - f * g[j]
                x = x - f * qk
        yield
        if not last:
            z[m + 1] = x
        upper.append(jnp.where(lane >= lo + 8, q, jnp.where(lane >= lo + row, p, 0.0)))
        inverse.append(jnp.where(lane < lo + 8, q, 0.0))
        if m + 2 < n:
            qh, ql = split(q)
            d = lax.dot_general(
                jnp.concatenate([qh, ql, qh], 0),
                jnp.concatenate([qh, qh, ql], 0),
                (((0,), (0,)), ((), ())),
                preferred_element_type=jnp.float32,
            )
            for i in range(m + 2, n):
                z[i] = jnp.where(here, 0.0, z[i]) - d[8 * i : 8 * i + 8, :]
        yield
    out.append((jnp.concatenate(upper, axis=0), jnp.concatenate(inverse, axis=0)))


def factor2(load0, load1):
    outs = [[], []]
    pair = [factor_steps(load0, outs[0]), factor_steps(load1, outs[1])]
    for _ in zip(*pair):
        pass
    for one in pair:
        for _ in one:
            pass
    return outs[0][0], outs[1][0]


PW = 256
CHIPS = 8
MESH = pl.DeviceIdType.MESH


def rows_of(flat_ref, sel_ref, cent_ref, rows, cols, l):
    width = flat_ref[rows, cols].shape[1]
    s = sel_ref[rows, pl.ds(pl.multiple_of(l * B, B), B)]
    s = jnp.concatenate([s] * (width // B), axis=1)
    return (flat_ref[rows, cols] - cent_ref[pl.ds(l, 1), cols]) * s


def gram_kernel(chips, flat_ref, sel_ref, cent_ref, out_ref, rt_ref, give_ref, take_ref, acc_ref, part_ref, cov_ref,
                pair_send, pair_recv, rs_send, rs_recv, ag_send, ag_recv, fw_send, fw_recv, out_sem):
    D = flat_ref.shape[1]
    slots = flat_ref.shape[0]
    group = lax.axis_index("group")
    me = lax.axis_index("member")
    chip = me // 2
    core = lax.rem(me, 2)
    partner = chip * 2 + (1 - core)
    others = [lax.rem(chip + d, chips) * 2 + core for d in range(1, chips)]

    barrier = pltpu.get_barrier_semaphore()
    for peer in [partner] + others:
        pl.semaphore_signal(barrier, inc=1, device_id=(group, peer), device_id_type=MESH)
    pl.semaphore_wait(barrier, chips)

    panels = D // PW
    first = [sum(D - PW * i for i in range(p)) for p in range(panels)]

    def remote(src, dst, ss, rs, peer):
        return pltpu.make_async_remote_copy(
            src_ref=src, dst_ref=dst, send_sem=ss, recv_sem=rs, device_id=(group, peer), device_id_type=MESH)

    @pl.loop(0, slots // 256)
    def _(i):
        rows = pl.ds(pl.multiple_of(i * 256, 256), 256)
        for c in range(0, D, 256):
            cols = pl.ds(c, 256)
            x = rows_of(flat_ref, sel_ref, cent_ref, rows, cols, 0) + rows_of(flat_ref, sel_ref, cent_ref, rows, cols, 1)
            hi, lo = split(x.T)
            rt_ref[0, pl.ds(c, 256), rows] = hi
            rt_ref[1, pl.ds(c, 256), rows] = lo

    def gram(p, l, dst):
        cols = pl.ds(p * PW, PW)
        mh, ml = split(rows_of(flat_ref, sel_ref, cent_ref, pl.ds(0, slots), cols, l))
        dot = functools.partial(lax.dot_general, dimension_numbers=NN, preferred_element_type=jnp.float32)

        @pl.loop(0, (D - p * PW) // 256)
        def _(i):
            feat = pl.ds(pl.multiple_of(p * PW + i * 256, 256), 256)
            th, tl = rt_ref[0, feat, :], rt_ref[1, feat, :]
            dst[pl.ds(pl.multiple_of(first[p] + i * 256, 256), 256), :] = dot(th, mh) + (dot(th, ml) + dot(tl, mh))
        if p == 0:
            count = jnp.sum(sel_ref[:, pl.ds(pl.multiple_of(l * B, B), B)], axis=0, keepdims=True)
            dst[0:8, B:2 * B] = jnp.broadcast_to(count, (8, B))

    def span(p):
        return pl.ds(first[p], D - p * PW)

    def pair(p):
        return remote(give_ref.at[span(p), :], take_ref.at[span(p), :], pair_send.at[p], pair_recv.at[p], partner)

    def share(p):
        return (D - p * PW) // chips

    def scatter(p, d):
        n = share(p)
        t = lax.rem(chip + d, chips)
        return remote(
            acc_ref.at[pl.ds(pl.multiple_of(first[p] + t * n, 8), n), :],
            part_ref.at[d - 1, pl.ds(first[p] // chips, n), :],
            rs_send.at[p, d - 1], rs_recv.at[p, d - 1], others[d - 1])

    def own(p):
        n = share(p)
        return cov_ref.at[core, pl.ds(pl.multiple_of(p * PW + chip * n, 8), n), pl.ds(p * PW, PW)]

    def gather(p, d):
        return remote(own(p), own(p), ag_send.at[p, d - 1], ag_recv.at[p, d - 1], others[d - 1])

    def forward(p):
        ref = cov_ref.at[core, pl.ds(p * PW, D - p * PW), pl.ds(p * PW, PW)]
        return remote(ref, ref, fw_send.at[p], fw_recv.at[p], partner)

    def compute(p):
        gram(p, 1 - core, give_ref)
        pair(p).start()
        gram(p, core, acc_ref)

    def reduce_pair(p):
        pair(p).wait_recv()
        acc_ref[span(p), :] += take_ref[span(p), :]
        for d in range(1, chips):
            scatter(p, d).start()

    def reduce_chips(p):
        n = share(p)
        for d in range(1, chips):
            scatter(p, d).wait_recv()
        total = acc_ref[pl.ds(pl.multiple_of(first[p] + chip * n, 8), n), :]
        for d in range(1, chips):
            total = total + part_ref[d - 1, pl.ds(first[p] // chips, n), :]
        own(p)[...] = total
        for d in range(1, chips):
            gather(p, d).start()

    def spread(p):
        for d in range(1, chips):
            gather(p, d).wait_recv()
        forward(p).start()

    compute(0)
    compute(1)
    reduce_pair(0)
    compute(2)
    reduce_pair(1)
    compute(3)
    reduce_pair(2)
    reduce_pair(3)
    reduce_chips(0)
    reduce_chips(1)
    spread(0)
    reduce_chips(2)
    spread(1)
    reduce_chips(3)
    spread(2)
    spread(3)
    copies = []
    for p in range(panels):
        forward(p).wait_recv()
        region = (pl.ds(0, 2), pl.ds(p * PW, D - p * PW), pl.ds(p * PW, PW))
        copies.append(pltpu.make_async_copy(cov_ref.at[region], out_ref.at[region], out_sem.at[p]))
        copies[-1].start()
    for p in range(panels):
        pair(p).wait_send()
        for d in range(1, chips):
            scatter(p, d).wait_send()
            gather(p, d).wait_send()
        forward(p).wait_send()
        copies[p].wait()


def gram_sum(flat, sel, cent):
    slots, D = flat.shape
    panels = D // PW
    total = sum(D - PW * i for i in range(panels))
    dma = pltpu.SemaphoreType.DMA
    return pl.pallas_call(
        functools.partial(gram_kernel, CHIPS),
        out_shape=jax.ShapeDtypeStruct((2, D, D), jnp.float32),
        in_specs=[pl.BlockSpec(memory_space=pltpu.VMEM)] * 3,
        out_specs=pl.BlockSpec(memory_space=pl.ANY),
        scratch_shapes=[
            pltpu.VMEM((2, D, slots), jnp.bfloat16),
            pltpu.VMEM((total, PW), jnp.float32),
            pltpu.VMEM((total, PW), jnp.float32),
            pltpu.VMEM((total, PW), jnp.float32),
            pltpu.VMEM((CHIPS - 1, total // CHIPS, PW), jnp.float32),
            pltpu.VMEM((2, D, D), jnp.float32),
            dma((panels,)), dma((panels,)),
            dma((panels, CHIPS - 1)), dma((panels, CHIPS - 1)),
            dma((panels, CHIPS - 1)), dma((panels, CHIPS - 1)),
            dma((panels,)), dma((panels,)), dma((panels,)),
        ],
        compiler_params=pltpu.CompilerParams(
            collective_id=0, has_side_effects=True, vmem_limit_bytes=60 * 2**20),
    )(flat, sel, cent)


def full(n, k):
    return jnp.full(jnp.shape(k), n, jnp.int32)


def over(k, n):
    return lax.div(k, full(n, k))


def target(k, group, member):
    x = lax.rem(member // 2 + k, full(4, k))
    y = lax.rem(group + over(k, 4) + k, full(4, k))
    z = lax.rem(member // 8 * 2 + group // 4 + over(k, 16) + k + over(k, 4), full(4, k))
    core = lax.rem(member + over(k, 64), full(2, k))
    return lax.rem(z, full(2, k)) * 4 + y, over(z, 2) * 8 + x * 2 + core


def move_kernel(groups, members, vec_ref, dest_ref, rank_ref, tag_ref, flat_ref, tags_ref, split_ref, data_ref, mark_ref,
                data_send, data_recv, mark_send, mark_recv, own_sem):
    group = lax.axis_index("group")
    member = lax.axis_index("member")
    me = group * members + member
    devices = groups * members
    cap = data_ref.shape[0] // devices
    row_dev, D = vec_ref.shape

    barrier = pltpu.get_barrier_semaphore()

    @pl.loop(1, devices)
    def _(k):
        pl.semaphore_signal(barrier, inc=1, device_id=target(k, group, member), device_id_type=MESH)

    x = vec_ref[...]
    for i in range(3):
        part = x.astype(jnp.bfloat16)
        split_ref[i] = part
        x = x - part.astype(jnp.float32)

    dest = dest_ref[...]
    rank = rank_ref[...]
    device = lax.broadcasted_iota(jnp.int32, (devices, row_dev), 0)
    slot = lax.broadcasted_iota(jnp.int32, (B, row_dev), 0)
    to_device = jnp.where(device == dest, 1.0, 0.0).astype(jnp.bfloat16)
    to_slot = jnp.where(slot == rank, tag_ref[...], 0.0).astype(jnp.bfloat16)
    marks = lax.dot_general(to_device, to_slot, NT, preferred_element_type=jnp.float32)
    mark_ref[...] = marks.reshape(devices, 1, B)

    mine = pl.ds(pl.multiple_of(me * cap, cap), cap)

    def data(k, there):
        return pltpu.make_async_remote_copy(
            src_ref=data_ref.at[pl.ds(pl.multiple_of(k * cap, cap), cap), :], dst_ref=flat_ref.at[mine, :],
            send_sem=data_send, recv_sem=data_recv, device_id=there, device_id_type=MESH)

    def mark(there):
        return pltpu.make_async_remote_copy(
            src_ref=mark_ref.at[pl.ds(there[0] * members + there[1], 1)], dst_ref=tags_ref.at[pl.ds(me, 1)],
            send_sem=mark_send, recv_sem=mark_recv, device_id=there, device_id_type=MESH)

    many = B // cap
    own = (
        pltpu.make_async_copy(data_ref.at[pl.ds(0, cap), :], flat_ref.at[mine, :], own_sem.at[0]),
        pltpu.make_async_copy(mark_ref.at[pl.ds(me, 1)], tags_ref.at[pl.ds(me, 1)], own_sem.at[1]),
    )
    line = lax.broadcasted_iota(jnp.int32, (B, B), 0)

    @pl.loop(0, devices // many)
    def _(i):
        g, m = target(i * many + (line >> 3), group, member)
        ids = (g * members + m) * cap + (line & 7)
        hit = jnp.concatenate([ids] * (row_dev // B), axis=1) == dest * cap + rank
        pick = jnp.where(hit, 1.0, 0.0).astype(jnp.bfloat16)
        at = pl.ds(pl.multiple_of(i * B, B), B)
        for c in range(0, D, 256):
            a, b, d = (
                lax.dot_general(pick, split_ref[k, :, c:c + 256], NN, preferred_element_type=jnp.float32)
                for k in range(3)
            )
            data_ref[at, c:c + 256] = (a + b) + d

        @pl.when(i == 0)
        def _():
            pl.semaphore_wait(barrier, devices - 1)
            for copy in own:
                copy.start()

        @pl.loop(0, many)
        def _(j):
            k = i * many + j

            @pl.when(k > 0)
            def _():
                there = target(k, group, member)
                data(k, there).start()
                mark(there).start()

    for copy in own:
        copy.wait()
    rest = pl.ds(0, (devices - 1) * cap)
    far = lax.rem(group + 1, groups)
    everything = pltpu.make_async_remote_copy(
        src_ref=data_ref.at[rest, :], dst_ref=flat_ref.at[rest, :], send_sem=data_send, recv_sem=data_recv,
        device_id=(far, member), device_id_type=MESH)
    rest = pl.ds(0, devices - 1)
    marked = pltpu.make_async_remote_copy(
        src_ref=mark_ref.at[rest], dst_ref=tags_ref.at[rest], send_sem=mark_send, recv_sem=mark_recv,
        device_id=(far, member), device_id_type=MESH)
    everything.wait_send()
    marked.wait_send()
    marked.wait_recv()
    everything.wait_recv()


def move(vectors, dest, rank, tag, groups, members, slots):
    row_dev, D = vectors.shape
    dma = pltpu.SemaphoreType.DMA
    devices = groups * members
    return pl.pallas_call(
        functools.partial(move_kernel, groups, members),
        out_shape=(
            jax.ShapeDtypeStruct((slots, D), jnp.float32),
            jax.ShapeDtypeStruct((devices, 1, B), jnp.float32),
        ),
        in_specs=[pl.BlockSpec(memory_space=pltpu.VMEM)] * 4,
        out_specs=[pl.BlockSpec(memory_space=pl.ANY)] * 2,
        scratch_shapes=[
            pltpu.VMEM((3, row_dev, D), jnp.bfloat16),
            pltpu.VMEM((slots, D), jnp.float32),
            pltpu.VMEM((devices, 1, B), jnp.float32),
            dma, dma, dma, dma, dma((2,)),
        ],
        compiler_params=pltpu.CompilerParams(collective_id=1, has_side_effects=True, vmem_limit_bytes=60 * 2**20),
    )(vectors, dest, rank, tag)


def chol_kernel(blocks, gram_ref, flat_ref, sel_ref, cent_ref, fac_ref, out_ref, a_ref, r_ref, uv_ref):
    D = blocks * B
    for l in range(2):
        count = jnp.maximum(gram_ref[l, 0:1, B:2 * B], 1.0)
        scale = jnp.concatenate([1.0 / count] * 2, axis=1)
        for p in range(0, D, 2 * B):
            a_ref[l, p:D, p:p + 2 * B] = gram_ref[l, p:D, p:p + 2 * B] * scale
        row, col = (lax.broadcasted_iota(jnp.int32, (B, B), i) for i in range(2))
        eye = jnp.where(row == col, ridge, 0.0)
        for p in range(0, D, B):
            a_ref[l, p:p + B, p:p + B] += eye
    for c in range(0, D, 256):
        cols = pl.ds(c, 256)
        every = pl.ds(0, flat_ref.shape[0])
        r_ref[:, c:c + 256] = rows_of(flat_ref, sel_ref, cent_ref, every, cols, 0) + rows_of(
            flat_ref, sel_ref, cent_ref, every, cols, 1)
    fac_ref[...] = jnp.zeros_like(fac_ref)

    def body(kb, _):
        off = pl.multiple_of(kb * B, B)
        def load(l):
            return lambda i: a_ref[l, pl.ds(pl.multiple_of(off + 8 * i, 8), 8), pl.ds(off, B)]
        for l, (u, v) in enumerate(factor2(load(0), load(1))):
            uv_ref[l] = v
            fac_ref[l, pl.ds(off, B), pl.ds(off, B)] = u.T
        for s in range(blocks):
            @pl.when(kb == s)
            def _():
                o = s * B
                vs = [split(uv_ref[l]) for l in range(2)]
                n = D - o - B
                if n:
                    for l in range(2):
                        panel = split(a_ref[l, o+B:D, o:o+B])
                        lp = dot3(panel, vs[l], NT)
                        fac_ref[l, o+B:D, o:o+B] = lp
                        lh = split(lp)
                        for j in range(s + 1, blocks, 2):
                            j2 = min(j + 2, blocks)
                            rj = (j - s - 1) * B
                            left = tuple(x[rj:] for x in lh)
                            right = tuple(x[rj:(j2 - s - 1) * B] for x in lh)
                            a_ref[l, j*B:D, j*B:j2*B] -= dot3(left, right, NT)
                vcat = tuple(jnp.concatenate([vs[0][i], vs[1][i]], axis=0) for i in range(2))
                if n:
                    lcat = split(jnp.concatenate([fac_ref[0, o+B:D, o:o+B], fac_ref[1, o+B:D, o:o+B]], axis=1))
                rows = r_ref.shape[0]
                step = 256
                for c in range(0, rows, step):
                    y = dot3(split(r_ref[c:c+step, o:o+B]), vcat, NT)
                    x0 = y[:, :B] * sel_ref[c:c+step, 0:B]
                    x1 = y[:, B:] * sel_ref[c:c+step, B:2*B]
                    out_ref[c:c+step, o:o+B] = x0 + x1
                    if n:
                        xs = split(jnp.concatenate([x0, x1], axis=1))
                        r_ref[c:c+step, o+B:D] -= dot3(xs, lcat, NT)
        return 0
    lax.fori_loop(0, blocks, body, 0)

def chol_whiten(gram, flat, sel, cent):
    D = gram.shape[1]
    return pl.pallas_call(
        functools.partial(chol_kernel, D // B),
        out_shape=(
            jax.ShapeDtypeStruct(gram.shape, jnp.float32),
            jax.ShapeDtypeStruct(flat.shape, jnp.float32),
        ),
        in_specs=[pl.BlockSpec(memory_space=pltpu.VMEM)] * 4,
        out_specs=[pl.BlockSpec(memory_space=pltpu.VMEM)] * 2,
        scratch_shapes=[
            pltpu.VMEM(gram.shape, jnp.float32),
            pltpu.VMEM(flat.shape, jnp.float32),
            pltpu.VMEM((2, B, B), jnp.float32),
        ],
        compiler_params=pltpu.CompilerParams(vmem_limit_bytes=60 * 2**20),
    )(gram, flat, sel, cent)


def on_device(rows, old_list, old_centroids, dest_device, new_local, centroids):
    n_group = lax.axis_size("group")
    n_member = lax.axis_size("member")
    devices = n_group * n_member
    row_dev = rows.shape[0]
    width = rows.shape[1]
    capacity = max(2, 2 * row_dev // devices)
    slots = devices * capacity
    old_hot = (
        old_list[:, None] == jnp.arange(old_centroids.shape[0], dtype=jnp.int32)[None, :]
    ).astype(jnp.float32)
    vectors = rows + jnp.dot(old_hot, old_centroids, precision=lax.Precision.HIGHEST)
    dest = dest_device[:, 0]
    index = jnp.arange(row_dev, dtype=jnp.int32)
    earlier = (dest[:, None] == dest[None, :]) & (index[None, :] < index[:, None])
    ranks = jnp.sum(earlier.astype(jnp.int32), axis=1)
    tag = (new_local + 1).astype(jnp.float32)
    flat, marks = move(vectors, dest[None, :], ranks[None, :], tag[None, :], n_group, n_member, slots)
    flat_tags = marks.reshape(devices, B)[:, :capacity].reshape(-1)
    lists = centroids.shape[0]
    lane = lax.broadcasted_iota(jnp.int32, (slots, lists * B), 1)
    sel = (flat_tags[:, None] == (1 + lane // B).astype(jnp.float32)).astype(jnp.float32)
    gram = gram_sum(flat, sel, centroids)
    factors, result = chol_whiten(gram, flat, sel, centroids)
    return (result, factors)


def solution(mesh):
    return jax.shard_map(
        on_device,
        mesh=mesh,
        in_specs=(
            P(("group", "member"), None),
            P(("group", "member")),
            P(),
            P(("group", "member"), None),
            P(("group", "member")),
            P("group", None),
        ),
        out_specs=(P(("group", "member"), None), P("group", None, None)),
        check_vma=False,
    )
```

```python
import functools

import jax, jax.numpy as jnp
from jax import lax
from jax.experimental import pallas as pl
from jax.experimental.pallas import tpu as pltpu
from jax.sharding import PartitionSpec as P
NT = (((1,), (1,)), ((), ()))
NN = (((1,), (0,)), ((), ()))
B = 128
ridge = 0.1

def split(x):
    hi = x.astype(jnp.bfloat16)
    return hi, (x - hi.astype(jnp.float32)).astype(jnp.bfloat16)

def dot3(a, b, dims):
    f = functools.partial(lax.dot_general, dimension_numbers=dims, preferred_element_type=jnp.float32)
    return f(a[0], b[0]) + (f(a[0], b[1]) + f(a[1], b[0]))

def lane_iota():
    return lax.broadcasted_iota(jnp.int32, (8, B), 1)


def row_iota():
    return lax.broadcasted_iota(jnp.int32, (8, B), 0)


def across(x, k):
    return jnp.broadcast_to(x[:, k : k + 1], (8, B))


def down(x, k):
    return jnp.broadcast_to(x[k : k + 1, :], (8, B))


def factor_steps(load, out):
    n = B // 8
    row, lane = row_iota(), lane_iota()
    z = [load(i) for i in range(n)]
    upper, inverse = [], []
    for m in range(n):
        lo = 8 * m
        last = m == n - 1
        here = (lane >= lo) & (lane < lo + 8)
        p = z[m]
        M = [across(p, lo + k) for k in range(8)]
        q = jnp.where(here, jnp.where(lane == row + lo, 1.0, 0.0), p)
        if not last:
            x = z[m + 1]
            N = [across(x, lo + k) for k in range(8)]
            x = jnp.where(here, 0.0, x)
        yield
        for k in range(8):
            pivots = [down(M[j], k) for j in range(k, 8)]
            s = lax.rsqrt(pivots[0])
            g = [None] * k + [v * s for v in pivots]
            F = jnp.where(row > k, M[k] * s, 0.0)
            for j in range(k + 1, 8):
                M[j] = M[j] - F * g[j]
            p = jnp.where(row == k, p * s, p)
            q = jnp.where(row == k, q * s, q)
            pk, qk = down(p, k), down(q, k)
            p = p - F * pk
            q = q - F * qk
            if not last:
                f = N[k] * s
                for j in range(k + 1, 8):
                    N[j] = N[j] - f * g[j]
                x = x - f * qk
        yield
        if not last:
            z[m + 1] = x
        upper.append(jnp.where(lane >= lo + 8, q, jnp.where(lane >= lo + row, p, 0.0)))
        inverse.append(jnp.where(lane < lo + 8, q, 0.0))
        if m + 2 < n:
            qh, ql = split(q)
            d = lax.dot_general(
                jnp.concatenate([qh, ql, qh], 0),
                jnp.concatenate([qh, qh, ql], 0),
                (((0,), (0,)), ((), ())),
                preferred_element_type=jnp.float32,
            )
            for i in range(m + 2, n):
                z[i] = jnp.where(here, 0.0, z[i]) - d[8 * i : 8 * i + 8, :]
        yield
    out.append((jnp.concatenate(upper, axis=0), jnp.concatenate(inverse, axis=0)))


def factor2(load0, load1):
    outs = [[], []]
    pair = [factor_steps(load0, outs[0]), factor_steps(load1, outs[1])]
    for _ in zip(*pair):
        pass
    for one in pair:
        for _ in one:
            pass
    return outs[0][0], outs[1][0]


PW = 256
CHIPS = 8
MESH = pl.DeviceIdType.MESH


def rows_of(flat_ref, sel_ref, cent_ref, rows, cols, l):
    width = flat_ref[rows, cols].shape[1]
    s = sel_ref[rows, pl.ds(pl.multiple_of(l * B, B), B)]
    s = jnp.concatenate([s] * (width // B), axis=1)
    return (flat_ref[rows, cols] - cent_ref[pl.ds(l, 1), cols]) * s


def main_kernel(chips, flat_ref, sel_ref, cent_ref, fac_ref, out_ref, rt_ref, give_ref, take_ref, acc_ref, part_ref, cov_ref,
                a_ref, r_ref, uv_ref, pair_send, pair_recv, rs_send, rs_recv, ag_send, ag_recv, fw_send, fw_recv):
    D = flat_ref.shape[1]
    slots = flat_ref.shape[0]
    group = lax.axis_index("group")
    me = lax.axis_index("member")
    chip = me // 2
    core = lax.rem(me, 2)
    partner = chip * 2 + (1 - core)
    others = [lax.rem(chip + d, chips) * 2 + core for d in range(1, chips)]

    barrier = pltpu.get_barrier_semaphore()
    for peer in [partner] + others:
        pl.semaphore_signal(barrier, inc=1, device_id=(group, peer), device_id_type=MESH)
    pl.semaphore_wait(barrier, chips)

    panels = D // PW
    first = [sum(D - PW * i for i in range(p)) for p in range(panels)]

    def remote(src, dst, ss, rs, peer):
        return pltpu.make_async_remote_copy(
            src_ref=src, dst_ref=dst, send_sem=ss, recv_sem=rs, device_id=(group, peer), device_id_type=MESH)

    @pl.loop(0, slots // 256)
    def _(i):
        rows = pl.ds(pl.multiple_of(i * 256, 256), 256)
        for c in range(0, D, 256):
            cols = pl.ds(c, 256)
            x = rows_of(flat_ref, sel_ref, cent_ref, rows, cols, 0) + rows_of(flat_ref, sel_ref, cent_ref, rows, cols, 1)
            hi, lo = split(x.T)
            rt_ref[0, pl.ds(c, 256), rows] = hi
            rt_ref[1, pl.ds(c, 256), rows] = lo

    def gram(p, l, dst):
        cols = pl.ds(p * PW, PW)
        mh, ml = split(rows_of(flat_ref, sel_ref, cent_ref, pl.ds(0, slots), cols, l))
        dot = functools.partial(lax.dot_general, dimension_numbers=NN, preferred_element_type=jnp.float32)

        @pl.loop(0, (D - p * PW) // 256)
        def _(i):
            feat = pl.ds(pl.multiple_of(p * PW + i * 256, 256), 256)
            th, tl = rt_ref[0, feat, :], rt_ref[1, feat, :]
            dst[pl.ds(pl.multiple_of(first[p] + i * 256, 256), 256), :] = dot(th, mh) + (dot(th, ml) + dot(tl, mh))
        if p == 0:
            count = jnp.sum(sel_ref[:, pl.ds(pl.multiple_of(l * B, B), B)], axis=0, keepdims=True)
            dst[0:8, B:2 * B] = jnp.broadcast_to(count, (8, B))

    def span(p):
        return pl.ds(first[p], D - p * PW)

    def pair(p):
        return remote(give_ref.at[span(p), :], take_ref.at[span(p), :], pair_send.at[p], pair_recv.at[p], partner)

    def share(p):
        return (D - p * PW) // chips

    def scatter(p, d):
        n = share(p)
        t = lax.rem(chip + d, chips)
        return remote(
            acc_ref.at[pl.ds(pl.multiple_of(first[p] + t * n, 8), n), :],
            part_ref.at[d - 1, pl.ds(first[p] // chips, n), :],
            rs_send.at[p, d - 1], rs_recv.at[p, d - 1], others[d - 1])

    def own(p):
        n = share(p)
        return cov_ref.at[core, pl.ds(pl.multiple_of(p * PW + chip * n, 8), n), pl.ds(p * PW, PW)]

    def gather(p, d):
        return remote(own(p), own(p), ag_send.at[p, d - 1], ag_recv.at[p, d - 1], others[d - 1])

    def forward(p):
        ref = cov_ref.at[core, pl.ds(p * PW, D - p * PW), pl.ds(p * PW, PW)]
        return remote(ref, ref, fw_send.at[p], fw_recv.at[p], partner)

    def compute(p):
        gram(p, 1 - core, give_ref)
        pair(p).start()
        gram(p, core, acc_ref)

    def reduce_pair(p):
        pair(p).wait_recv()
        acc_ref[span(p), :] += take_ref[span(p), :]
        for d in range(1, chips):
            scatter(p, d).start()

    def reduce_chips(p):
        n = share(p)
        for d in range(1, chips):
            scatter(p, d).wait_recv()
        total = acc_ref[pl.ds(pl.multiple_of(first[p] + chip * n, 8), n), :]
        for d in range(1, chips):
            total = total + part_ref[d - 1, pl.ds(first[p] // chips, n), :]
        own(p)[...] = total
        for d in range(1, chips):
            gather(p, d).start()

    def spread(p):
        for d in range(1, chips):
            gather(p, d).wait_recv()
        forward(p).start()

    def arrive(p):
        forward(p).wait_recv()
        o = p * PW
        row, col = (lax.broadcasted_iota(jnp.int32, (PW, PW), i) for i in range(2))
        eye = jnp.where(row == col, ridge, 0.0)
        for l in range(2):
            count = jnp.maximum(cov_ref[l, 0:1, B:2 * B], 1.0)
            scale = jnp.concatenate([1.0 / count] * (PW // B), axis=1)
            top = cov_ref[l, o:o + PW, o:o + PW] * scale + eye
            right = split(fac_ref[l, o:o + PW, 0:o]) if p else None
            a_ref[l, o:o + PW, o:o + PW] = top - dot3(right, right, NT) if p else top
            for i in range(o + PW, D, PW):
                rest = cov_ref[l, i:i + PW, o:o + PW] * scale
                if p:
                    rest = rest - dot3(split(fac_ref[l, i:i + PW, 0:o]), right, NT)
                a_ref[l, i:i + PW, o:o + PW] = rest

    def start_of(kb):
        if kb == 0:
            arrive(0)
        elif kb == 1:
            reduce_chips(1)
            reduce_pair(2)
        elif kb == 2:
            spread(1)
            reduce_chips(2)
            reduce_pair(3)
            arrive(1)
        elif kb == 3:
            reduce_chips(3)
        elif kb == 4:
            spread(2)
            arrive(2)
        elif kb == 5:
            spread(3)
        elif kb == 6:
            arrive(3)

    compute(0)
    reduce_pair(0)
    for p in range(1, panels):
        compute(p)
    for c in range(0, D, 256):
        cols = pl.ds(c, 256)
        every = pl.ds(0, slots)
        r_ref[:, c:c + 256] = rows_of(flat_ref, sel_ref, cent_ref, every, cols, 0) + rows_of(
            flat_ref, sel_ref, cent_ref, every, cols, 1)
    fac_ref[...] = jnp.zeros_like(fac_ref)
    reduce_chips(0)
    reduce_pair(1)
    spread(0)
    blocks = D // B

    def body(kb, _):
        for s in range(blocks - 1):
            @pl.when(kb == s)
            def _():
                start_of(s)
        off = pl.multiple_of(kb * B, B)

        def load(l):
            return lambda i: a_ref[l, pl.ds(pl.multiple_of(off + 8 * i, 8), 8), pl.ds(off, B)]

        for l, (u, v) in enumerate(factor2(load(0), load(1))):
            uv_ref[l] = v
            fac_ref[l, pl.ds(off, B), pl.ds(off, B)] = u.T
        for s in range(blocks):
            @pl.when(kb == s)
            def _():
                o = s * B
                vs = [split(uv_ref[l]) for l in range(2)]
                n = D - o - B
                if n:
                    for l in range(2):
                        lp = dot3(split(a_ref[l, o + B:D, o:o + B]), vs[l], NT)
                        fac_ref[l, o + B:D, o:o + B] = lp
                        if s % 2 == 0:
                            lh = split(lp)
                            a_ref[l, o + B:D, o + B:o + 2 * B] -= dot3(lh, tuple(x[:B] for x in lh), NT)
                vcat = tuple(jnp.concatenate([vs[0][i], vs[1][i]], axis=0) for i in range(2))
                if n:
                    lcat = split(jnp.concatenate([fac_ref[0, o + B:D, o:o + B], fac_ref[1, o + B:D, o:o + B]], axis=1))
                step = 256
                for c in range(0, slots, step):
                    y = dot3(split(r_ref[c:c + step, o:o + B]), vcat, NT)
                    x0 = y[:, :B] * sel_ref[c:c + step, 0:B]
                    x1 = y[:, B:] * sel_ref[c:c + step, B:2 * B]
                    out_ref[c:c + step, o:o + B] = x0 + x1
                    if n:
                        xs = split(jnp.concatenate([x0, x1], axis=1))
                        r_ref[c:c + step, o + B:D] -= dot3(xs, lcat, NT)
        return 0

    lax.fori_loop(0, blocks, body, 0)
    for p in range(panels):
        pair(p).wait_send()
        for d in range(1, chips):
            scatter(p, d).wait_send()
            gather(p, d).wait_send()
        forward(p).wait_send()


def factor_all(flat, sel, cent):
    slots, D = flat.shape
    panels = D // PW
    total = sum(D - PW * i for i in range(panels))
    dma = pltpu.SemaphoreType.DMA
    return pl.pallas_call(
        functools.partial(main_kernel, CHIPS),
        out_shape=(
            jax.ShapeDtypeStruct((2, D, D), jnp.float32),
            jax.ShapeDtypeStruct((slots, D), jnp.float32),
        ),
        in_specs=[pl.BlockSpec(memory_space=pltpu.VMEM)] * 3,
        out_specs=[pl.BlockSpec(memory_space=pltpu.VMEM)] * 2,
        scratch_shapes=[
            pltpu.VMEM((2, D, slots), jnp.bfloat16),
            pltpu.VMEM((total, PW), jnp.float32),
            pltpu.VMEM((total, PW), jnp.float32),
            pltpu.VMEM((total, PW), jnp.float32),
            pltpu.VMEM((CHIPS - 1, total // CHIPS, PW), jnp.float32),
            pltpu.VMEM((2, D, D), jnp.float32),
            pltpu.VMEM((2, D, D), jnp.float32),
            pltpu.VMEM((slots, D), jnp.float32),
            pltpu.VMEM((2, B, B), jnp.float32),
            dma((panels,)), dma((panels,)),
            dma((panels, CHIPS - 1)), dma((panels, CHIPS - 1)),
            dma((panels, CHIPS - 1)), dma((panels, CHIPS - 1)),
            dma((panels,)), dma((panels,)),
        ],
        compiler_params=pltpu.CompilerParams(
            collective_id=0, has_side_effects=True, vmem_limit_bytes=60 * 2**20),
    )(flat, sel, cent)


def full(n, k):
    return jnp.full(jnp.shape(k), n, jnp.int32)


def over(k, n):
    return lax.div(k, full(n, k))


def target(k, group, member):
    x = lax.rem(member // 2 + k, full(4, k))
    y = lax.rem(group + over(k, 4) + k, full(4, k))
    z = lax.rem(member // 8 * 2 + group // 4 + over(k, 16) + k + over(k, 4), full(4, k))
    core = lax.rem(member + over(k, 64), full(2, k))
    return lax.rem(z, full(2, k)) * 4 + y, over(z, 2) * 8 + x * 2 + core


def move_kernel(groups, members, vec_ref, dest_ref, rank_ref, tag_ref, flat_ref, tags_ref, split_ref, data_ref, mark_ref,
                data_send, data_recv, mark_send, mark_recv, own_sem):
    group = lax.axis_index("group")
    member = lax.axis_index("member")
    me = group * members + member
    devices = groups * members
    cap = data_ref.shape[0] // devices
    row_dev, D = vec_ref.shape

    barrier = pltpu.get_barrier_semaphore()

    @pl.loop(1, devices)
    def _(k):
        pl.semaphore_signal(barrier, inc=1, device_id=target(k, group, member), device_id_type=MESH)

    x = vec_ref[...]
    for i in range(3):
        part = x.astype(jnp.bfloat16)
        split_ref[i] = part
        x = x - part.astype(jnp.float32)

    dest = dest_ref[...]
    rank = rank_ref[...]
    device = lax.broadcasted_iota(jnp.int32, (devices, row_dev), 0)
    slot = lax.broadcasted_iota(jnp.int32, (B, row_dev), 0)
    to_device = jnp.where(device == dest, 1.0, 0.0).astype(jnp.bfloat16)
    to_slot = jnp.where(slot == rank, tag_ref[...], 0.0).astype(jnp.bfloat16)
    marks = lax.dot_general(to_device, to_slot, NT, preferred_element_type=jnp.float32)
    mark_ref[...] = marks.reshape(devices, 1, B)

    mine = pl.ds(pl.multiple_of(me * cap, cap), cap)

    def data(k, there):
        return pltpu.make_async_remote_copy(
            src_ref=data_ref.at[pl.ds(pl.multiple_of(k * cap, cap), cap), :], dst_ref=flat_ref.at[mine, :],
            send_sem=data_send, recv_sem=data_recv, device_id=there, device_id_type=MESH)

    def mark(there):
        return pltpu.make_async_remote_copy(
            src_ref=mark_ref.at[pl.ds(there[0] * members + there[1], 1)], dst_ref=tags_ref.at[pl.ds(me, 1)],
            send_sem=mark_send, recv_sem=mark_recv, device_id=there, device_id_type=MESH)

    many = B // cap
    own = (
        pltpu.make_async_copy(data_ref.at[pl.ds(0, cap), :], flat_ref.at[mine, :], own_sem.at[0]),
        pltpu.make_async_copy(mark_ref.at[pl.ds(me, 1)], tags_ref.at[pl.ds(me, 1)], own_sem.at[1]),
    )
    line = lax.broadcasted_iota(jnp.int32, (B, B), 0)

    @pl.loop(0, devices // many)
    def _(i):
        g, m = target(i * many + (line >> 3), group, member)
        ids = (g * members + m) * cap + (line & 7)
        hit = jnp.concatenate([ids] * (row_dev // B), axis=1) == dest * cap + rank
        pick = jnp.where(hit, 1.0, 0.0).astype(jnp.bfloat16)
        at = pl.ds(pl.multiple_of(i * B, B), B)
        for c in range(0, D, 256):
            a, b, d = (
                lax.dot_general(pick, split_ref[k, :, c:c + 256], NN, preferred_element_type=jnp.float32)
                for k in range(3)
            )
            data_ref[at, c:c + 256] = (a + b) + d

        @pl.when(i == 0)
        def _():
            pl.semaphore_wait(barrier, devices - 1)
            for copy in own:
                copy.start()

        @pl.loop(0, many)
        def _(j):
            k = i * many + j

            @pl.when(k > 0)
            def _():
                there = target(k, group, member)
                data(k, there).start()
                mark(there).start()

    for copy in own:
        copy.wait()
    rest = pl.ds(0, (devices - 1) * cap)
    far = lax.rem(group + 1, groups)
    everything = pltpu.make_async_remote_copy(
        src_ref=data_ref.at[rest, :], dst_ref=flat_ref.at[rest, :], send_sem=data_send, recv_sem=data_recv,
        device_id=(far, member), device_id_type=MESH)
    rest = pl.ds(0, devices - 1)
    marked = pltpu.make_async_remote_copy(
        src_ref=mark_ref.at[rest], dst_ref=tags_ref.at[rest], send_sem=mark_send, recv_sem=mark_recv,
        device_id=(far, member), device_id_type=MESH)
    everything.wait_send()
    marked.wait_send()
    marked.wait_recv()
    everything.wait_recv()


def move(vectors, dest, rank, tag, groups, members, slots):
    row_dev, D = vectors.shape
    dma = pltpu.SemaphoreType.DMA
    devices = groups * members
    return pl.pallas_call(
        functools.partial(move_kernel, groups, members),
        out_shape=(
            jax.ShapeDtypeStruct((slots, D), jnp.float32),
            jax.ShapeDtypeStruct((devices, 1, B), jnp.float32),
        ),
        in_specs=[pl.BlockSpec(memory_space=pltpu.VMEM)] * 4,
        out_specs=[pl.BlockSpec(memory_space=pl.ANY)] * 2,
        scratch_shapes=[
            pltpu.VMEM((3, row_dev, D), jnp.bfloat16),
            pltpu.VMEM((slots, D), jnp.float32),
            pltpu.VMEM((devices, 1, B), jnp.float32),
            dma, dma, dma, dma, dma((2,)),
        ],
        compiler_params=pltpu.CompilerParams(collective_id=1, has_side_effects=True, vmem_limit_bytes=60 * 2**20),
    )(vectors, dest, rank, tag)


def on_device(rows, old_list, old_centroids, dest_device, new_local, centroids):
    n_group = lax.axis_size("group")
    n_member = lax.axis_size("member")
    devices = n_group * n_member
    row_dev = rows.shape[0]
    width = rows.shape[1]
    capacity = max(2, 2 * row_dev // devices)
    slots = devices * capacity
    old_hot = (
        old_list[:, None] == jnp.arange(old_centroids.shape[0], dtype=jnp.int32)[None, :]
    ).astype(jnp.float32)
    vectors = rows + jnp.dot(old_hot, old_centroids, precision=lax.Precision.HIGHEST)
    dest = dest_device[:, 0]
    index = jnp.arange(row_dev, dtype=jnp.int32)
    earlier = (dest[:, None] == dest[None, :]) & (index[None, :] < index[:, None])
    ranks = jnp.sum(earlier.astype(jnp.int32), axis=1)
    tag = (new_local + 1).astype(jnp.float32)
    flat, marks = move(vectors, dest[None, :], ranks[None, :], tag[None, :], n_group, n_member, slots)
    flat_tags = marks.reshape(devices, B)[:, :capacity].reshape(-1)
    lists = centroids.shape[0]
    lane = lax.broadcasted_iota(jnp.int32, (slots, lists * B), 1)
    sel = (flat_tags[:, None] == (1 + lane // B).astype(jnp.float32)).astype(jnp.float32)
    factors, result = factor_all(flat, sel, centroids)
    return (result, factors)


def solution(mesh):
    return jax.shard_map(
        on_device,
        mesh=mesh,
        in_specs=(
            P(("group", "member"), None),
            P(("group", "member")),
            P(),
            P(("group", "member"), None),
            P(("group", "member")),
            P("group", None),
        ),
        out_specs=(P(("group", "member"), None), P("group", None, None)),
        check_vma=False,
    )
```

```python
import functools

import jax, jax.numpy as jnp
from jax import lax
from jax.experimental import pallas as pl
from jax.experimental.pallas import tpu as pltpu
from jax.sharding import PartitionSpec as P
NT = (((1,), (1,)), ((), ()))
NN = (((1,), (0,)), ((), ()))
B = 128
ridge = 0.1

def split(x):
    hi = x.astype(jnp.bfloat16)
    return hi, (x - hi.astype(jnp.float32)).astype(jnp.bfloat16)

def dot3(a, b, dims):
    f = functools.partial(lax.dot_general, dimension_numbers=dims, preferred_element_type=jnp.float32)
    return f(a[0], b[0]) + (f(a[0], b[1]) + f(a[1], b[0]))

def lane_iota():
    return lax.broadcasted_iota(jnp.int32, (8, B), 1)


def row_iota():
    return lax.broadcasted_iota(jnp.int32, (8, B), 0)


def across(x, k):
    return jnp.broadcast_to(x[:, k : k + 1], (8, B))


def down(x, k):
    return jnp.broadcast_to(x[k : k + 1, :], (8, B))


def factor_steps(load, out):
    n = B // 8
    row, lane = row_iota(), lane_iota()
    z = [load(i) for i in range(n)]
    upper, inverse = [], []
    for m in range(n):
        lo = 8 * m
        last = m == n - 1
        here = (lane >= lo) & (lane < lo + 8)
        p = z[m]
        M = [across(p, lo + k) for k in range(8)]
        q = jnp.where(here, jnp.where(lane == row + lo, 1.0, 0.0), p)
        if not last:
            x = z[m + 1]
            N = [across(x, lo + k) for k in range(8)]
            x = jnp.where(here, 0.0, x)
        yield
        for k in range(8):
            pivots = [down(M[j], k) for j in range(k, 8)]
            s = lax.rsqrt(pivots[0])
            g = [None] * k + [v * s for v in pivots]
            F = jnp.where(row > k, M[k] * s, 0.0)
            for j in range(k + 1, 8):
                M[j] = M[j] - F * g[j]
            p = jnp.where(row == k, p * s, p)
            q = jnp.where(row == k, q * s, q)
            pk, qk = down(p, k), down(q, k)
            p = p - F * pk
            q = q - F * qk
            if not last:
                f = N[k] * s
                for j in range(k + 1, 8):
                    N[j] = N[j] - f * g[j]
                x = x - f * qk
        yield
        if not last:
            z[m + 1] = x
        upper.append(jnp.where(lane >= lo + 8, q, jnp.where(lane >= lo + row, p, 0.0)))
        inverse.append(jnp.where(lane < lo + 8, q, 0.0))
        if m + 2 < n:
            qh, ql = split(q)
            d = lax.dot_general(
                jnp.concatenate([qh, ql, qh], 0),
                jnp.concatenate([qh, qh, ql], 0),
                (((0,), (0,)), ((), ())),
                preferred_element_type=jnp.float32,
            )
            for i in range(m + 2, n):
                z[i] = jnp.where(here, 0.0, z[i]) - d[8 * i : 8 * i + 8, :]
        yield
    out.append((jnp.concatenate(upper, axis=0), jnp.concatenate(inverse, axis=0)))


def factor2(load0, load1):
    outs = [[], []]
    pair = [factor_steps(load0, outs[0]), factor_steps(load1, outs[1])]
    for _ in zip(*pair):
        pass
    for one in pair:
        for _ in one:
            pass
    return outs[0][0], outs[1][0]


PW = 256
MESH = pl.DeviceIdType.MESH


def rows_of(flat_ref, sel_ref, cent_ref, rows, cols, l):
    width = flat_ref[rows, cols].shape[1]
    s = sel_ref[rows, pl.ds(pl.multiple_of(l * B, B), B)]
    s = jnp.concatenate([s] * (width // B), axis=1)
    return (flat_ref[rows, cols] - cent_ref[pl.ds(l, 1), cols]) * s


def main_kernel(flat_ref, sel_ref, cent_ref, fac_ref, out_ref, rt_ref, give_ref, take_ref, acc_ref, xa_ref, za_ref, xb_ref, zb_ref,
                cov_ref, a_ref, r_ref, uv_ref, pair_sem, xa_sem, za_sem, xb_sem, zb_sem, xc_sem, zc_sem, xd_sem, zd_sem, fw_sem):
    D = flat_ref.shape[1]
    slots = flat_ref.shape[0]
    group = lax.axis_index("group")
    me = lax.axis_index("member")
    core = lax.rem(me, 2)
    zh = me // 8
    x = lax.rem(me // 2, 4)
    partner = me + 1 - 2 * core
    zpeer = lax.rem(me + 8, 16)
    others = [lax.rem(x + d, 4) for d in range(1, 4)]
    xpeers = [zh * 8 + o * 2 + core for o in others]

    barrier = pltpu.get_barrier_semaphore()
    for peer in [partner, zpeer] + xpeers:
        pl.semaphore_signal(barrier, inc=1, device_id=(group, peer), device_id_type=MESH)
    pl.semaphore_wait(barrier, 5)

    panels = D // PW
    first = [sum(D - PW * i for i in range(p)) for p in range(panels)]

    def remote(src, dst, sem, at, peer):
        return pltpu.make_async_remote_copy(
            src_ref=src, dst_ref=dst, send_sem=sem.at[(0, *at)], recv_sem=sem.at[(1, *at)], device_id=(group, peer),
            device_id_type=MESH)

    def go(copies):
        for copy in copies:
            copy.start()

    def landed(copies):
        for copy in copies:
            copy.wait_recv()

    @pl.loop(0, slots // 256)
    def _(i):
        rows = pl.ds(pl.multiple_of(i * 256, 256), 256)
        for c in range(0, D, 256):
            cols = pl.ds(c, 256)
            x = rows_of(flat_ref, sel_ref, cent_ref, rows, cols, 0) + rows_of(flat_ref, sel_ref, cent_ref, rows, cols, 1)
            hi, lo = split(x.T)
            rt_ref[0, pl.ds(c, 256), rows] = hi
            rt_ref[1, pl.ds(c, 256), rows] = lo

    def gram(p, l, dst):
        cols = pl.ds(p * PW, PW)
        mh, ml = split(rows_of(flat_ref, sel_ref, cent_ref, pl.ds(0, slots), cols, l))
        dot = functools.partial(lax.dot_general, dimension_numbers=NN, preferred_element_type=jnp.float32)

        @pl.loop(0, (D - p * PW) // 256)
        def _(i):
            feat = pl.ds(pl.multiple_of(p * PW + i * 256, 256), 256)
            th, tl = rt_ref[0, feat, :], rt_ref[1, feat, :]
            dst[pl.ds(pl.multiple_of(first[p] + i * 256, 256), 256), :] = dot(th, mh) + (dot(th, ml) + dot(tl, mh))
        if p == 0:
            count = jnp.sum(sel_ref[:, pl.ds(pl.multiple_of(l * B, B), B)], axis=0, keepdims=True)
            dst[0:8, B:2 * B] = jnp.broadcast_to(count, (8, B))

    def span(p):
        return pl.ds(first[p], D - p * PW)

    def pair(p):
        return [remote(give_ref.at[span(p), :], take_ref.at[span(p), :], pair_sem, (p,), partner)]

    def at(start, n):
        return pl.ds(start if isinstance(start, int) else pl.multiple_of(start, 8), n)

    def sizes(p):
        return first[p], (D - p * PW) // 2, (D - p * PW) // 16

    def xa(p):
        f, h, e = sizes(p)
        return [remote(acc_ref.at[at(f + others[d] * 2 * e, 2 * e), :], xa_ref.at[d, pl.ds(f // 8, 2 * e), :],
                       xa_sem, (p, d), xpeers[d]) for d in range(3)]

    def za(p):
        f, h, e = sizes(p)
        return [remote(acc_ref.at[at(f + h + (1 - zh) * 4 * e, 4 * e), :], za_ref.at[pl.ds(f // 4, 4 * e), :],
                       za_sem, (p,), zpeer)]

    def zb(p):
        f, h, e = sizes(p)
        return [remote(acc_ref.at[at(f + x * 2 * e + (1 - zh) * e, e), :], zb_ref.at[pl.ds(f // 16, e), :],
                       zb_sem, (p,), zpeer)]

    def xb(p):
        f, h, e = sizes(p)
        return [remote(acc_ref.at[at(f + h + zh * 4 * e + others[d] * e, e), :], xb_ref.at[d, pl.ds(f // 16, e), :],
                       xb_sem, (p, d), xpeers[d]) for d in range(3)]

    def cov(p, start, n):
        return cov_ref.at[core, at(p * PW + start, n), pl.ds(p * PW, PW)]

    def zc(p):
        f, h, e = sizes(p)
        ref = cov(p, x * 2 * e + zh * e, e)
        return [remote(ref, ref, zc_sem, (p,), zpeer)]

    def xc(p):
        f, h, e = sizes(p)
        ref = cov(p, h + zh * 4 * e + x * e, e)
        return [remote(ref, ref, xc_sem, (p, d), xpeers[d]) for d in range(3)]

    def xd(p):
        f, h, e = sizes(p)
        ref = cov(p, x * 2 * e, 2 * e)
        return [remote(ref, ref, xd_sem, (p, d), xpeers[d]) for d in range(3)]

    def zd(p):
        f, h, e = sizes(p)
        ref = cov(p, h + zh * 4 * e, 4 * e)
        return [remote(ref, ref, zd_sem, (p,), zpeer)]

    def forward(p):
        ref = cov_ref.at[core, pl.ds(p * PW, D - p * PW), pl.ds(p * PW, PW)]
        return [remote(ref, ref, fw_sem, (p,), partner)]

    def compute(p):
        gram(p, 1 - core, give_ref)
        go(pair(p))
        gram(p, core, acc_ref)

    def stage1(p):
        landed(pair(p))
        acc_ref[span(p), :] += take_ref[span(p), :]
        go(xa(p))
        go(za(p))

    def stage2(p):
        f, h, e = sizes(p)
        landed(xa(p))
        total = acc_ref[at(f + x * 2 * e, 2 * e), :]
        for d in range(3):
            total = total + xa_ref[d, pl.ds(f // 8, 2 * e), :]
        acc_ref[at(f + x * 2 * e, 2 * e), :] = total
        go(zb(p))
        landed(za(p))
        acc_ref[at(f + h + zh * 4 * e, 4 * e), :] += za_ref[pl.ds(f // 4, 4 * e), :]
        go(xb(p))

    def stage3(p):
        f, h, e = sizes(p)
        landed(zb(p))
        cov(p, x * 2 * e + zh * e, e)[...] = acc_ref[at(f + x * 2 * e + zh * e, e), :] + zb_ref[pl.ds(f // 16, e), :]
        go(zc(p))
        landed(xb(p))
        total = acc_ref[at(f + h + zh * 4 * e + x * e, e), :]
        for d in range(3):
            total = total + xb_ref[d, pl.ds(f // 16, e), :]
        cov(p, h + zh * 4 * e + x * e, e)[...] = total
        go(xc(p))

    def stage4(p):
        landed(zc(p))
        go(xd(p))
        landed(xc(p))
        go(zd(p))

    def stage5(p):
        landed(xd(p))
        landed(zd(p))
        go(forward(p))

    def arrive(p):
        landed(forward(p))
        o = p * PW
        row, col = (lax.broadcasted_iota(jnp.int32, (PW, PW), i) for i in range(2))
        eye = jnp.where(row == col, ridge, 0.0)
        for l in range(2):
            count = jnp.maximum(cov_ref[l, 0:1, B:2 * B], 1.0)
            scale = jnp.concatenate([1.0 / count] * (PW // B), axis=1)
            top = cov_ref[l, o:o + PW, o:o + PW] * scale + eye
            right = split(fac_ref[l, o:o + PW, 0:o]) if p else None
            a_ref[l, o:o + PW, o:o + PW] = top - dot3(right, right, NT) if p else top
            for i in range(o + PW, D, PW):
                rest = cov_ref[l, i:i + PW, o:o + PW] * scale
                if p:
                    rest = rest - dot3(split(fac_ref[l, i:i + PW, 0:o]), right, NT)
                a_ref[l, i:i + PW, o:o + PW] = rest

    def start_of(kb):
        if kb == 0:
            stage3(1)
            stage1(2)
            arrive(0)
        elif kb == 1:
            stage4(1)
            stage2(2)
            stage1(3)
        elif kb == 2:
            stage5(1)
            stage3(2)
            stage2(3)
            arrive(1)
        elif kb == 3:
            stage4(2)
            stage3(3)
        elif kb == 4:
            stage5(2)
            stage4(3)
            arrive(2)
        elif kb == 5:
            stage5(3)
        elif kb == 6:
            arrive(3)

    compute(0)
    stage1(0)
    compute(1)
    stage2(0)
    compute(2)
    stage3(0)
    stage1(1)
    compute(3)
    stage4(0)
    for c in range(0, D, 256):
        cols = pl.ds(c, 256)
        every = pl.ds(0, slots)
        r_ref[:, c:c + 256] = rows_of(flat_ref, sel_ref, cent_ref, every, cols, 0) + rows_of(
            flat_ref, sel_ref, cent_ref, every, cols, 1)
    fac_ref[...] = jnp.zeros_like(fac_ref)
    stage2(1)
    stage5(0)
    blocks = D // B

    def body(kb, _):
        for s in range(blocks - 1):
            @pl.when(kb == s)
            def _():
                start_of(s)
        off = pl.multiple_of(kb * B, B)

        def load(l):
            return lambda i: a_ref[l, pl.ds(pl.multiple_of(off + 8 * i, 8), 8), pl.ds(off, B)]

        for l, (u, v) in enumerate(factor2(load(0), load(1))):
            uv_ref[l] = v
            fac_ref[l, pl.ds(off, B), pl.ds(off, B)] = u.T
        for s in range(blocks):
            @pl.when(kb == s)
            def _():
                o = s * B
                vs = [split(uv_ref[l]) for l in range(2)]
                n = D - o - B
                if n:
                    for l in range(2):
                        lp = dot3(split(a_ref[l, o + B:D, o:o + B]), vs[l], NT)
                        fac_ref[l, o + B:D, o:o + B] = lp
                        if s % 2 == 0:
                            lh = split(lp)
                            a_ref[l, o + B:D, o + B:o + 2 * B] -= dot3(lh, tuple(x[:B] for x in lh), NT)
                vcat = tuple(jnp.concatenate([vs[0][i], vs[1][i]], axis=0) for i in range(2))
                if n:
                    lcat = split(jnp.concatenate([fac_ref[0, o + B:D, o:o + B], fac_ref[1, o + B:D, o:o + B]], axis=1))
                step = 256
                for c in range(0, slots, step):
                    y = dot3(split(r_ref[c:c + step, o:o + B]), vcat, NT)
                    x0 = y[:, :B] * sel_ref[c:c + step, 0:B]
                    x1 = y[:, B:] * sel_ref[c:c + step, B:2 * B]
                    out_ref[c:c + step, o:o + B] = x0 + x1
                    if n:
                        xs = split(jnp.concatenate([x0, x1], axis=1))
                        r_ref[c:c + step, o + B:D] -= dot3(xs, lcat, NT)
        return 0

    lax.fori_loop(0, blocks, body, 0)
    for p in range(panels):
        for make in (pair, xa, za, xb, zb, xc, zc, xd, zd, forward):
            for copy in make(p):
                copy.wait_send()


def factor_all(flat, sel, cent):
    slots, D = flat.shape
    panels = D // PW
    total = sum(D - PW * i for i in range(panels))
    dma = pltpu.SemaphoreType.DMA
    return pl.pallas_call(
        main_kernel,
        out_shape=(
            jax.ShapeDtypeStruct((2, D, D), jnp.float32),
            jax.ShapeDtypeStruct((slots, D), jnp.float32),
        ),
        in_specs=[pl.BlockSpec(memory_space=pltpu.VMEM)] * 3,
        out_specs=[pl.BlockSpec(memory_space=pltpu.VMEM)] * 2,
        scratch_shapes=[
            pltpu.VMEM((2, D, slots), jnp.bfloat16),
            pltpu.VMEM((total, PW), jnp.float32),
            pltpu.VMEM((total, PW), jnp.float32),
            pltpu.VMEM((total, PW), jnp.float32),
            pltpu.VMEM((3, total // 8, PW), jnp.float32),
            pltpu.VMEM((total // 4, PW), jnp.float32),
            pltpu.VMEM((3, total // 16, PW), jnp.float32),
            pltpu.VMEM((total // 16, PW), jnp.float32),
            pltpu.VMEM((2, D, D), jnp.float32),
            pltpu.VMEM((2, D, D), jnp.float32),
            pltpu.VMEM((slots, D), jnp.float32),
            pltpu.VMEM((2, B, B), jnp.float32),
            dma((2, panels)),
            dma((2, panels, 3)), dma((2, panels)), dma((2, panels, 3)), dma((2, panels)),
            dma((2, panels, 3)), dma((2, panels)), dma((2, panels, 3)), dma((2, panels)),
            dma((2, panels)),
        ],
        compiler_params=pltpu.CompilerParams(
            collective_id=0, has_side_effects=True, vmem_limit_bytes=60 * 2**20),
    )(flat, sel, cent)


def full(n, k):
    return jnp.full(jnp.shape(k), n, jnp.int32)


def over(k, n):
    return lax.div(k, full(n, k))


def target(k, group, member):
    x = lax.rem(member // 2 + k, full(4, k))
    y = lax.rem(group + over(k, 4) + k, full(4, k))
    z = lax.rem(member // 8 * 2 + group // 4 + over(k, 16) + k + over(k, 4), full(4, k))
    core = lax.rem(member + over(k, 64), full(2, k))
    return lax.rem(z, full(2, k)) * 4 + y, over(z, 2) * 8 + x * 2 + core


def move_kernel(groups, members, vec_ref, dest_ref, rank_ref, tag_ref, flat_ref, tags_ref, split_ref, data_ref, mark_ref,
                data_send, data_recv, mark_send, mark_recv, own_sem):
    group = lax.axis_index("group")
    member = lax.axis_index("member")
    me = group * members + member
    devices = groups * members
    cap = data_ref.shape[0] // devices
    row_dev, D = vec_ref.shape

    barrier = pltpu.get_barrier_semaphore()

    @pl.loop(1, devices)
    def _(k):
        pl.semaphore_signal(barrier, inc=1, device_id=target(k, group, member), device_id_type=MESH)

    x = vec_ref[...]
    for i in range(3):
        part = x.astype(jnp.bfloat16)
        split_ref[i] = part
        x = x - part.astype(jnp.float32)

    dest = dest_ref[...]
    rank = rank_ref[...]
    device = lax.broadcasted_iota(jnp.int32, (devices, row_dev), 0)
    slot = lax.broadcasted_iota(jnp.int32, (B, row_dev), 0)
    to_device = jnp.where(device == dest, 1.0, 0.0).astype(jnp.bfloat16)
    to_slot = jnp.where(slot == rank, tag_ref[...], 0.0).astype(jnp.bfloat16)
    marks = lax.dot_general(to_device, to_slot, NT, preferred_element_type=jnp.float32)
    mark_ref[...] = marks.reshape(devices, 1, B)

    mine = pl.ds(pl.multiple_of(me * cap, cap), cap)

    def data(k, there):
        return pltpu.make_async_remote_copy(
            src_ref=data_ref.at[pl.ds(pl.multiple_of(k * cap, cap), cap), :], dst_ref=flat_ref.at[mine, :],
            send_sem=data_send, recv_sem=data_recv, device_id=there, device_id_type=MESH)

    def mark(there):
        return pltpu.make_async_remote_copy(
            src_ref=mark_ref.at[pl.ds(there[0] * members + there[1], 1)], dst_ref=tags_ref.at[pl.ds(me, 1)],
            send_sem=mark_send, recv_sem=mark_recv, device_id=there, device_id_type=MESH)

    many = B // cap
    own = (
        pltpu.make_async_copy(data_ref.at[pl.ds(0, cap), :], flat_ref.at[mine, :], own_sem.at[0]),
        pltpu.make_async_copy(mark_ref.at[pl.ds(me, 1)], tags_ref.at[pl.ds(me, 1)], own_sem.at[1]),
    )
    line = lax.broadcasted_iota(jnp.int32, (B, B), 0)

    @pl.loop(0, devices // many)
    def _(i):
        g, m = target(i * many + (line >> 3), group, member)
        ids = (g * members + m) * cap + (line & 7)
        hit = jnp.concatenate([ids] * (row_dev // B), axis=1) == dest * cap + rank
        pick = jnp.where(hit, 1.0, 0.0).astype(jnp.bfloat16)
        at = pl.ds(pl.multiple_of(i * B, B), B)
        for c in range(0, D, 256):
            a, b, d = (
                lax.dot_general(pick, split_ref[k, :, c:c + 256], NN, preferred_element_type=jnp.float32)
                for k in range(3)
            )
            data_ref[at, c:c + 256] = (a + b) + d

        @pl.when(i == 0)
        def _():
            pl.semaphore_wait(barrier, devices - 1)
            for copy in own:
                copy.start()

        @pl.loop(0, many)
        def _(j):
            k = i * many + j

            @pl.when(k > 0)
            def _():
                there = target(k, group, member)
                data(k, there).start()
                mark(there).start()

    for copy in own:
        copy.wait()
    rest = pl.ds(0, (devices - 1) * cap)
    far = lax.rem(group + 1, groups)
    everything = pltpu.make_async_remote_copy(
        src_ref=data_ref.at[rest, :], dst_ref=flat_ref.at[rest, :], send_sem=data_send, recv_sem=data_recv,
        device_id=(far, member), device_id_type=MESH)
    rest = pl.ds(0, devices - 1)
    marked = pltpu.make_async_remote_copy(
        src_ref=mark_ref.at[rest], dst_ref=tags_ref.at[rest], send_sem=mark_send, recv_sem=mark_recv,
        device_id=(far, member), device_id_type=MESH)
    everything.wait_send()
    marked.wait_send()
    marked.wait_recv()
    everything.wait_recv()


def move(vectors, dest, rank, tag, groups, members, slots):
    row_dev, D = vectors.shape
    dma = pltpu.SemaphoreType.DMA
    devices = groups * members
    return pl.pallas_call(
        functools.partial(move_kernel, groups, members),
        out_shape=(
            jax.ShapeDtypeStruct((slots, D), jnp.float32),
            jax.ShapeDtypeStruct((devices, 1, B), jnp.float32),
        ),
        in_specs=[pl.BlockSpec(memory_space=pltpu.VMEM)] * 4,
        out_specs=[pl.BlockSpec(memory_space=pl.ANY)] * 2,
        scratch_shapes=[
            pltpu.VMEM((3, row_dev, D), jnp.bfloat16),
            pltpu.VMEM((slots, D), jnp.float32),
            pltpu.VMEM((devices, 1, B), jnp.float32),
            dma, dma, dma, dma, dma((2,)),
        ],
        compiler_params=pltpu.CompilerParams(collective_id=1, has_side_effects=True, vmem_limit_bytes=60 * 2**20),
    )(vectors, dest, rank, tag)


def on_device(rows, old_list, old_centroids, dest_device, new_local, centroids):
    n_group = lax.axis_size("group")
    n_member = lax.axis_size("member")
    devices = n_group * n_member
    row_dev = rows.shape[0]
    width = rows.shape[1]
    capacity = max(2, 2 * row_dev // devices)
    slots = devices * capacity
    old_hot = (
        old_list[:, None] == jnp.arange(old_centroids.shape[0], dtype=jnp.int32)[None, :]
    ).astype(jnp.float32)
    vectors = rows + jnp.dot(old_hot, old_centroids, precision=lax.Precision.HIGHEST)
    dest = dest_device[:, 0]
    index = jnp.arange(row_dev, dtype=jnp.int32)
    earlier = (dest[:, None] == dest[None, :]) & (index[None, :] < index[:, None])
    ranks = jnp.sum(earlier.astype(jnp.int32), axis=1)
    tag = (new_local + 1).astype(jnp.float32)
    flat, marks = move(vectors, dest[None, :], ranks[None, :], tag[None, :], n_group, n_member, slots)
    flat_tags = marks.reshape(devices, B)[:, :capacity].reshape(-1)
    lists = centroids.shape[0]
    lane = lax.broadcasted_iota(jnp.int32, (slots, lists * B), 1)
    sel = (flat_tags[:, None] == (1 + lane // B).astype(jnp.float32)).astype(jnp.float32)
    factors, result = factor_all(flat, sel, centroids)
    return (result, factors)


def solution(mesh):
    return jax.shard_map(
        on_device,
        mesh=mesh,
        in_specs=(
            P(("group", "member"), None),
            P(("group", "member")),
            P(),
            P(("group", "member"), None),
            P(("group", "member")),
            P("group", None),
        ),
        out_specs=(P(("group", "member"), None), P("group", None, None)),
        check_vma=False,
    )
```

```python
import functools

import jax, jax.numpy as jnp
from jax import lax
from jax.experimental import pallas as pl
from jax.experimental.pallas import tpu as pltpu
from jax.sharding import PartitionSpec as P
NT = (((1,), (1,)), ((), ()))
NN = (((1,), (0,)), ((), ()))
B = 128
ridge = 0.1

def split(x):
    hi = x.astype(jnp.bfloat16)
    return hi, (x - hi.astype(jnp.float32)).astype(jnp.bfloat16)

def dot3(a, b, dims):
    f = functools.partial(lax.dot_general, dimension_numbers=dims, preferred_element_type=jnp.float32)
    return f(a[0], b[0]) + (f(a[0], b[1]) + f(a[1], b[0]))

def lane_iota():
    return lax.broadcasted_iota(jnp.int32, (8, B), 1)


def row_iota():
    return lax.broadcasted_iota(jnp.int32, (8, B), 0)


def across(x, k):
    return jnp.broadcast_to(x[:, k : k + 1], (8, B))


def down(x, k):
    return jnp.broadcast_to(x[k : k + 1, :], (8, B))


def factor_steps(load, out):
    n = B // 8
    row, lane = row_iota(), lane_iota()
    z = [load(i) for i in range(n)]
    upper, inverse = [], []
    for m in range(n):
        lo = 8 * m
        last = m == n - 1
        here = (lane >= lo) & (lane < lo + 8)
        p = z[m]
        M = [across(p, lo + k) for k in range(8)]
        q = jnp.where(here, jnp.where(lane == row + lo, 1.0, 0.0), p)
        if not last:
            x = z[m + 1]
            N = [across(x, lo + k) for k in range(8)]
            x = jnp.where(here, 0.0, x)
        yield
        for k in range(8):
            pivots = [down(M[j], k) for j in range(k, 8)]
            s = lax.rsqrt(pivots[0])
            g = [None] * k + [v * s for v in pivots]
            F = jnp.where(row > k, M[k] * s, 0.0)
            for j in range(k + 1, 8):
                M[j] = M[j] - F * g[j]
            p = jnp.where(row == k, p * s, p)
            q = jnp.where(row == k, q * s, q)
            pk, qk = down(p, k), down(q, k)
            p = p - F * pk
            q = q - F * qk
            if not last:
                f = N[k] * s
                for j in range(k + 1, 8):
                    N[j] = N[j] - f * g[j]
                x = x - f * qk
        yield
        if not last:
            z[m + 1] = x
        upper.append(jnp.where(lane >= lo + 8, q, jnp.where(lane >= lo + row, p, 0.0)))
        inverse.append(jnp.where(lane < lo + 8, q, 0.0))
        if m + 2 < n:
            qh, ql = split(q)
            d = lax.dot_general(
                jnp.concatenate([qh, ql, qh], 0),
                jnp.concatenate([qh, qh, ql], 0),
                (((0,), (0,)), ((), ())),
                preferred_element_type=jnp.float32,
            )
            for i in range(m + 2, n):
                z[i] = jnp.where(here, 0.0, z[i]) - d[8 * i : 8 * i + 8, :]
        yield
    out.append((jnp.concatenate(upper, axis=0), jnp.concatenate(inverse, axis=0)))


def factor2(load0, load1):
    outs = [[], []]
    pair = [factor_steps(load0, outs[0]), factor_steps(load1, outs[1])]
    for _ in zip(*pair):
        pass
    for one in pair:
        for _ in one:
            pass
    return outs[0][0], outs[1][0]


PW = 256
MESH = pl.DeviceIdType.MESH


def rows_of(flat_ref, sel_ref, cent_ref, rows, cols, l):
    width = flat_ref[rows, cols].shape[1]
    s = sel_ref[rows, pl.ds(pl.multiple_of(l * B, B), B)]
    s = jnp.concatenate([s] * (width // B), axis=1)
    return (flat_ref[rows, cols] - cent_ref[pl.ds(l, 1), cols]) * s


def main_kernel(flat_ref, sel_ref, cent_ref, fac_ref, out_ref, rt_ref, give_ref, take_ref, acc_ref, xa_ref, za_ref, xb_ref, zb_ref,
                cov_ref, a_ref, r_ref, uv_ref, pair_sem, xa_sem, za_sem, xb_sem, zb_sem, xc_sem, zc_sem, xd_sem, zd_sem, fw_sem):
    D = flat_ref.shape[1]
    slots = flat_ref.shape[0]
    group = lax.axis_index("group")
    me = lax.axis_index("member")
    core = lax.rem(me, 2)
    zh = me // 8
    x = lax.rem(me // 2, 4)
    partner = me + 1 - 2 * core
    zpeer = lax.rem(me + 8, 16)
    others = [lax.rem(x + d, 4) for d in range(1, 4)]
    xpeers = [zh * 8 + o * 2 + core for o in others]

    barrier = pltpu.get_barrier_semaphore()
    for peer in [partner, zpeer] + xpeers:
        pl.semaphore_signal(barrier, inc=1, device_id=(group, peer), device_id_type=MESH)
    pl.semaphore_wait(barrier, 5)

    panels = D // PW
    first = [sum(D - PW * i for i in range(p)) for p in range(panels)]

    def remote(src, dst, sem, at, peer):
        return pltpu.make_async_remote_copy(
            src_ref=src, dst_ref=dst, send_sem=sem.at[(0, *at)], recv_sem=sem.at[(1, *at)], device_id=(group, peer),
            device_id_type=MESH)

    def go(copies):
        for copy in copies:
            copy.start()

    def landed(copies):
        for copy in copies:
            copy.wait_recv()

    @pl.loop(0, slots // 256)
    def _(i):
        rows = pl.ds(pl.multiple_of(i * 256, 256), 256)
        for c in range(0, D, 256):
            cols = pl.ds(c, 256)
            x = rows_of(flat_ref, sel_ref, cent_ref, rows, cols, 0) + rows_of(flat_ref, sel_ref, cent_ref, rows, cols, 1)
            hi, lo = split(x.T)
            rt_ref[0, pl.ds(c, 256), rows] = hi
            rt_ref[1, pl.ds(c, 256), rows] = lo

    def gram(p, l, dst):
        cols = pl.ds(p * PW, PW)
        mh, ml = split(rows_of(flat_ref, sel_ref, cent_ref, pl.ds(0, slots), cols, l))
        dot = functools.partial(lax.dot_general, dimension_numbers=NN, preferred_element_type=jnp.float32)

        @pl.loop(0, (D - p * PW) // 256)
        def _(i):
            feat = pl.ds(pl.multiple_of(p * PW + i * 256, 256), 256)
            th, tl = rt_ref[0, feat, :], rt_ref[1, feat, :]
            dst[pl.ds(pl.multiple_of(first[p] + i * 256, 256), 256), :] = dot(th, mh) + (dot(th, ml) + dot(tl, mh))
        if p == 0:
            count = jnp.sum(sel_ref[:, pl.ds(pl.multiple_of(l * B, B), B)], axis=0, keepdims=True)
            dst[0:8, B:2 * B] = jnp.broadcast_to(count, (8, B))

    def span(p):
        return pl.ds(first[p], D - p * PW)

    def pair(p):
        return [remote(give_ref.at[span(p), :], take_ref.at[span(p), :], pair_sem, (p,), partner)]

    def at(start, n):
        return pl.ds(start if isinstance(start, int) else pl.multiple_of(start, 8), n)

    def sizes(p):
        return first[p], (D - p * PW) // 2, (D - p * PW) // 16

    def xa(p):
        f, h, e = sizes(p)
        return [remote(acc_ref.at[at(f + others[d] * 2 * e, 2 * e), :], xa_ref.at[d, pl.ds(f // 8, 2 * e), :],
                       xa_sem, (p, d), xpeers[d]) for d in range(3)]

    def za(p):
        f, h, e = sizes(p)
        return [remote(acc_ref.at[at(f + h + (1 - zh) * 4 * e, 4 * e), :], za_ref.at[pl.ds(f // 4, 4 * e), :],
                       za_sem, (p,), zpeer)]

    def zb(p):
        f, h, e = sizes(p)
        return [remote(acc_ref.at[at(f + x * 2 * e + (1 - zh) * e, e), :], zb_ref.at[pl.ds(f // 16, e), :],
                       zb_sem, (p,), zpeer)]

    def xb(p):
        f, h, e = sizes(p)
        return [remote(acc_ref.at[at(f + h + zh * 4 * e + others[d] * e, e), :], xb_ref.at[d, pl.ds(f // 16, e), :],
                       xb_sem, (p, d), xpeers[d]) for d in range(3)]

    def cov(p, start, n):
        return cov_ref.at[core, at(p * PW + start, n), pl.ds(p * PW, PW)]

    def zc(p):
        f, h, e = sizes(p)
        ref = cov(p, x * 2 * e + zh * e, e)
        return [remote(ref, ref, zc_sem, (p,), zpeer)]

    def xc(p):
        f, h, e = sizes(p)
        ref = cov(p, h + zh * 4 * e + x * e, e)
        return [remote(ref, ref, xc_sem, (p, d), xpeers[d]) for d in range(3)]

    def xd(p):
        f, h, e = sizes(p)
        ref = cov(p, x * 2 * e, 2 * e)
        return [remote(ref, ref, xd_sem, (p, d), xpeers[d]) for d in range(3)]

    def zd(p):
        f, h, e = sizes(p)
        ref = cov(p, h + zh * 4 * e, 4 * e)
        return [remote(ref, ref, zd_sem, (p,), zpeer)]

    def forward(p):
        ref = cov_ref.at[core, pl.ds(p * PW, D - p * PW), pl.ds(p * PW, PW)]
        return [remote(ref, ref, fw_sem, (p,), partner)]

    def compute(p):
        gram(p, 1 - core, give_ref)
        go(pair(p))
        gram(p, core, acc_ref)

    def stage1(p):
        landed(pair(p))
        acc_ref[span(p), :] += take_ref[span(p), :]
        go(xa(p))
        go(za(p))

    def stage2(p):
        f, h, e = sizes(p)
        landed(xa(p))
        total = acc_ref[at(f + x * 2 * e, 2 * e), :]
        for d in range(3):
            total = total + xa_ref[d, pl.ds(f // 8, 2 * e), :]
        acc_ref[at(f + x * 2 * e, 2 * e), :] = total
        go(zb(p))
        landed(za(p))
        acc_ref[at(f + h + zh * 4 * e, 4 * e), :] += za_ref[pl.ds(f // 4, 4 * e), :]
        go(xb(p))

    def stage3(p):
        f, h, e = sizes(p)
        landed(zb(p))
        cov(p, x * 2 * e + zh * e, e)[...] = acc_ref[at(f + x * 2 * e + zh * e, e), :] + zb_ref[pl.ds(f // 16, e), :]
        go(zc(p))
        landed(xb(p))
        total = acc_ref[at(f + h + zh * 4 * e + x * e, e), :]
        for d in range(3):
            total = total + xb_ref[d, pl.ds(f // 16, e), :]
        cov(p, h + zh * 4 * e + x * e, e)[...] = total
        go(xc(p))

    def stage4(p):
        landed(zc(p))
        go(xd(p))
        landed(xc(p))
        go(zd(p))

    def stage5(p):
        landed(xd(p))
        landed(zd(p))
        go(forward(p))

    def arrive(p):
        landed(forward(p))
        o = p * PW
        row, col = (lax.broadcasted_iota(jnp.int32, (PW, PW), i) for i in range(2))
        eye = jnp.where(row == col, ridge, 0.0)
        for l in range(2):
            count = jnp.maximum(cov_ref[l, 0:1, B:2 * B], 1.0)
            scale = jnp.concatenate([1.0 / count] * (PW // B), axis=1)
            top = cov_ref[l, o:o + PW, o:o + PW] * scale + eye
            right = split(fac_ref[l, o:o + PW, 0:o]) if p else None
            a_ref[l, o:o + PW, o:o + PW] = top - dot3(right, right, NT) if p else top
            for i in range(o + PW, D, PW):
                rest = cov_ref[l, i:i + PW, o:o + PW] * scale
                if p:
                    rest = rest - dot3(split(fac_ref[l, i:i + PW, 0:o]), right, NT)
                a_ref[l, i:i + PW, o:o + PW] = rest

    def start_of(kb):
        if kb == 0:
            stage3(1)
            stage1(2)
            arrive(0)
        elif kb == 1:
            stage4(1)
            stage2(2)
            stage1(3)
        elif kb == 2:
            stage5(1)
            stage3(2)
            stage2(3)
            arrive(1)
        elif kb == 3:
            stage4(2)
            stage3(3)
        elif kb == 4:
            stage5(2)
            stage4(3)
            arrive(2)
        elif kb == 5:
            stage5(3)
        elif kb == 6:
            arrive(3)

    compute(0)
    stage1(0)
    compute(1)
    stage2(0)
    compute(2)
    stage3(0)
    stage1(1)
    compute(3)
    stage4(0)
    for c in range(0, D, 256):
        cols = pl.ds(c, 256)
        every = pl.ds(0, slots)
        r_ref[:, c:c + 256] = rows_of(flat_ref, sel_ref, cent_ref, every, cols, 0) + rows_of(
            flat_ref, sel_ref, cent_ref, every, cols, 1)
    fac_ref[...] = jnp.zeros_like(fac_ref)
    stage2(1)
    stage5(0)
    blocks = D // B

    def body(kb, _):
        for s in range(blocks - 1):
            @pl.when(kb == s)
            def _():
                start_of(s)
        off = pl.multiple_of(kb * B, B)

        def load(l):
            return lambda i: a_ref[l, pl.ds(pl.multiple_of(off + 8 * i, 8), 8), pl.ds(off, B)]

        for l, (u, v) in enumerate(factor2(load(0), load(1))):
            uv_ref[l] = v
            fac_ref[l, pl.ds(off, B), pl.ds(off, B)] = u.T
        for s in range(blocks):
            @pl.when(kb == s)
            def _():
                o = s * B
                vs = [split(uv_ref[l]) for l in range(2)]
                n = D - o - B
                if n:
                    for l in range(2):
                        lp = dot3(split(a_ref[l, o + B:D, o:o + B]), vs[l], NT)
                        fac_ref[l, o + B:D, o:o + B] = lp
                        if s % 2 == 0:
                            lh = split(lp)
                            a_ref[l, o + B:D, o + B:o + 2 * B] -= dot3(lh, tuple(x[:B] for x in lh), NT)
                vcat = tuple(jnp.concatenate([vs[0][i], vs[1][i]], axis=0) for i in range(2))
                if n:
                    lcat = split(jnp.concatenate([fac_ref[0, o + B:D, o:o + B], fac_ref[1, o + B:D, o:o + B]], axis=1))
                step = 256
                for c in range(0, slots, step):
                    y = dot3(split(r_ref[c:c + step, o:o + B]), vcat, NT)
                    x0 = y[:, :B] * sel_ref[c:c + step, 0:B]
                    x1 = y[:, B:] * sel_ref[c:c + step, B:2 * B]
                    out_ref[c:c + step, o:o + B] = x0 + x1
                    if n:
                        xs = split(jnp.concatenate([x0, x1], axis=1))
                        r_ref[c:c + step, o + B:D] -= dot3(xs, lcat, NT)
        return 0

    lax.fori_loop(0, blocks, body, 0)
    for p in range(panels):
        for make in (pair, xa, za, xb, zb, xc, zc, xd, zd, forward):
            for copy in make(p):
                copy.wait_send()


def factor_all(flat, sel, cent):
    slots, D = flat.shape
    panels = D // PW
    total = sum(D - PW * i for i in range(panels))
    dma = pltpu.SemaphoreType.DMA
    return pl.pallas_call(
        main_kernel,
        out_shape=(pltpu.VMEM((2, D, D), jnp.float32), pltpu.VMEM((slots, D), jnp.float32)),
        in_specs=[pl.BlockSpec(memory_space=pltpu.VMEM)] * 3,
        out_specs=[pl.BlockSpec(memory_space=pltpu.VMEM)] * 2,
        scratch_shapes=[
            pltpu.VMEM((2, D, slots), jnp.bfloat16),
            pltpu.VMEM((total, PW), jnp.float32),
            pltpu.VMEM((total, PW), jnp.float32),
            pltpu.VMEM((total, PW), jnp.float32),
            pltpu.VMEM((3, total // 8, PW), jnp.float32),
            pltpu.VMEM((total // 4, PW), jnp.float32),
            pltpu.VMEM((3, total // 16, PW), jnp.float32),
            pltpu.VMEM((total // 16, PW), jnp.float32),
            pltpu.VMEM((2, D, D), jnp.float32),
            pltpu.VMEM((2, D, D), jnp.float32),
            pltpu.VMEM((slots, D), jnp.float32),
            pltpu.VMEM((2, B, B), jnp.float32),
            dma((2, panels)),
            dma((2, panels, 3)), dma((2, panels)), dma((2, panels, 3)), dma((2, panels)),
            dma((2, panels, 3)), dma((2, panels)), dma((2, panels, 3)), dma((2, panels)),
            dma((2, panels)),
        ],
        compiler_params=pltpu.CompilerParams(
            collective_id=0, has_side_effects=True, vmem_limit_bytes=50 * 2**20),
    )(flat, sel, cent)


def full(n, k):
    return jnp.full(jnp.shape(k), n, jnp.int32)


def over(k, n):
    return lax.div(k, full(n, k))


def target(k, group, member):
    x = lax.rem(member // 2 + k, full(4, k))
    y = lax.rem(group + over(k, 4) + k, full(4, k))
    z = lax.rem(member // 8 * 2 + group // 4 + over(k, 16) + k + over(k, 4), full(4, k))
    core = lax.rem(member + over(k, 64), full(2, k))
    return lax.rem(z, full(2, k)) * 4 + y, over(z, 2) * 8 + x * 2 + core


def move_kernel(groups, members, rows_ref, hold_ref, old_ref, dest_ref, local_ref, flat_ref, tags_ref, split_ref, data_ref, mark_ref,
                data_send, data_recv, mark_send, mark_recv, own_sem):
    group = lax.axis_index("group")
    member = lax.axis_index("member")
    me = group * members + member
    devices = groups * members
    cap = data_ref.shape[0] // devices
    row_dev, D = rows_ref.shape

    barrier = pltpu.get_barrier_semaphore()

    @pl.loop(1, devices)
    def _(k):
        pl.semaphore_signal(barrier, inc=1, device_id=target(k, group, member), device_id_type=MESH)

    def parts(x):
        out = []
        for _ in range(3):
            out.append(x.astype(jnp.bfloat16))
            x = x - out[-1].astype(jnp.float32)
        return out

    def ones(hit):
        return jnp.where(hit, 1.0, 0.0).astype(jnp.bfloat16)

    dot = functools.partial(lax.dot_general, preferred_element_type=jnp.float32)
    olds = old_ref.shape[0]
    held = ones(lax.broadcasted_iota(jnp.int32, (olds, row_dev), 0) == hold_ref[...])
    for c in range(0, D, 256):
        a, b, d = (dot(held, part, (((0,), (0,)), ((), ()))) for part in parts(old_ref[:, c:c + 256]))
        for i, part in enumerate(parts(rows_ref[:, c:c + 256] + ((a + b) + d))):
            split_ref[i, :, c:c + 256] = part

    dest = dest_ref[...]
    to_device = ones(lax.broadcasted_iota(jnp.int32, (devices, row_dev), 0) == dest)
    row, col = (lax.broadcasted_iota(jnp.int32, (row_dev, row_dev), i) for i in range(2))
    before = dot(to_device, ones(row < col), NN)
    rank = jnp.sum(before * to_device.astype(jnp.float32), axis=0, keepdims=True).astype(jnp.int32)
    slot = lax.broadcasted_iota(jnp.int32, (B, row_dev), 0)
    tag = (local_ref[...] + 1).astype(jnp.float32)
    to_slot = jnp.where(slot == rank, tag, 0.0).astype(jnp.bfloat16)
    mark_ref[...] = dot(to_device, to_slot, NT).reshape(devices, 1, B)

    mine = pl.ds(pl.multiple_of(me * cap, cap), cap)

    def data(k, there):
        return pltpu.make_async_remote_copy(
            src_ref=data_ref.at[pl.ds(pl.multiple_of(k * cap, cap), cap), :], dst_ref=flat_ref.at[mine, :],
            send_sem=data_send, recv_sem=data_recv, device_id=there, device_id_type=MESH)

    def mark(there):
        return pltpu.make_async_remote_copy(
            src_ref=mark_ref.at[pl.ds(there[0] * members + there[1], 1)], dst_ref=tags_ref.at[pl.ds(me, 1)],
            send_sem=mark_send, recv_sem=mark_recv, device_id=there, device_id_type=MESH)

    many = B // cap
    own = (
        pltpu.make_async_copy(data_ref.at[pl.ds(0, cap), :], flat_ref.at[mine, :], own_sem.at[0]),
        pltpu.make_async_copy(mark_ref.at[pl.ds(me, 1)], tags_ref.at[pl.ds(me, 1)], own_sem.at[1]),
    )
    line = lax.broadcasted_iota(jnp.int32, (B, B), 0)

    @pl.loop(0, devices // many)
    def _(i):
        g, m = target(i * many + (line >> 3), group, member)
        ids = (g * members + m) * cap + (line & 7)
        hit = jnp.concatenate([ids] * (row_dev // B), axis=1) == dest * cap + rank
        pick = jnp.where(hit, 1.0, 0.0).astype(jnp.bfloat16)
        at = pl.ds(pl.multiple_of(i * B, B), B)
        for c in range(0, D, 256):
            a, b, d = (
                lax.dot_general(pick, split_ref[k, :, c:c + 256], NN, preferred_element_type=jnp.float32)
                for k in range(3)
            )
            data_ref[at, c:c + 256] = (a + b) + d

        @pl.when(i == 0)
        def _():
            pl.semaphore_wait(barrier, devices - 1)
            for copy in own:
                copy.start()

        @pl.loop(0, many)
        def _(j):
            k = i * many + j

            @pl.when(k > 0)
            def _():
                there = target(k, group, member)
                data(k, there).start()
                mark(there).start()

    for copy in own:
        copy.wait()
    rest = pl.ds(0, (devices - 1) * cap)
    far = lax.rem(group + 1, groups)
    everything = pltpu.make_async_remote_copy(
        src_ref=data_ref.at[rest, :], dst_ref=flat_ref.at[rest, :], send_sem=data_send, recv_sem=data_recv,
        device_id=(far, member), device_id_type=MESH)
    rest = pl.ds(0, devices - 1)
    marked = pltpu.make_async_remote_copy(
        src_ref=mark_ref.at[rest], dst_ref=tags_ref.at[rest], send_sem=mark_send, recv_sem=mark_recv,
        device_id=(far, member), device_id_type=MESH)
    everything.wait_send()
    marked.wait_send()
    marked.wait_recv()
    everything.wait_recv()


def move(rows, hold, old, dest, local, groups, members, slots):
    row_dev, D = rows.shape
    dma = pltpu.SemaphoreType.DMA
    devices = groups * members
    return pl.pallas_call(
        functools.partial(move_kernel, groups, members),
        out_shape=(
            jax.ShapeDtypeStruct((slots, D), jnp.float32),
            jax.ShapeDtypeStruct((devices, 1, B), jnp.float32),
        ),
        in_specs=[pl.BlockSpec(memory_space=pltpu.VMEM)] * 5,
        out_specs=[pl.BlockSpec(memory_space=pl.ANY)] * 2,
        scratch_shapes=[
            pltpu.VMEM((3, row_dev, D), jnp.bfloat16),
            pltpu.VMEM((slots, D), jnp.float32),
            pltpu.VMEM((devices, 1, B), jnp.float32),
            dma, dma, dma, dma, dma((2,)),
        ],
        compiler_params=pltpu.CompilerParams(collective_id=1, has_side_effects=True, vmem_limit_bytes=60 * 2**20),
    )(rows, hold, old, dest, local)


def on_device(rows, old_list, old_centroids, dest_device, new_local, centroids):
    n_group = lax.axis_size("group")
    n_member = lax.axis_size("member")
    devices = n_group * n_member
    row_dev = rows.shape[0]
    width = rows.shape[1]
    capacity = max(2, 2 * row_dev // devices)
    slots = devices * capacity
    flat, marks = move(
        rows, old_list[None, :], old_centroids, dest_device.reshape(1, row_dev), new_local[None, :], n_group, n_member, slots)
    flat_tags = marks.reshape(devices, B)[:, :capacity].reshape(-1)
    lists = centroids.shape[0]
    lane = lax.broadcasted_iota(jnp.int32, (slots, lists * B), 1)
    sel = (flat_tags[:, None] == (1 + lane // B).astype(jnp.float32)).astype(jnp.float32)
    factors, result = factor_all(flat, sel, centroids)
    return (result, factors)


def solution(mesh):
    return jax.shard_map(
        on_device,
        mesh=mesh,
        in_specs=(
            P(("group", "member"), None),
            P(("group", "member")),
            P(),
            P(("group", "member"), None),
            P(("group", "member")),
            P("group", None),
        ),
        out_specs=(P(("group", "member"), None), P("group", None, None)),
        check_vma=False,
    )
```

```python
import functools

import jax, jax.numpy as jnp
from jax import lax
from jax.experimental import pallas as pl
from jax.experimental.pallas import tpu as pltpu
from jax.sharding import PartitionSpec as P
NT = (((1,), (1,)), ((), ()))
NN = (((1,), (0,)), ((), ()))
B = 128
ridge = 0.1

def split(x):
    hi = x.astype(jnp.bfloat16)
    return hi, (x - hi.astype(jnp.float32)).astype(jnp.bfloat16)

def dot3(a, b, dims):
    f = functools.partial(lax.dot_general, dimension_numbers=dims, preferred_element_type=jnp.float32)
    return f(a[0], b[0]) + (f(a[0], b[1]) + f(a[1], b[0]))

def lane_iota():
    return lax.broadcasted_iota(jnp.int32, (8, B), 1)


def row_iota():
    return lax.broadcasted_iota(jnp.int32, (8, B), 0)


def across(x, k):
    return jnp.broadcast_to(x[:, k : k + 1], (8, B))


def down(x, k):
    return jnp.broadcast_to(x[k : k + 1, :], (8, B))


def factor_steps(load, out):
    n = B // 8
    row, lane = row_iota(), lane_iota()
    z = [load(i) for i in range(n)]
    upper, inverse = [], []
    for m in range(n):
        lo = 8 * m
        last = m == n - 1
        here = (lane >= lo) & (lane < lo + 8)
        p = z[m]
        M = [across(p, lo + k) for k in range(8)]
        q = jnp.where(here, jnp.where(lane == row + lo, 1.0, 0.0), p)
        if not last:
            x = z[m + 1]
            N = [across(x, lo + k) for k in range(8)]
            x = jnp.where(here, 0.0, x)
        yield
        for k in range(8):
            pivots = [down(M[j], k) for j in range(k, 8)]
            s = lax.rsqrt(pivots[0])
            g = [None] * k + [v * s for v in pivots]
            F = jnp.where(row > k, M[k] * s, 0.0)
            for j in range(k + 1, 8):
                M[j] = M[j] - F * g[j]
            p = jnp.where(row == k, p * s, p)
            q = jnp.where(row == k, q * s, q)
            pk, qk = down(p, k), down(q, k)
            p = p - F * pk
            q = q - F * qk
            if not last:
                f = N[k] * s
                for j in range(k + 1, 8):
                    N[j] = N[j] - f * g[j]
                x = x - f * qk
        yield
        if not last:
            z[m + 1] = x
        upper.append(jnp.where(lane >= lo + 8, q, jnp.where(lane >= lo + row, p, 0.0)))
        inverse.append(jnp.where(lane < lo + 8, q, 0.0))
        if m + 2 < n:
            qh, ql = split(q)
            d = lax.dot_general(
                jnp.concatenate([qh, ql, qh], 0),
                jnp.concatenate([qh, qh, ql], 0),
                (((0,), (0,)), ((), ())),
                preferred_element_type=jnp.float32,
            )
            for i in range(m + 2, n):
                z[i] = jnp.where(here, 0.0, z[i]) - d[8 * i : 8 * i + 8, :]
        yield
    out.append((jnp.concatenate(upper, axis=0), jnp.concatenate(inverse, axis=0)))


def factor2(load0, load1):
    outs = [[], []]
    pair = [factor_steps(load0, outs[0]), factor_steps(load1, outs[1])]
    for _ in zip(*pair):
        pass
    for one in pair:
        for _ in one:
            pass
    return outs[0][0], outs[1][0]


PW = 256
MESH = pl.DeviceIdType.MESH


def rows_of(flat_ref, sel_ref, cent_ref, rows, cols, l):
    width = flat_ref[rows, cols].shape[1]
    s = sel_ref[rows, pl.ds(pl.multiple_of(l * B, B), B)]
    s = jnp.concatenate([s] * (width // B), axis=1)
    return (flat_ref[rows, cols] - cent_ref[pl.ds(l, 1), cols]) * s


def main_kernel(flat_ref, marks_ref, cent_ref, fac_ref, out_ref, rt_ref, give_ref, take_ref, acc_ref, xa_ref, za_ref, xb_ref, zb_ref,
                cov_ref, a_ref, r_ref, uv_ref, sel_ref, pair_sem, xa_sem, za_sem, xb_sem, zb_sem, xc_sem, zc_sem, xd_sem, zd_sem, fw_sem):
    D = flat_ref.shape[1]
    slots = flat_ref.shape[0]
    group = lax.axis_index("group")
    me = lax.axis_index("member")
    core = lax.rem(me, 2)
    zh = me // 8
    x = lax.rem(me // 2, 4)
    partner = me + 1 - 2 * core
    zpeer = lax.rem(me + 8, 16)
    others = [lax.rem(x + d, 4) for d in range(1, 4)]
    xpeers = [zh * 8 + o * 2 + core for o in others]

    barrier = pltpu.get_barrier_semaphore()
    for peer in [partner, zpeer] + xpeers:
        pl.semaphore_signal(barrier, inc=1, device_id=(group, peer), device_id_type=MESH)

    panels = D // PW
    first = [sum(D - PW * i for i in range(p)) for p in range(panels)]

    def remote(src, dst, sem, at, peer):
        return pltpu.make_async_remote_copy(
            src_ref=src, dst_ref=dst, send_sem=sem.at[(0, *at)], recv_sem=sem.at[(1, *at)], device_id=(group, peer),
            device_id_type=MESH)

    def go(copies):
        for copy in copies:
            copy.start()

    def landed(copies):
        for copy in copies:
            copy.wait_recv()

    marks = marks_ref[...].astype(jnp.bfloat16)
    senders = marks_ref.shape[0]

    @pl.loop(0, slots // 256)
    def _(i):
        rows = pl.ds(pl.multiple_of(i * 256, 256), 256)
        slot, lane = (lax.broadcasted_iota(jnp.int32, (256, B), d) for d in range(2))
        slot = slot + i * 256
        of_sender = jnp.where(over(slot, slots // senders) == lane, 1.0, 0.0).astype(jnp.bfloat16)
        own_marks = lax.dot_general(of_sender, marks, NN, preferred_element_type=jnp.float32)
        here = lax.rem(slot, full(slots // senders, slot)) == lane
        tag = jnp.sum(jnp.where(here, own_marks, 0.0), axis=1, keepdims=True)
        for l in range(2):
            sel_ref[rows, l * B:(l + 1) * B] = jnp.broadcast_to(jnp.where(tag == l + 1.0, 1.0, 0.0), (256, B))
        for c in range(0, D, 256):
            cols = pl.ds(c, 256)
            x = rows_of(flat_ref, sel_ref, cent_ref, rows, cols, 0) + rows_of(flat_ref, sel_ref, cent_ref, rows, cols, 1)
            hi, lo = split(x.T)
            rt_ref[0, pl.ds(c, 256), rows] = hi
            rt_ref[1, pl.ds(c, 256), rows] = lo

    pl.semaphore_wait(barrier, 5)

    def gram(p, l, dst):
        cols = pl.ds(p * PW, PW)
        mh, ml = split(rows_of(flat_ref, sel_ref, cent_ref, pl.ds(0, slots), cols, l))
        dot = functools.partial(lax.dot_general, dimension_numbers=NN, preferred_element_type=jnp.float32)

        @pl.loop(0, (D - p * PW) // 256)
        def _(i):
            feat = pl.ds(pl.multiple_of(p * PW + i * 256, 256), 256)
            th, tl = rt_ref[0, feat, :], rt_ref[1, feat, :]
            dst[pl.ds(pl.multiple_of(first[p] + i * 256, 256), 256), :] = dot(th, mh) + (dot(th, ml) + dot(tl, mh))
        if p == 0:
            count = jnp.sum(sel_ref[:, pl.ds(pl.multiple_of(l * B, B), B)], axis=0, keepdims=True)
            dst[0:8, B:2 * B] = jnp.broadcast_to(count, (8, B))

    def span(p):
        return pl.ds(first[p], D - p * PW)

    def pair(p):
        return [remote(give_ref.at[span(p), :], take_ref.at[span(p), :], pair_sem, (p,), partner)]

    def at(start, n):
        return pl.ds(start if isinstance(start, int) else pl.multiple_of(start, 8), n)

    def sizes(p):
        return first[p], (D - p * PW) // 2, (D - p * PW) // 16

    def xa(p):
        f, h, e = sizes(p)
        return [remote(acc_ref.at[at(f + others[d] * 2 * e, 2 * e), :], xa_ref.at[d, pl.ds(f // 8, 2 * e), :],
                       xa_sem, (p, d), xpeers[d]) for d in range(3)]

    def za(p):
        f, h, e = sizes(p)
        return [remote(acc_ref.at[at(f + h + (1 - zh) * 4 * e, 4 * e), :], za_ref.at[pl.ds(f // 4, 4 * e), :],
                       za_sem, (p,), zpeer)]

    def zb(p):
        f, h, e = sizes(p)
        return [remote(acc_ref.at[at(f + x * 2 * e + (1 - zh) * e, e), :], zb_ref.at[pl.ds(f // 16, e), :],
                       zb_sem, (p,), zpeer)]

    def xb(p):
        f, h, e = sizes(p)
        return [remote(acc_ref.at[at(f + h + zh * 4 * e + others[d] * e, e), :], xb_ref.at[d, pl.ds(f // 16, e), :],
                       xb_sem, (p, d), xpeers[d]) for d in range(3)]

    def cov(p, start, n):
        return cov_ref.at[core, at(p * PW + start, n), pl.ds(p * PW, PW)]

    def zc(p):
        f, h, e = sizes(p)
        ref = cov(p, x * 2 * e + zh * e, e)
        return [remote(ref, ref, zc_sem, (p,), zpeer)]

    def xc(p):
        f, h, e = sizes(p)
        ref = cov(p, h + zh * 4 * e + x * e, e)
        return [remote(ref, ref, xc_sem, (p, d), xpeers[d]) for d in range(3)]

    def xd(p):
        f, h, e = sizes(p)
        ref = cov(p, x * 2 * e, 2 * e)
        return [remote(ref, ref, xd_sem, (p, d), xpeers[d]) for d in range(3)]

    def zd(p):
        f, h, e = sizes(p)
        ref = cov(p, h + zh * 4 * e, 4 * e)
        return [remote(ref, ref, zd_sem, (p,), zpeer)]

    def forward(p):
        ref = cov_ref.at[core, pl.ds(p * PW, D - p * PW), pl.ds(p * PW, PW)]
        return [remote(ref, ref, fw_sem, (p,), partner)]

    def compute(p):
        gram(p, 1 - core, give_ref)
        go(pair(p))
        gram(p, core, acc_ref)

    def stage1(p):
        landed(pair(p))
        acc_ref[span(p), :] += take_ref[span(p), :]
        go(xa(p))
        go(za(p))

    def stage2(p):
        f, h, e = sizes(p)
        landed(xa(p))
        total = acc_ref[at(f + x * 2 * e, 2 * e), :]
        for d in range(3):
            total = total + xa_ref[d, pl.ds(f // 8, 2 * e), :]
        acc_ref[at(f + x * 2 * e, 2 * e), :] = total
        go(zb(p))
        landed(za(p))
        acc_ref[at(f + h + zh * 4 * e, 4 * e), :] += za_ref[pl.ds(f // 4, 4 * e), :]
        go(xb(p))

    def stage3(p):
        f, h, e = sizes(p)
        landed(zb(p))
        cov(p, x * 2 * e + zh * e, e)[...] = acc_ref[at(f + x * 2 * e + zh * e, e), :] + zb_ref[pl.ds(f // 16, e), :]
        go(zc(p))
        landed(xb(p))
        total = acc_ref[at(f + h + zh * 4 * e + x * e, e), :]
        for d in range(3):
            total = total + xb_ref[d, pl.ds(f // 16, e), :]
        cov(p, h + zh * 4 * e + x * e, e)[...] = total
        go(xc(p))

    def stage4(p):
        landed(zc(p))
        go(xd(p))
        landed(xc(p))
        go(zd(p))

    def stage5(p):
        landed(xd(p))
        landed(zd(p))
        go(forward(p))

    def arrive(p):
        landed(forward(p))
        o = p * PW
        row, col = (lax.broadcasted_iota(jnp.int32, (PW, PW), i) for i in range(2))
        eye = jnp.where(row == col, ridge, 0.0)
        for l in range(2):
            count = jnp.maximum(cov_ref[l, 0:1, B:2 * B], 1.0)
            scale = jnp.concatenate([1.0 / count] * (PW // B), axis=1)
            top = cov_ref[l, o:o + PW, o:o + PW] * scale + eye
            right = split(fac_ref[l, o:o + PW, 0:o]) if p else None
            a_ref[l, o:o + PW, o:o + PW] = top - dot3(right, right, NT) if p else top
            for i in range(o + PW, D, PW):
                rest = cov_ref[l, i:i + PW, o:o + PW] * scale
                if p:
                    rest = rest - dot3(split(fac_ref[l, i:i + PW, 0:o]), right, NT)
                a_ref[l, i:i + PW, o:o + PW] = rest

    def start_of(kb):
        if kb == 0:
            stage1(2)
            arrive(0)
        elif kb == 1:
            stage4(1)
            stage2(2)
            stage1(3)
        elif kb == 2:
            stage2(3)
            arrive(1)
        elif kb == 3:
            stage3(3)
        elif kb == 4:
            arrive(2)
        elif kb == 6:
            arrive(3)

    def middle_of(kb):
        if kb == 0:
            stage3(1)
        elif kb == 1:
            stage5(1)
            stage3(2)
        elif kb == 2:
            stage4(2)
        elif kb == 3:
            stage5(2)
            stage4(3)
        elif kb == 4:
            stage5(3)

    compute(0)
    stage1(0)
    compute(1)
    stage2(0)
    compute(2)
    stage3(0)
    stage1(1)
    compute(3)
    stage4(0)
    for c in range(0, D, 256):
        cols = pl.ds(c, 256)
        every = pl.ds(0, slots)
        r_ref[:, c:c + 256] = rows_of(flat_ref, sel_ref, cent_ref, every, cols, 0) + rows_of(
            flat_ref, sel_ref, cent_ref, every, cols, 1)
    fac_ref[...] = jnp.zeros_like(fac_ref)
    stage2(1)
    stage5(0)
    blocks = D // B

    def body(kb, _):
        for s in range(blocks - 1):
            @pl.when(kb == s)
            def _():
                start_of(s)
        off = pl.multiple_of(kb * B, B)

        def load(l):
            return lambda i: a_ref[l, pl.ds(pl.multiple_of(off + 8 * i, 8), 8), pl.ds(off, B)]

        for l, (u, v) in enumerate(factor2(load(0), load(1))):
            uv_ref[l] = v
            fac_ref[l, pl.ds(off, B), pl.ds(off, B)] = u.T
        for s in range(blocks):
            @pl.when(kb == s)
            def _():
                middle_of(s)
                o = s * B
                vs = [split(uv_ref[l]) for l in range(2)]
                n = D - o - B
                if n:
                    for l in range(2):
                        lp = dot3(split(a_ref[l, o + B:D, o:o + B]), vs[l], NT)
                        fac_ref[l, o + B:D, o:o + B] = lp
                        if s % 2 == 0:
                            lh = split(lp)
                            a_ref[l, o + B:D, o + B:o + 2 * B] -= dot3(lh, tuple(x[:B] for x in lh), NT)
                vcat = tuple(jnp.concatenate([vs[0][i], vs[1][i]], axis=0) for i in range(2))
                if n:
                    lcat = split(jnp.concatenate([fac_ref[0, o + B:D, o:o + B], fac_ref[1, o + B:D, o:o + B]], axis=1))
                step = 256
                for c in range(0, slots, step):
                    y = dot3(split(r_ref[c:c + step, o:o + B]), vcat, NT)
                    x0 = y[:, :B] * sel_ref[c:c + step, 0:B]
                    x1 = y[:, B:] * sel_ref[c:c + step, B:2 * B]
                    out_ref[c:c + step, o:o + B] = x0 + x1
                    if n:
                        xs = split(jnp.concatenate([x0, x1], axis=1))
                        r_ref[c:c + step, o + B:D] -= dot3(xs, lcat, NT)
        return 0

    lax.fori_loop(0, blocks, body, 0)
    for p in range(panels):
        for make in (pair, xa, za, xb, zb, xc, zc, xd, zd, forward):
            for copy in make(p):
                copy.wait_send()


def factor_all(flat, marks, cent):
    slots, D = flat.shape
    panels = D // PW
    total = sum(D - PW * i for i in range(panels))
    dma = pltpu.SemaphoreType.DMA
    return pl.pallas_call(
        main_kernel,
        out_shape=(pltpu.VMEM((2, D, D), jnp.float32), pltpu.VMEM((slots, D), jnp.float32)),
        in_specs=[pl.BlockSpec(memory_space=pltpu.VMEM)] * 3,
        out_specs=[pl.BlockSpec(memory_space=pltpu.VMEM)] * 2,
        scratch_shapes=[
            pltpu.VMEM((2, D, slots), jnp.bfloat16),
            pltpu.VMEM((total, PW), jnp.float32),
            pltpu.VMEM((total, PW), jnp.float32),
            pltpu.VMEM((total, PW), jnp.float32),
            pltpu.VMEM((3, total // 8, PW), jnp.float32),
            pltpu.VMEM((total // 4, PW), jnp.float32),
            pltpu.VMEM((3, total // 16, PW), jnp.float32),
            pltpu.VMEM((total // 16, PW), jnp.float32),
            pltpu.VMEM((2, D, D), jnp.float32),
            pltpu.VMEM((2, D, D), jnp.float32),
            pltpu.VMEM((slots, D), jnp.float32),
            pltpu.VMEM((2, B, B), jnp.float32),
            pltpu.VMEM((slots, 2 * B), jnp.float32),
            dma((2, panels)),
            dma((2, panels, 3)), dma((2, panels)), dma((2, panels, 3)), dma((2, panels)),
            dma((2, panels, 3)), dma((2, panels)), dma((2, panels, 3)), dma((2, panels)),
            dma((2, panels)),
        ],
        compiler_params=pltpu.CompilerParams(
            collective_id=0, has_side_effects=True, vmem_limit_bytes=50 * 2**20),
    )(flat, marks, cent)


def full(n, k):
    return jnp.full(jnp.shape(k), n, jnp.int32)


def over(k, n):
    return lax.div(k, full(n, k))


def target(k, group, member):
    x = lax.rem(member // 2 + k, full(4, k))
    y = lax.rem(group + over(k, 4) + k, full(4, k))
    z = lax.rem(member // 8 * 2 + group // 4 + over(k, 16) + k + over(k, 4), full(4, k))
    core = lax.rem(member + over(k, 64), full(2, k))
    return lax.rem(z, full(2, k)) * 4 + y, over(z, 2) * 8 + x * 2 + core


def move_kernel(groups, members, rows_ref, hold_ref, old_ref, dest_ref, local_ref, flat_ref, tags_ref, split_ref, data_ref, mark_ref,
                data_send, data_recv, mark_send, mark_recv, own_sem):
    group = lax.axis_index("group")
    member = lax.axis_index("member")
    me = group * members + member
    devices = groups * members
    cap = data_ref.shape[0] // devices
    row_dev, D = rows_ref.shape

    barrier = pltpu.get_barrier_semaphore()

    @pl.loop(1, devices)
    def _(k):
        pl.semaphore_signal(barrier, inc=1, device_id=target(k, group, member), device_id_type=MESH)

    def parts(x):
        out = []
        for _ in range(3):
            out.append(x.astype(jnp.bfloat16))
            x = x - out[-1].astype(jnp.float32)
        return out

    def ones(hit):
        return jnp.where(hit, 1.0, 0.0).astype(jnp.bfloat16)

    dot = functools.partial(lax.dot_general, preferred_element_type=jnp.float32)
    olds = old_ref.shape[0]
    held = ones(lax.broadcasted_iota(jnp.int32, (olds, row_dev), 0) == hold_ref[...])
    for c in range(0, D, 256):
        a, b, d = (dot(held, part, (((0,), (0,)), ((), ()))) for part in parts(old_ref[:, c:c + 256]))
        for i, part in enumerate(parts(rows_ref[:, c:c + 256] + ((a + b) + d))):
            split_ref[i, :, c:c + 256] = part

    dest = dest_ref[...]
    to_device = ones(lax.broadcasted_iota(jnp.int32, (devices, row_dev), 0) == dest)
    row, col = (lax.broadcasted_iota(jnp.int32, (row_dev, row_dev), i) for i in range(2))
    before = dot(to_device, ones(row < col), NN)
    rank = jnp.sum(before * to_device.astype(jnp.float32), axis=0, keepdims=True).astype(jnp.int32)
    slot = lax.broadcasted_iota(jnp.int32, (B, row_dev), 0)
    tag = (local_ref[...] + 1).astype(jnp.float32)
    to_slot = jnp.where(slot == rank, tag, 0.0).astype(jnp.bfloat16)
    mark_ref[...] = dot(to_device, to_slot, NT).reshape(devices, 1, B)

    mine = pl.ds(pl.multiple_of(me * cap, cap), cap)

    def data(k, there):
        return pltpu.make_async_remote_copy(
            src_ref=data_ref.at[pl.ds(pl.multiple_of(k * cap, cap), cap), :], dst_ref=flat_ref.at[mine, :],
            send_sem=data_send, recv_sem=data_recv, device_id=there, device_id_type=MESH)

    def mark(there):
        return pltpu.make_async_remote_copy(
            src_ref=mark_ref.at[pl.ds(there[0] * members + there[1], 1)], dst_ref=tags_ref.at[pl.ds(me, 1)],
            send_sem=mark_send, recv_sem=mark_recv, device_id=there, device_id_type=MESH)

    many = B // cap
    own = (
        pltpu.make_async_copy(data_ref.at[pl.ds(0, cap), :], flat_ref.at[mine, :], own_sem.at[0]),
        pltpu.make_async_copy(mark_ref.at[pl.ds(me, 1)], tags_ref.at[pl.ds(me, 1)], own_sem.at[1]),
    )
    line = lax.broadcasted_iota(jnp.int32, (B, B), 0)

    @pl.loop(0, devices // many)
    def _(i):
        g, m = target(i * many + (line >> 3), group, member)
        ids = (g * members + m) * cap + (line & 7)
        hit = jnp.concatenate([ids] * (row_dev // B), axis=1) == dest * cap + rank
        pick = jnp.where(hit, 1.0, 0.0).astype(jnp.bfloat16)
        at = pl.ds(pl.multiple_of(i * B, B), B)
        for c in range(0, D, 256):
            a, b, d = (
                lax.dot_general(pick, split_ref[k, :, c:c + 256], NN, preferred_element_type=jnp.float32)
                for k in range(3)
            )
            data_ref[at, c:c + 256] = (a + b) + d

        @pl.when(i == 0)
        def _():
            pl.semaphore_wait(barrier, devices - 1)
            for copy in own:
                copy.start()

        @pl.loop(0, many)
        def _(j):
            k = i * many + j

            @pl.when(k > 0)
            def _():
                there = target(k, group, member)
                data(k, there).start()
                mark(there).start()

    for copy in own:
        copy.wait()
    rest = pl.ds(0, (devices - 1) * cap)
    far = lax.rem(group + 1, groups)
    everything = pltpu.make_async_remote_copy(
        src_ref=data_ref.at[rest, :], dst_ref=flat_ref.at[rest, :], send_sem=data_send, recv_sem=data_recv,
        device_id=(far, member), device_id_type=MESH)
    rest = pl.ds(0, devices - 1)
    marked = pltpu.make_async_remote_copy(
        src_ref=mark_ref.at[rest], dst_ref=tags_ref.at[rest], send_sem=mark_send, recv_sem=mark_recv,
        device_id=(far, member), device_id_type=MESH)
    everything.wait_send()
    marked.wait_send()
    marked.wait_recv()
    everything.wait_recv()


def move(rows, hold, old, dest, local, groups, members, slots):
    row_dev, D = rows.shape
    dma = pltpu.SemaphoreType.DMA
    devices = groups * members
    return pl.pallas_call(
        functools.partial(move_kernel, groups, members),
        out_shape=(
            jax.ShapeDtypeStruct((slots, D), jnp.float32),
            jax.ShapeDtypeStruct((devices, 1, B), jnp.float32),
        ),
        in_specs=[pl.BlockSpec(memory_space=pltpu.VMEM)] * 5,
        out_specs=[pl.BlockSpec(memory_space=pl.ANY)] * 2,
        scratch_shapes=[
            pltpu.VMEM((3, row_dev, D), jnp.bfloat16),
            pltpu.VMEM((slots, D), jnp.float32),
            pltpu.VMEM((devices, 1, B), jnp.float32),
            dma, dma, dma, dma, dma((2,)),
        ],
        compiler_params=pltpu.CompilerParams(collective_id=1, has_side_effects=True, vmem_limit_bytes=60 * 2**20),
    )(rows, hold, old, dest, local)


def on_device(rows, old_list, old_centroids, dest_device, new_local, centroids):
    n_group = lax.axis_size("group")
    n_member = lax.axis_size("member")
    devices = n_group * n_member
    row_dev = rows.shape[0]
    width = rows.shape[1]
    capacity = max(2, 2 * row_dev // devices)
    slots = devices * capacity
    flat, marks = move(
        rows, old_list[None, :], old_centroids, dest_device.reshape(1, row_dev), new_local[None, :], n_group, n_member, slots)
    factors, result = factor_all(flat, marks.reshape(devices, B), centroids)
    return (result, factors)


def solution(mesh):
    return jax.shard_map(
        on_device,
        mesh=mesh,
        in_specs=(
            P(("group", "member"), None),
            P(("group", "member")),
            P(),
            P(("group", "member"), None),
            P(("group", "member")),
            P("group", None),
        ),
        out_specs=(P(("group", "member"), None), P("group", None, None)),
        check_vma=False,
    )
```

```python
import functools

import jax, jax.numpy as jnp
from jax import lax
from jax.experimental import pallas as pl
from jax.experimental.pallas import tpu as pltpu
from jax.sharding import PartitionSpec as P
NT = (((1,), (1,)), ((), ()))
NN = (((1,), (0,)), ((), ()))
B = 128
ridge = 0.1

def split(x):
    hi = x.astype(jnp.bfloat16)
    return hi, (x - hi.astype(jnp.float32)).astype(jnp.bfloat16)

def dot3(a, b, dims):
    f = functools.partial(lax.dot_general, dimension_numbers=dims, preferred_element_type=jnp.float32)
    return f(a[0], b[0]) + (f(a[0], b[1]) + f(a[1], b[0]))

def lane_iota():
    return lax.broadcasted_iota(jnp.int32, (8, B), 1)


def row_iota():
    return lax.broadcasted_iota(jnp.int32, (8, B), 0)


def across(x, k):
    return jnp.broadcast_to(x[:, k : k + 1], (8, B))


def down(x, k):
    return jnp.broadcast_to(x[k : k + 1, :], (8, B))


def factor_steps(load, out):
    n = B // 8
    row, lane = row_iota(), lane_iota()
    z = [load(i) for i in range(n)]
    upper, inverse = [], []
    for m in range(n):
        lo = 8 * m
        last = m == n - 1
        here = (lane >= lo) & (lane < lo + 8)
        p = z[m]
        M = [across(p, lo + k) for k in range(8)]
        q = jnp.where(here, jnp.where(lane == row + lo, 1.0, 0.0), p)
        if not last:
            x = z[m + 1]
            N = [across(x, lo + k) for k in range(8)]
            x = jnp.where(here, 0.0, x)
        yield
        for k in range(8):
            pivots = [down(M[j], k) for j in range(k, 8)]
            s = lax.rsqrt(pivots[0])
            g = [None] * k + [v * s for v in pivots]
            F = jnp.where(row > k, M[k] * s, 0.0)
            for j in range(k + 1, 8):
                M[j] = M[j] - F * g[j]
            p = jnp.where(row == k, p * s, p)
            q = jnp.where(row == k, q * s, q)
            pk, qk = down(p, k), down(q, k)
            p = p - F * pk
            q = q - F * qk
            if not last:
                f = N[k] * s
                for j in range(k + 1, 8):
                    N[j] = N[j] - f * g[j]
                x = x - f * qk
        yield
        if not last:
            z[m + 1] = x
        upper.append(jnp.where(lane >= lo + 8, q, jnp.where(lane >= lo + row, p, 0.0)))
        inverse.append(jnp.where(lane < lo + 8, q, 0.0))
        if m + 2 < n:
            qh, ql = split(q)
            d = lax.dot_general(
                jnp.concatenate([qh, ql, qh], 0),
                jnp.concatenate([qh, qh, ql], 0),
                (((0,), (0,)), ((), ())),
                preferred_element_type=jnp.float32,
            )
            for i in range(m + 2, n):
                z[i] = jnp.where(here, 0.0, z[i]) - d[8 * i : 8 * i + 8, :]
        yield
    out.append((jnp.concatenate(upper, axis=0), jnp.concatenate(inverse, axis=0)))


def factor2(load0, load1):
    outs = [[], []]
    pair = [factor_steps(load0, outs[0]), factor_steps(load1, outs[1])]
    for _ in zip(*pair):
        pass
    for one in pair:
        for _ in one:
            pass
    return outs[0][0], outs[1][0]


PW = 256
MESH = pl.DeviceIdType.MESH


def rows_of(flat_ref, sel_ref, cent_ref, rows, cols, l):
    width = flat_ref[rows, cols].shape[1]
    s = sel_ref[rows, pl.ds(pl.multiple_of(l * B, B), B)]
    s = jnp.concatenate([s] * (width // B), axis=1)
    return (flat_ref[rows, cols] - cent_ref[pl.ds(l, 1), cols]) * s


def main_kernel(flat_ref, marks_ref, cent_ref, fac_ref, out_ref, rt_ref, give_ref, take_ref, acc_ref, xa_ref, za_ref, xb_ref, zb_ref,
                cov_ref, a_ref, r_ref, uv_ref, sel_ref, pair_sem, xa_sem, za_sem, xb_sem, zb_sem, xc_sem, zc_sem, xd_sem, zd_sem, fw_sem):
    D = flat_ref.shape[1]
    slots = flat_ref.shape[0]
    group = lax.axis_index("group")
    me = lax.axis_index("member")
    core = lax.rem(me, 2)
    zh = me // 8
    x = lax.rem(me // 2, 4)
    partner = me + 1 - 2 * core
    zpeer = lax.rem(me + 8, 16)
    others = [lax.rem(x + d, 4) for d in range(1, 4)]
    xpeers = [zh * 8 + o * 2 + core for o in others]

    barrier = pltpu.get_barrier_semaphore()
    for peer in [partner, zpeer] + xpeers:
        pl.semaphore_signal(barrier, inc=1, device_id=(group, peer), device_id_type=MESH)

    panels = D // PW
    first = [sum(D - PW * i for i in range(p)) for p in range(panels)]

    def remote(src, dst, sem, at, peer):
        return pltpu.make_async_remote_copy(
            src_ref=src, dst_ref=dst, send_sem=sem.at[(0, *at)], recv_sem=sem.at[(1, *at)], device_id=(group, peer),
            device_id_type=MESH)

    def go(copies):
        for copy in copies:
            copy.start()

    def landed(copies):
        for copy in copies:
            copy.wait_recv()

    marks = marks_ref[...].astype(jnp.bfloat16)
    senders = marks_ref.shape[0]

    @pl.loop(0, slots // 256)
    def _(i):
        rows = pl.ds(pl.multiple_of(i * 256, 256), 256)
        slot, lane = (lax.broadcasted_iota(jnp.int32, (256, B), d) for d in range(2))
        slot = slot + i * 256
        of_sender = jnp.where(over(slot, slots // senders) == lane, 1.0, 0.0).astype(jnp.bfloat16)
        own_marks = lax.dot_general(of_sender, marks, NN, preferred_element_type=jnp.float32)
        here = lax.rem(slot, full(slots // senders, slot)) == lane
        tag = jnp.sum(jnp.where(here, own_marks, 0.0), axis=1, keepdims=True)
        for l in range(2):
            sel_ref[rows, l * B:(l + 1) * B] = jnp.broadcast_to(jnp.where(tag == l + 1.0, 1.0, 0.0), (256, B))
        for c in range(0, D, 256):
            cols = pl.ds(c, 256)
            x = rows_of(flat_ref, sel_ref, cent_ref, rows, cols, 0) + rows_of(flat_ref, sel_ref, cent_ref, rows, cols, 1)
            r_ref[rows, cols] = x
            hi, lo = split(x.T)
            rt_ref[0, pl.ds(c, 256), rows] = hi
            rt_ref[1, pl.ds(c, 256), rows] = lo

    pl.semaphore_wait(barrier, 5)

    def gram(p, l, dst):
        cols = pl.ds(p * PW, PW)
        mh, ml = split(rows_of(flat_ref, sel_ref, cent_ref, pl.ds(0, slots), cols, l))
        dot = functools.partial(lax.dot_general, dimension_numbers=NN, preferred_element_type=jnp.float32)

        @pl.loop(0, (D - p * PW) // 256)
        def _(i):
            feat = pl.ds(pl.multiple_of(p * PW + i * 256, 256), 256)
            th, tl = rt_ref[0, feat, :], rt_ref[1, feat, :]
            dst[pl.ds(pl.multiple_of(first[p] + i * 256, 256), 256), :] = dot(th, mh) + (dot(th, ml) + dot(tl, mh))
        if p == 0:
            count = jnp.sum(sel_ref[:, pl.ds(pl.multiple_of(l * B, B), B)], axis=0, keepdims=True)
            dst[0:8, B:2 * B] = jnp.broadcast_to(count, (8, B))

    def span(p):
        return pl.ds(first[p], D - p * PW)

    def pair(p):
        return [remote(give_ref.at[span(p), :], take_ref.at[span(p), :], pair_sem, (p,), partner)]

    def at(start, n):
        return pl.ds(start if isinstance(start, int) else pl.multiple_of(start, 8), n)

    def sizes(p):
        return first[p], (D - p * PW) // 2, (D - p * PW) // 16

    def xa(p):
        f, h, e = sizes(p)
        return [remote(acc_ref.at[at(f + others[d] * 2 * e, 2 * e), :], xa_ref.at[d, pl.ds(f // 8, 2 * e), :],
                       xa_sem, (p, d), xpeers[d]) for d in range(3)]

    def za(p):
        f, h, e = sizes(p)
        return [remote(acc_ref.at[at(f + h + (1 - zh) * 4 * e, 4 * e), :], za_ref.at[pl.ds(f // 4, 4 * e), :],
                       za_sem, (p,), zpeer)]

    def zb(p):
        f, h, e = sizes(p)
        return [remote(acc_ref.at[at(f + x * 2 * e + (1 - zh) * e, e), :], zb_ref.at[pl.ds(f // 16, e), :],
                       zb_sem, (p,), zpeer)]

    def xb(p):
        f, h, e = sizes(p)
        return [remote(acc_ref.at[at(f + h + zh * 4 * e + others[d] * e, e), :], xb_ref.at[d, pl.ds(f // 16, e), :],
                       xb_sem, (p, d), xpeers[d]) for d in range(3)]

    def cov(p, start, n):
        return cov_ref.at[core, at(p * PW + start, n), pl.ds(p * PW, PW)]

    def zc(p):
        f, h, e = sizes(p)
        ref = cov(p, x * 2 * e + zh * e, e)
        return [remote(ref, ref, zc_sem, (p,), zpeer)]

    def xc(p):
        f, h, e = sizes(p)
        ref = cov(p, h + zh * 4 * e + x * e, e)
        return [remote(ref, ref, xc_sem, (p, d), xpeers[d]) for d in range(3)]

    def xd(p):
        f, h, e = sizes(p)
        ref = cov(p, x * 2 * e, 2 * e)
        return [remote(ref, ref, xd_sem, (p, d), xpeers[d]) for d in range(3)]

    def zd(p):
        f, h, e = sizes(p)
        ref = cov(p, h + zh * 4 * e, 4 * e)
        return [remote(ref, ref, zd_sem, (p,), zpeer)]

    def forward(p):
        ref = cov_ref.at[core, pl.ds(p * PW, D - p * PW), pl.ds(p * PW, PW)]
        return [remote(ref, ref, fw_sem, (p,), partner)]

    def compute(p):
        gram(p, 1 - core, give_ref)
        go(pair(p))
        gram(p, core, acc_ref)

    def stage1(p):
        landed(pair(p))
        acc_ref[span(p), :] += take_ref[span(p), :]
        go(xa(p))
        go(za(p))

    def stage2(p):
        f, h, e = sizes(p)
        landed(xa(p))
        total = acc_ref[at(f + x * 2 * e, 2 * e), :]
        for d in range(3):
            total = total + xa_ref[d, pl.ds(f // 8, 2 * e), :]
        acc_ref[at(f + x * 2 * e, 2 * e), :] = total
        go(zb(p))
        landed(za(p))
        acc_ref[at(f + h + zh * 4 * e, 4 * e), :] += za_ref[pl.ds(f // 4, 4 * e), :]
        go(xb(p))

    def stage3(p):
        f, h, e = sizes(p)
        landed(zb(p))
        cov(p, x * 2 * e + zh * e, e)[...] = acc_ref[at(f + x * 2 * e + zh * e, e), :] + zb_ref[pl.ds(f // 16, e), :]
        go(zc(p))
        landed(xb(p))
        total = acc_ref[at(f + h + zh * 4 * e + x * e, e), :]
        for d in range(3):
            total = total + xb_ref[d, pl.ds(f // 16, e), :]
        cov(p, h + zh * 4 * e + x * e, e)[...] = total
        go(xc(p))

    def stage4(p):
        landed(zc(p))
        go(xd(p))
        landed(xc(p))
        go(zd(p))

    def stage5(p):
        landed(xd(p))
        landed(zd(p))
        go(forward(p))

    def arrive(p):
        landed(forward(p))
        o = p * PW
        row, col = (lax.broadcasted_iota(jnp.int32, (PW, PW), i) for i in range(2))
        eye = jnp.where(row == col, ridge, 0.0)
        for l in range(2):
            count = jnp.maximum(cov_ref[l, 0:1, B:2 * B], 1.0)
            scale = jnp.concatenate([1.0 / count] * (PW // B), axis=1)
            top = cov_ref[l, o:o + PW, o:o + PW] * scale + eye
            right = split(fac_ref[l, o:o + PW, 0:o]) if p else None
            a_ref[l, o:o + PW, o:o + PW] = top - dot3(right, right, NT) if p else top
            for i in range(o + PW, D, PW):
                rest = cov_ref[l, i:i + PW, o:o + PW] * scale
                if p:
                    rest = rest - dot3(split(fac_ref[l, i:i + PW, 0:o]), right, NT)
                a_ref[l, i:i + PW, o:o + PW] = rest

    def start_of(kb):
        if kb == 0:
            stage1(2)
            arrive(0)
        elif kb == 1:
            stage4(1)
            stage2(2)
            stage1(3)
        elif kb == 2:
            stage2(3)
            arrive(1)
        elif kb == 3:
            stage3(3)
        elif kb == 4:
            arrive(2)
        elif kb == 6:
            arrive(3)

    def middle_of(kb):
        if kb == 0:
            stage3(1)
        elif kb == 1:
            stage5(1)
            stage3(2)
        elif kb == 2:
            stage4(2)
        elif kb == 3:
            stage5(2)
            stage4(3)
        elif kb == 4:
            stage5(3)

    compute(0)
    stage1(0)
    compute(1)
    stage2(0)
    compute(2)
    stage3(0)
    stage1(1)
    compute(3)
    stage4(0)
    for c in range(B, D, B):
        fac_ref[:, c - B:c, c:] = jnp.zeros((2, B, D - c), jnp.float32)
    stage2(1)
    stage5(0)
    blocks = D // B

    def body(kb, _):
        for s in range(blocks - 1):
            @pl.when(kb == s)
            def _():
                start_of(s)
        off = pl.multiple_of(kb * B, B)

        def load(l):
            return lambda i: a_ref[l, pl.ds(pl.multiple_of(off + 8 * i, 8), 8), pl.ds(off, B)]

        for l, (u, v) in enumerate(factor2(load(0), load(1))):
            uv_ref[l] = v
            fac_ref[l, pl.ds(off, B), pl.ds(off, B)] = u.T
        for s in range(blocks):
            @pl.when(kb == s)
            def _():
                middle_of(s)
                o = s * B
                vs = [split(uv_ref[l]) for l in range(2)]
                n = D - o - B
                if n:
                    for l in range(2):
                        lp = dot3(split(a_ref[l, o + B:D, o:o + B]), vs[l], NT)
                        fac_ref[l, o + B:D, o:o + B] = lp
                        if s % 2 == 0:
                            lh = split(lp)
                            a_ref[l, o + B:D, o + B:o + 2 * B] -= dot3(lh, tuple(x[:B] for x in lh), NT)
                vcat = tuple(jnp.concatenate([vs[0][i], vs[1][i]], axis=0) for i in range(2))
                if n:
                    lcat = split(jnp.concatenate([fac_ref[0, o + B:D, o:o + B], fac_ref[1, o + B:D, o:o + B]], axis=1))
                step = 256
                for c in range(0, slots, step):
                    y = dot3(split(r_ref[c:c + step, o:o + B]), vcat, NT)
                    x0 = y[:, :B] * sel_ref[c:c + step, 0:B]
                    x1 = y[:, B:] * sel_ref[c:c + step, B:2 * B]
                    out_ref[c:c + step, o:o + B] = x0 + x1
                    if n:
                        xs = split(jnp.concatenate([x0, x1], axis=1))
                        r_ref[c:c + step, o + B:D] -= dot3(xs, lcat, NT)
        return 0

    lax.fori_loop(0, blocks, body, 0)
    for p in range(panels):
        for make in (pair, xa, za, xb, zb, xc, zc, xd, zd, forward):
            for copy in make(p):
                copy.wait_send()


def factor_all(flat, marks, cent):
    slots, D = flat.shape
    panels = D // PW
    total = sum(D - PW * i for i in range(panels))
    dma = pltpu.SemaphoreType.DMA
    return pl.pallas_call(
        main_kernel,
        out_shape=(pltpu.VMEM((2, D, D), jnp.float32), pltpu.VMEM((slots, D), jnp.float32)),
        in_specs=[pl.BlockSpec(memory_space=pltpu.VMEM)] * 3,
        out_specs=[pl.BlockSpec(memory_space=pltpu.VMEM)] * 2,
        scratch_shapes=[
            pltpu.VMEM((2, D, slots), jnp.bfloat16),
            pltpu.VMEM((total, PW), jnp.float32),
            pltpu.VMEM((total, PW), jnp.float32),
            pltpu.VMEM((total, PW), jnp.float32),
            pltpu.VMEM((3, total // 8, PW), jnp.float32),
            pltpu.VMEM((total // 4, PW), jnp.float32),
            pltpu.VMEM((3, total // 16, PW), jnp.float32),
            pltpu.VMEM((total // 16, PW), jnp.float32),
            pltpu.VMEM((2, D, D), jnp.float32),
            pltpu.VMEM((2, D, D), jnp.float32),
            pltpu.VMEM((slots, D), jnp.float32),
            pltpu.VMEM((2, B, B), jnp.float32),
            pltpu.VMEM((slots, 2 * B), jnp.float32),
            dma((2, panels)),
            dma((2, panels, 3)), dma((2, panels)), dma((2, panels, 3)), dma((2, panels)),
            dma((2, panels, 3)), dma((2, panels)), dma((2, panels, 3)), dma((2, panels)),
            dma((2, panels)),
        ],
        compiler_params=pltpu.CompilerParams(
            collective_id=0, has_side_effects=True, vmem_limit_bytes=50 * 2**20),
    )(flat, marks, cent)


def full(n, k):
    return jnp.full(jnp.shape(k), n, jnp.int32)


def over(k, n):
    return lax.div(k, full(n, k))


def target(k, group, member):
    x = lax.rem(member // 2 + k, full(4, k))
    y = lax.rem(group + over(k, 4) + k, full(4, k))
    z = lax.rem(member // 8 * 2 + group // 4 + over(k, 16) + k + over(k, 4), full(4, k))
    core = lax.rem(member + over(k, 64), full(2, k))
    return lax.rem(z, full(2, k)) * 4 + y, over(z, 2) * 8 + x * 2 + core


def move_kernel(groups, members, rows_ref, hold_ref, old_ref, dest_ref, local_ref, flat_ref, tags_ref, split_ref, data_ref, mark_ref,
                data_send, data_recv, mark_send, mark_recv, own_sem):
    group = lax.axis_index("group")
    member = lax.axis_index("member")
    me = group * members + member
    devices = groups * members
    cap = data_ref.shape[0] // devices
    row_dev, D = rows_ref.shape

    barrier = pltpu.get_barrier_semaphore()

    @pl.loop(1, devices)
    def _(k):
        pl.semaphore_signal(barrier, inc=1, device_id=target(k, group, member), device_id_type=MESH)

    def parts(x):
        out = []
        for _ in range(3):
            out.append(x.astype(jnp.bfloat16))
            x = x - out[-1].astype(jnp.float32)
        return out

    def ones(hit):
        return jnp.where(hit, 1.0, 0.0).astype(jnp.bfloat16)

    dot = functools.partial(lax.dot_general, preferred_element_type=jnp.float32)
    olds = old_ref.shape[0]
    held = ones(lax.broadcasted_iota(jnp.int32, (olds, row_dev), 0) == hold_ref[...])
    for c in range(0, D, 256):
        a, b, d = (dot(held, part, (((0,), (0,)), ((), ()))) for part in parts(old_ref[:, c:c + 256]))
        for i, part in enumerate(parts(rows_ref[:, c:c + 256] + ((a + b) + d))):
            split_ref[i, :, c:c + 256] = part

    dest = dest_ref[...]
    to_device = ones(lax.broadcasted_iota(jnp.int32, (devices, row_dev), 0) == dest)
    row, col = (lax.broadcasted_iota(jnp.int32, (row_dev, row_dev), i) for i in range(2))
    before = dot(to_device, ones(row < col), NN)
    rank = jnp.sum(before * to_device.astype(jnp.float32), axis=0, keepdims=True).astype(jnp.int32)
    slot = lax.broadcasted_iota(jnp.int32, (B, row_dev), 0)
    tag = (local_ref[...] + 1).astype(jnp.float32)
    to_slot = jnp.where(slot == rank, tag, 0.0).astype(jnp.bfloat16)
    mark_ref[...] = dot(to_device, to_slot, NT).reshape(devices, 1, B)

    mine = pl.ds(pl.multiple_of(me * cap, cap), cap)

    def data(k, there):
        return pltpu.make_async_remote_copy(
            src_ref=data_ref.at[pl.ds(pl.multiple_of(k * cap, cap), cap), :], dst_ref=flat_ref.at[mine, :],
            send_sem=data_send, recv_sem=data_recv, device_id=there, device_id_type=MESH)

    def mark(there):
        return pltpu.make_async_remote_copy(
            src_ref=mark_ref.at[pl.ds(there[0] * members + there[1], 1)], dst_ref=tags_ref.at[pl.ds(me, 1)],
            send_sem=mark_send, recv_sem=mark_recv, device_id=there, device_id_type=MESH)

    many = B // cap
    own = (
        pltpu.make_async_copy(data_ref.at[pl.ds(0, cap), :], flat_ref.at[mine, :], own_sem.at[0]),
        pltpu.make_async_copy(mark_ref.at[pl.ds(me, 1)], tags_ref.at[pl.ds(me, 1)], own_sem.at[1]),
    )
    line = lax.broadcasted_iota(jnp.int32, (B, B), 0)

    @pl.loop(0, devices // many)
    def _(i):
        g, m = target(i * many + (line >> 3), group, member)
        ids = (g * members + m) * cap + (line & 7)
        hit = jnp.concatenate([ids] * (row_dev // B), axis=1) == dest * cap + rank
        pick = jnp.where(hit, 1.0, 0.0).astype(jnp.bfloat16)
        at = pl.ds(pl.multiple_of(i * B, B), B)
        for c in range(0, D, 256):
            a, b, d = (
                lax.dot_general(pick, split_ref[k, :, c:c + 256], NN, preferred_element_type=jnp.float32)
                for k in range(3)
            )
            data_ref[at, c:c + 256] = (a + b) + d

        @pl.when(i == 0)
        def _():
            pl.semaphore_wait(barrier, devices - 1)
            for copy in own:
                copy.start()

        @pl.loop(0, many)
        def _(j):
            k = i * many + j

            @pl.when(k > 0)
            def _():
                there = target(k, group, member)
                data(k, there).start()
                mark(there).start()

    for copy in own:
        copy.wait()
    rest = pl.ds(0, (devices - 1) * cap)
    far = lax.rem(group + 1, groups)
    everything = pltpu.make_async_remote_copy(
        src_ref=data_ref.at[rest, :], dst_ref=flat_ref.at[rest, :], send_sem=data_send, recv_sem=data_recv,
        device_id=(far, member), device_id_type=MESH)
    rest = pl.ds(0, devices - 1)
    marked = pltpu.make_async_remote_copy(
        src_ref=mark_ref.at[rest], dst_ref=tags_ref.at[rest], send_sem=mark_send, recv_sem=mark_recv,
        device_id=(far, member), device_id_type=MESH)
    everything.wait_send()
    marked.wait_send()
    marked.wait_recv()
    everything.wait_recv()


def move(rows, hold, old, dest, local, groups, members, slots):
    row_dev, D = rows.shape
    dma = pltpu.SemaphoreType.DMA
    devices = groups * members
    return pl.pallas_call(
        functools.partial(move_kernel, groups, members),
        out_shape=(
            jax.ShapeDtypeStruct((slots, D), jnp.float32),
            jax.ShapeDtypeStruct((devices, 1, B), jnp.float32),
        ),
        in_specs=[pl.BlockSpec(memory_space=pltpu.VMEM)] * 5,
        out_specs=[pl.BlockSpec(memory_space=pl.ANY)] * 2,
        scratch_shapes=[
            pltpu.VMEM((3, row_dev, D), jnp.bfloat16),
            pltpu.VMEM((slots, D), jnp.float32),
            pltpu.VMEM((devices, 1, B), jnp.float32),
            dma, dma, dma, dma, dma((2,)),
        ],
        compiler_params=pltpu.CompilerParams(collective_id=1, has_side_effects=True, vmem_limit_bytes=60 * 2**20),
    )(rows, hold, old, dest, local)


def on_device(rows, old_list, old_centroids, dest_device, new_local, centroids):
    n_group = lax.axis_size("group")
    n_member = lax.axis_size("member")
    devices = n_group * n_member
    row_dev = rows.shape[0]
    width = rows.shape[1]
    capacity = max(2, 2 * row_dev // devices)
    slots = devices * capacity
    flat, marks = move(
        rows, old_list[None, :], old_centroids, dest_device.reshape(1, row_dev), new_local[None, :], n_group, n_member, slots)
    factors, result = factor_all(flat, marks.reshape(devices, B), centroids)
    return (result, factors)


def solution(mesh):
    return jax.shard_map(
        on_device,
        mesh=mesh,
        in_specs=(
            P(("group", "member"), None),
            P(("group", "member")),
            P(),
            P(("group", "member"), None),
            P(("group", "member")),
            P("group", None),
        ),
        out_specs=(P(("group", "member"), None), P("group", None, None)),
        check_vma=False,
    )
```
